32 devices in a mesh: seq: 4 (over z), fsdp: 8 (over y, x, core).
Axes of the slice: x: 2, y: 2, z: 4, core: 2. Of those that a mesh axis runs over, the one named last changes fastest.
Arguments:
- tokens: bfloat16 [8, 1024, 2048], P('fsdp', 'seq'), may hold values from -6 to 6
- segments: int32 [8, 1024], P('fsdp'), may hold values from 0 to 3, never falling along the last dimension, each value on 1 to 512 neighbouring positions
- expert_ids: int32 [8, 1024, 4], P('fsdp', 'seq'), may hold values from 0 to 7, all different within a row; in each aligned block of 256 rows (0 to 255, 256 to 511, ..., all dimensions but the last counted through in order) at most 192 rows name the same one
- expert_gates: float32 [8, 1024, 4], P('fsdp', 'seq'), may hold values from 0.15 to 0.35
- attn_gain: bfloat16 [2048], P('fsdp'), may hold values from 0.5 to 1.5
- qkv_weight: bfloat16 [2048, 6144], P('fsdp'), may hold values from -0.125 to 0.125
- qkv_bias: bfloat16 [6144], P('fsdp'), may hold values from -0.59765625 to 0.59765625
- out_weight: bfloat16 [2048, 2048], P('fsdp'), may hold values from -1 to 1
- ffn_gain: bfloat16 [2048], P('fsdp'), may hold values from 0.5 to 1.5
- shared_gate_up: bfloat16 [2048, 2, 5632], P(None, None, 'fsdp'), may hold values from -0.125 to 0.125
- shared_down: bfloat16 [5632, 2048], P('fsdp'), may hold values from -0.078125 to 0.078125
- shared_gate: bfloat16 [2048], P('fsdp'), may hold values from -0.125 to 0.125
- expert_gate_up: bfloat16 [8, 2048, 2816], P(None, 'fsdp'), may hold values from -0.125 to 0.125
- expert_down: bfloat16 [8, 1408, 2048], P(None, 'fsdp'), may hold values from -0.15625 to 0.15625
- cotangent: bfloat16 [8, 1024, 2048], P('fsdp', 'seq'), may hold values from -6 to 6
Outputs:
- output: bfloat16 [8, 1024, 2048], P('fsdp', 'seq')
- input_grad: bfloat16 [8, 1024, 2048], P('fsdp', 'seq')
- attn_gain_grad: float32 [2048], P('fsdp')
- qkv_weight_grad: float32 [2048, 6144], P('fsdp')
- qkv_bias_grad: float32 [6144], P('fsdp')
- out_weight_grad: float32 [2048, 2048], P('fsdp')
- ffn_gain_grad: float32 [2048], P('fsdp')
- shared_gate_up_grad: float32 [2048, 2, 5632], P(None, None, 'fsdp')
- shared_down_grad: float32 [5632, 2048], P('fsdp')
- shared_gate_grad: float32 [2048], P('fsdp')
- expert_gate_up_grad: float32 [8, 2048, 2816], P(None, 'fsdp')
- expert_down_grad: float32 [8, 1408, 2048], P(None, 'fsdp')
The draws below stay inside these ranges and needn't reach their ends.
Inputs may be any that keep to these rules, and one draw needn't show every extreme that they name: `segments`: segment numbers never fall along a sequence; a document holds at most 512 positions, and some document exactly that many. `expert_ids`: each position names 4 different experts. Among the 256 positions that one device holds, no expert is named more than 192 times, and some expert exactly that often.
All inputs are finite; a program needn't handle non-finite values.
Results may differ from the reference program's by a relative error of at most 0.019.
Values may be sent and summed in bfloat16 or wider, within the bound.
A program may use at most 448 MiB of HBM per device.

```python
import math
import jax
import jax.numpy as jnp
import numpy as np
from jax import lax

D = 2048
HEADS = 16
HEAD_DIM = 128
FF_EXPERT = 1408
FF_SHARED = 5632
TOP = 4
EXPERTS = 8
QBLOCK = 512
DOCS = 4
SEQ_LEN = 1024
TOK = 256
SEQS = 8
DOC_MOST = 512
CAP = 512
SLOT = 192


def shard_levels(stream_key, shape, cuts, least, largest):
    factor_of = 1.0
    for position, shards_of in cuts:
        steps = jax.random.uniform(jax.random.fold_in(jax.random.fold_in(stream_key, 6), position), (shards_of,), jnp.float32, least / len(cuts), largest / len(cuts))
        factor_of = factor_of * jnp.repeat(jnp.exp(steps), shape[position] // shards_of).reshape((-1,) + (1,) * (len(shape) - 1 - position))
    return factor_of


def length_profile(count, total, reach, skew):
    portions = [(1 << 20) // math.isqrt(standing ** skew) + 1 for standing in range(2, count + 1)]
    spare, given = total - reach - (count - 1), [1] * (count - 1)
    while spare > 0:
        free = [i for i in range(count - 1) if given[i] < reach]
        mass, left = sum([portions[i] for i in free]), spare
        for i in free:
            more = min(reach - given[i], max(1, left * portions[i] // mass), spare)
            given[i] = given[i] + more
            spare = spare - more
    return np.array([reach] + given)


def uneven(stream_key, count, total, most, skew):
    if count == 2:
        one = jax.random.randint(stream_key, (), max(1, total - most), min(most, total - 1) + 1)
        return jnp.stack([one, total - one])
    tallies = jnp.asarray(length_profile(count, total, most, skew), jnp.int32)
    twos = (count - 1) // 2
    giver, taker = tallies[1:1 + 2 * twos:2], tallies[2:2 + 2 * twos:2]
    slack = jnp.minimum(giver - 1, most - taker)
    passed = jax.random.randint(jax.random.fold_in(stream_key, 1), (twos,), 0, 1 << 20) % (slack + 1)
    tallies = tallies.at[1:1 + 2 * twos:2].set(giver - passed).at[2:2 + 2 * twos:2].set(taker + passed)
    return tallies[jax.random.permutation(jax.random.fold_in(stream_key, 2), count)]


def assign_block(rng, own, number, rows, amount, top, bound, slope):
    order = jax.random.permutation(rng, amount)
    packed, usual = portions_of(amount, rows * top, bound, slope, True), portions_of(amount, rows * top, bound, slope, False)
    places = jnp.arange(amount)

    def named(tallies, offset_by):
        used = int((tallies > 0).sum())
        fixed = max(1, used // 4)
        passed = fixed + (places - fixed + offset_by * (used - fixed)) % max(1, amount - fixed)
        return jnp.zeros((amount,), jnp.int32).at[order[jnp.where(places < fixed, places, passed)]].set(jnp.asarray(tallies, jnp.int32))

    tallies = jnp.where(number % 4 == 0, named(packed, number // 4), named(usual, number - number // 4 - 1))
    mixed = jax.random.permutation(jax.random.fold_in(own, 3), amount)
    source_of, taker = mixed[0:amount // 2 * 2:2], mixed[1:amount // 2 * 2:2]
    slack = jnp.minimum(tallies[source_of] - 1, bound - tallies[taker]) // 2
    slack = jnp.where((source_of == order[0]) | (taker == order[0]) | (tallies[taker] == 0), 0, jnp.maximum(slack, 0))
    passed = jax.random.randint(jax.random.fold_in(own, 4), (amount // 2,), 0, 1 << 20) % (slack + 1)
    tallies = tallies.at[source_of].add(-passed).at[taker].add(passed)
    labels = jnp.searchsorted(jnp.cumsum(tallies), jnp.arange(rows * top), side="right").astype(jnp.int32)
    listing = labels.reshape(top, rows).T
    listing = listing[jax.random.permutation(jax.random.fold_in(own, 1), rows)]
    offset_by = jax.random.randint(jax.random.fold_in(own, 2), (rows, 1), 0, top)
    return jnp.take_along_axis(listing, (jnp.arange(top)[None, :] + offset_by) % top, axis=1)


def portions_of(count, total, most, skew, full):
    portions = [(1 << 20) // math.isqrt(standing ** skew) + 1 for standing in range(1, count + 1)]
    largest = most if full else min(most, max(-(-total // count), total * portions[0] // sum(portions)))
    least = 1 if total - largest >= count - 1 else 0
    given, rest = [largest] + [least] * (count - 1), total - largest - least * (count - 1)
    while rest > 0:
        candidates = [i for i in range(1, count) if given[i] < largest] or [i for i in range(1, count) if given[i] < most]
        mass, left = sum([portions[i] for i in candidates]), rest
        for i in candidates:
            extra = min(most - given[i], max(1, left * portions[i] // mass), rest)
            given[i] = given[i] + extra
            rest = rest - extra
    return np.array(given)


def bell_draw(rng, shape, scale, most, split=(), kind=jnp.bfloat16):
    drawn = scale * jax.random.normal(rng, shape, jnp.float32)
    if split:
        drawn = drawn * shard_levels(rng, shape, split, -0.22, 0.18)
    return jnp.clip(drawn, -most, most).astype(kind)


def setup_inputs(seed: int = 0) -> dict:
    keys = jax.random.split(jax.random.key(seed), 16)
    tokens = bell_draw(keys[0], (SEQS, SEQ_LEN, D), 1.0, 6.0, ((0, 8), (1, 4)))
    segments = jax.vmap(lambda own: jnp.searchsorted(jnp.cumsum(uneven(own, DOCS, SEQ_LEN, DOC_MOST, 1)), jnp.arange(SEQ_LEN), side="right"))(jax.random.split(keys[1], SEQS)).reshape((SEQS, SEQ_LEN)).astype(jnp.int32)
    expert_ids_keys = jax.random.split(jax.random.fold_in(keys[2], 1), SEQS * SEQ_LEN // TOK)
    expert_ids_turns = jax.random.permutation(jax.random.fold_in(keys[2], 3), SEQS * SEQ_LEN // TOK)
    expert_ids = jax.vmap(lambda own, number: assign_block(jax.random.fold_in(keys[2], 2), own, number, TOK, EXPERTS, TOP, SLOT, 1))(expert_ids_keys, expert_ids_turns).reshape((SEQS, SEQ_LEN, TOP))
    expert_gates = jnp.clip(0.15 + 0.19999999 * jax.random.uniform(keys[3], (SEQS, SEQ_LEN, TOP), jnp.float32) ** shard_levels(keys[3], (SEQS, SEQ_LEN, TOP), ((0, 8), (1, 4)), -0.2, 0.2), 0.15, 0.35)
    attn_gain = jnp.clip(1.0 + 0.1 * jax.random.normal(keys[4], (D,), jnp.float32), 0.5, 1.5).astype(jnp.bfloat16)
    qkv_weight = bell_draw(keys[5], (D, 3 * D), D ** -0.5, 0.125, ((0, 8),))
    qkv_bias = bell_draw(keys[6], (3 * D,), 0.1, 0.59765625, ((0, 8),))
    out_weight = bell_draw(keys[7], (D, D), (D // 64) ** -0.5, 1.0, ((0, 8),))
    ffn_gain = jnp.clip(1.0 + 0.1 * jax.random.normal(keys[8], (D,), jnp.float32), 0.5, 1.5).astype(jnp.bfloat16)
    shared_gate_up = bell_draw(keys[9], (D, 2, FF_SHARED), D ** -0.5, 0.125, ((2, 8),))
    shared_down = bell_draw(keys[10], (FF_SHARED, D), FF_SHARED ** -0.5, 0.078125, ((0, 8),))
    shared_gate = bell_draw(keys[11], (D,), D ** -0.5, 0.125, ((0, 8),))
    expert_gate_up = bell_draw(keys[12], (EXPERTS, D, 2 * FF_EXPERT), D ** -0.5, 0.125, ((1, 8),))
    expert_down = bell_draw(keys[13], (EXPERTS, FF_EXPERT, D), FF_EXPERT ** -0.5, 0.15625, ((1, 8),))
    cotangent = bell_draw(keys[14], (SEQS, SEQ_LEN, D), 1.0, 6.0, ((0, 8), (1, 4)))
    return dict(tokens=tokens, segments=segments, expert_ids=expert_ids, expert_gates=expert_gates, attn_gain=attn_gain, qkv_weight=qkv_weight, qkv_bias=qkv_bias, out_weight=out_weight, ffn_gain=ffn_gain, shared_gate_up=shared_gate_up, shared_down=shared_down, shared_gate=shared_gate, expert_gate_up=expert_gate_up, expert_down=expert_down, cotangent=cotangent)


EPSILON = 1e-06
THETA = 1000000.0
HIGHEST = lax.Precision.HIGHEST

@jax.custom_vjp
def low(v):
    return lax.optimization_barrier(v.astype(jnp.bfloat16)).astype(jnp.float32)

@jax.custom_vjp
def low_back(v):
    return v

def low_keep(v):
    return (low(v), None)

def low_pass(kept, grad):
    return (grad,)

def back_keep(v):
    return (v, None)

def back_low(kept, grad):
    return (low(grad),)
low.defvjp(low_keep, low_pass)
low_back.defvjp(back_keep, back_low)

def norm_rows(values, norm_gain):
    return values * lax.rsqrt(lax.optimization_barrier(jnp.mean(values * values, axis=-1, keepdims=True)) + EPSILON) * norm_gain

def rope_tables(positions):
    steps_half = jnp.arange(HEAD_DIM // 2, dtype=jnp.int32).astype(jnp.float32)
    frequency = jnp.exp(steps_half * (-2.0 * math.log(THETA) / HEAD_DIM))
    angles = positions.astype(jnp.float32)[:, None] * frequency[None, :]
    angles = jnp.concatenate([angles, angles], axis=-1)
    return (jnp.cos(angles), jnp.sin(angles))

def rotate(head_rows, cosine, sine_table):
    middle = head_rows.shape[-1] // 2
    turned = jnp.concatenate([-head_rows[..., middle:], head_rows[..., :middle]], axis=-1)
    return head_rows * cosine[:, None, :] + turned * sine_table[:, None, :]

def attend(queries, key_rows, value_rows, documents):
    length = queries.shape[0]
    factor = 1.0 / math.sqrt(HEAD_DIM)
    key_place = jnp.arange(length, dtype=jnp.int32)

    def one_block(block_index):
        first_row = block_index * QBLOCK
        query_block = lax.dynamic_slice_in_dim(queries, first_row, QBLOCK, 0)
        block_docs = lax.dynamic_slice_in_dim(documents, first_row, QBLOCK, 0)
        scores = low_back(jnp.einsum('qhd,khd->hqk', query_block, key_rows, precision=HIGHEST) * factor)
        row_place = first_row + jnp.arange(QBLOCK, dtype=jnp.int32)
        allowed = (row_place[:, None] >= key_place[None, :]) & (block_docs[:, None] == documents[None, :])
        scores = jnp.where(allowed[None], scores, -1e+30)
        top_score = lax.optimization_barrier(jnp.max(scores, axis=-1, keepdims=True))
        weights = jnp.exp(scores - top_score)
        probability = low(weights / lax.optimization_barrier(jnp.sum(weights, axis=-1, keepdims=True)))
        return jnp.einsum('hqk,khd->qhd', probability, value_rows, precision=HIGHEST)
    mixture = lax.map(jax.checkpoint(one_block), jnp.arange(length // QBLOCK, dtype=jnp.int32))
    return mixture.reshape(length, HEADS, HEAD_DIM)

def experts(second, picked, gate_values, expert_gate_up, expert_down):
    length = second.shape[0]
    expert_names = jnp.arange(EXPERTS, dtype=jnp.int32)
    matches = picked[:, :, None] == expert_names[None, None, :]
    chosen = lax.optimization_barrier(jnp.sum(matches.astype(jnp.int32), axis=1))
    earlier = jnp.cumsum(chosen, axis=0) - chosen
    retained = (chosen > 0) & (earlier < CAP)
    portion = lax.optimization_barrier(jnp.sum(jnp.where(matches, gate_values[:, :, None], 0.0), axis=1)) * retained.astype(jnp.float32)
    column = jnp.where(retained, earlier, CAP).astype(jnp.int32)
    owners = jnp.broadcast_to(expert_names[None, :], (length, EXPERTS))
    position_all = jnp.broadcast_to(jnp.arange(length, dtype=jnp.int32)[:, None], (length, EXPERTS))
    slot_table = jnp.full((EXPERTS, CAP + 1), length, jnp.int32).at[owners, column].set(position_all)[:, :CAP]
    padded = jnp.concatenate([second, jnp.zeros((1, D), jnp.float32)], axis=0)
    portion_pad = jnp.concatenate([portion, jnp.zeros((1, EXPERTS), jnp.float32)], axis=0)
    gathered = padded[slot_table]
    slot_share = portion_pad[slot_table, expert_names[:, None]]
    both_parts = low_back(jnp.einsum('ecd,edf->ecf', gathered, expert_gate_up, precision=HIGHEST))
    inner_rows = low(jax.nn.silu(both_parts[..., :FF_EXPERT]) * both_parts[..., FF_EXPERT:])
    results = low_back(jnp.einsum('ecf,efd->ecd', inner_rows, expert_down, precision=HIGHEST))
    placed = jnp.zeros((length + 1, D), jnp.float32).at[slot_table].add(results * slot_share[..., None])
    return placed[:length]

def sequence(weights, token_rows, documents, picked, gate_values):
    attn_gain, qkv_weight, qkv_bias, out_weight, ffn_gain, shared_gate_up, shared_down, shared_gate, expert_gate_up, expert_down = weights
    cosine, sine_table = rope_tables(jnp.arange(SEQ_LEN, dtype=jnp.int32))
    normed = low(norm_rows(token_rows, attn_gain))
    joined_qkv = low_back(jnp.dot(normed, qkv_weight, precision=HIGHEST) + qkv_bias)
    split_heads = joined_qkv.reshape(SEQ_LEN, 3, HEADS, HEAD_DIM)
    queries = low_back(low(rotate(split_heads[:, 0], cosine, sine_table)))
    key_rows = low_back(low(rotate(split_heads[:, 1], cosine, sine_table)))
    value_rows = low_back(low(split_heads[:, 2]))
    mixture = low_back(low(attend(queries, key_rows, value_rows, documents))).reshape(SEQ_LEN, D)
    hidden = token_rows + low_back(jnp.dot(mixture, out_weight, precision=HIGHEST))
    second = low(norm_rows(hidden, ffn_gain))
    shared_both = low_back(jnp.einsum('td,dcf->tcf', second, shared_gate_up, precision=HIGHEST))
    shared_inner = low(jax.nn.silu(shared_both[:, 0]) * shared_both[:, 1])
    branch = low_back(jnp.dot(shared_inner, shared_down, precision=HIGHEST))
    opening = jax.nn.sigmoid(jnp.dot(second, shared_gate, precision=HIGHEST))
    routed = experts(second, picked, gate_values, expert_gate_up, expert_down)
    return hidden + opening[:, None] * branch + routed

def reference(tokens, segments, expert_ids, expert_gates, attn_gain, qkv_weight, qkv_bias, out_weight, ffn_gain, shared_gate_up, shared_down, shared_gate, expert_gate_up, expert_down, cotangent):
    params = tuple((weight_item.astype(jnp.float32) for weight_item in (attn_gain, qkv_weight, qkv_bias, out_weight, ffn_gain, shared_gate_up, shared_down, shared_gate, expert_gate_up, expert_down)))
    gate_floats = expert_gates.astype(jnp.float32)

    def forward(inputs, weights):

        def one_sequence(pieces):
            token_rows, documents, picked, gate_values = pieces
            return sequence(weights, token_rows, documents, picked, gate_values)
        return lax.map(one_sequence, (inputs, segments, expert_ids, gate_floats))
    output, pullback = jax.vjp(forward, tokens.astype(jnp.float32), params)
    input_grad, weight_grads = pullback(cotangent.astype(jnp.float32))
    return (output.astype(jnp.bfloat16), input_grad.astype(jnp.bfloat16), weight_grads[0].astype(jnp.float32), weight_grads[1].astype(jnp.float32), weight_grads[2].astype(jnp.float32), weight_grads[3].astype(jnp.float32), weight_grads[4].astype(jnp.float32), weight_grads[5].astype(jnp.float32), weight_grads[6].astype(jnp.float32), weight_grads[7].astype(jnp.float32), weight_grads[8].astype(jnp.float32), weight_grads[9].astype(jnp.float32))
```

```python
import math

import jax
import jax.numpy as jnp
from jax import lax
from jax.sharding import PartitionSpec as P

D = 2048
HEADS = 16
HEAD_DIM = 128
FF_EXPERT = 1408
TOP = 4
EXPERTS = 8
QBLOCK = 256
DOC_MOST = 512

EPSILON = 1e-06
THETA = 1000000.0

bf16 = jnp.bfloat16
f32 = jnp.float32


def dot(a, b, contract, kind=f32):
    return lax.dot_general(a, b, (contract, ((), ())), preferred_element_type=f32).astype(kind)


def rms_scale(values):
    return lax.rsqrt(jnp.mean(values * values, axis=-1, keepdims=True) + EPSILON)


def norm_back(values, scale, gain, grad):
    scaled = grad * gain
    centre = jnp.mean(scaled * values, axis=-1, keepdims=True)
    return scale * (scaled - values * (scale * scale) * centre)


def rope_tables(positions):
    steps_half = jnp.arange(HEAD_DIM // 2, dtype=jnp.int32).astype(f32)
    frequency = jnp.exp(steps_half * (-2.0 * math.log(THETA) / HEAD_DIM))
    angles = positions.astype(f32)[:, None] * frequency[None, :]
    angles = jnp.concatenate([angles, angles], axis=-1)
    return (jnp.cos(angles), jnp.sin(angles))


def rotate(rows, cosine, sine):
    middle = rows.shape[-1] // 2
    turned = jnp.concatenate([-rows[..., middle:], rows[..., :middle]], axis=-1)
    return rows * cosine[:, None, :] + turned * sine[:, None, :]


def rotate_back(rows, cosine, sine):
    middle = rows.shape[-1] // 2
    turned = rows * sine[:, None, :]
    turned = jnp.concatenate([turned[..., middle:], -turned[..., :middle]], axis=-1)
    return rows * cosine[:, None, :] + turned


def key_start(block):
    return max(0, block * QBLOCK - DOC_MOST)


def block_scores(block, queries, keys, documents, factor):
    first, start = block * QBLOCK, key_start(block)
    stop = first + QBLOCK
    scores = (
        jnp.einsum(
            "qhd,khd->hqk", queries[first:stop], keys[start:stop], preferred_element_type=f32
        )
        * factor
    )
    rows = first + jnp.arange(QBLOCK, dtype=jnp.int32)
    columns = start + jnp.arange(stop - start, dtype=jnp.int32)
    allowed = (rows[:, None] >= columns[None, :]) & (
        documents[first:stop, None] == documents[None, start:stop]
    )
    return jnp.where(allowed[None], scores, -1e30)


def attend(queries, keys, values, documents, factor):
    mixed, logs = [], []
    for block in range(queries.shape[0] // QBLOCK):
        start, stop = key_start(block), (block + 1) * QBLOCK
        scores = block_scores(block, queries, keys, documents, factor)
        top = jnp.max(scores, axis=-1, keepdims=True)
        weights = jnp.exp(scores - top)
        totals = jnp.sum(weights, axis=-1, keepdims=True)
        probability = (weights / totals).astype(bf16)
        mixed.append(
            jnp.einsum(
                "hqk,khd->qhd", probability, values[start:stop], preferred_element_type=f32
            ).astype(bf16)
        )
        logs.append(top + jnp.log(totals))
    return jnp.concatenate(mixed, axis=0), logs


def attend_back(queries, keys, values, documents, factor, logs, grads):
    length = queries.shape[0]
    grad_queries = []
    grad_keys = jnp.zeros(keys.shape, f32)
    grad_values = jnp.zeros(values.shape, f32)
    for block in range(length // QBLOCK):
        start, stop = key_start(block), (block + 1) * QBLOCK
        scores = block_scores(block, queries, keys, documents, factor)
        probability = jnp.exp(scores - logs[block])
        grad_block = grads[block * QBLOCK : stop]
        query_block = queries[block * QBLOCK : stop]
        grad_values = grad_values.at[start:stop].add(
            jnp.einsum(
                "hqk,qhd->khd", probability.astype(bf16), grad_block, preferred_element_type=f32
            )
        )
        grad_probability = jnp.einsum(
            "qhd,khd->hqk", grad_block, values[start:stop], preferred_element_type=f32
        )
        centre = jnp.sum(grad_probability * probability, axis=-1, keepdims=True)
        grad_scores = (probability * (grad_probability - centre)).astype(bf16)
        grad_queries.append(
            jnp.einsum("hqk,khd->qhd", grad_scores, keys[start:stop], preferred_element_type=f32)
            * factor
        )
        grad_keys = grad_keys.at[start:stop].add(
            jnp.einsum("hqk,qhd->khd", grad_scores, query_block, preferred_element_type=f32)
            * factor
        )
    return jnp.concatenate(grad_queries, axis=0), grad_keys, grad_values


def sum_seq(value):
    return lax.psum(value.astype(bf16), "seq").astype(f32)


def on_device(
    tokens,
    segments,
    expert_ids,
    expert_gates,
    attn_gain,
    qkv_weight,
    qkv_bias,
    out_weight,
    ffn_gain,
    shared_gate_up,
    shared_down,
    shared_gate,
    expert_gate_up,
    expert_down,
    cotangent,
):
    fsdp, seq = lax.axis_size("fsdp"), lax.axis_size("seq")
    me, place = lax.axis_index("fsdp"), lax.axis_index("seq")
    row_count, length = tokens.shape[1], segments.shape[1]
    heads = HEADS // seq
    copies = fsdp // EXPERTS
    width = D // fsdp
    hidden_own = FF_EXPERT // copies
    piece = hidden_own // fsdp
    factor = 1.0 / math.sqrt(HEAD_DIM)
    capacity = length * TOP // EXPERTS

    vectors = jnp.concatenate([attn_gain, ffn_gain, shared_gate, qkv_bias])
    vectors = lax.all_gather(vectors, "fsdp", axis=0)
    gain_one = vectors[:, :width].reshape(D).astype(f32)
    gain_two = vectors[:, width : 2 * width].reshape(D).astype(f32)
    gate_vector = vectors[:, 2 * width : 3 * width].reshape(D)
    bias = vectors[:, 3 * width :].reshape(3, seq, heads * HEAD_DIM)
    bias = lax.dynamic_index_in_dim(bias, place, 1, keepdims=False).reshape(-1).astype(f32)

    all_tokens = lax.all_gather(tokens[0], "seq", axis=0, tiled=True)
    weight_qkv = qkv_weight.reshape(width, 3, seq, heads * HEAD_DIM)
    weight_qkv = lax.dynamic_index_in_dim(weight_qkv, place, 2, keepdims=False)
    weight_qkv = lax.all_gather(
        weight_qkv.reshape(width, 3 * heads * HEAD_DIM), "fsdp", axis=0, tiled=True
    )
    weight_out = lax.all_gather(out_weight, "fsdp", axis=0, tiled=True)
    upstream_all = lax.all_gather(cotangent[0], "fsdp", axis=0, tiled=True)

    up_sent = expert_gate_up.reshape(EXPERTS, width, 2, fsdp, copies, piece)
    up_sent = up_sent.transpose(0, 4, 1, 2, 3, 5).reshape(fsdp, width, 2 * hidden_own)
    weight_up = lax.all_to_all(up_sent, "fsdp", 0, 0, tiled=True).reshape(D, 2 * hidden_own)
    down_sent = expert_down.reshape(fsdp, piece, D)
    weight_down = lax.all_to_all(down_sent, "fsdp", 0, 0, tiled=True).reshape(hidden_own, D)

    x_all = all_tokens.astype(f32)
    normed_unit = x_all * rms_scale(x_all)
    normed = (normed_unit * gain_one).astype(bf16)
    cosine, sine = rope_tables(jnp.arange(length, dtype=jnp.int32))
    joined = dot(normed, weight_qkv, ((1,), (0,))) + bias
    split = joined.reshape(length, 3, heads, HEAD_DIM)
    queries = rotate(split[:, 0], cosine, sine).astype(bf16)
    keys = rotate(split[:, 1], cosine, sine).astype(bf16)
    values = split[:, 2].astype(bf16)
    documents = segments[0]
    mixed, logs = attend(queries, keys, values, documents, factor)
    mixed_rows = lax.all_to_all(mixed, "seq", 0, 1, tiled=True).reshape(row_count, D)
    inputs = tokens[0].astype(f32)
    hidden = inputs + dot(mixed_rows, weight_out, ((1,), (0,)))
    scale_two = rms_scale(hidden)
    second = (hidden * scale_two * gain_two).astype(bf16)
    second_all = lax.all_gather(second, "fsdp", axis=0, tiled=True)

    names = jnp.arange(EXPERTS, dtype=jnp.int32)
    matches = expert_ids[0][:, :, None] == names[None, None, :]
    chosen = jnp.sum(matches.astype(jnp.int32), axis=1)
    earlier = jnp.cumsum(chosen, axis=0) - chosen
    tallies = lax.all_gather(jnp.sum(chosen, axis=0), "seq")
    before = jnp.arange(seq, dtype=jnp.int32)[:, None] < place
    offsets = jnp.sum(jnp.where(before, tallies, 0), axis=0)
    retained = (chosen > 0) & (offsets[None, :] + earlier < capacity)
    portion = jnp.sum(
        jnp.where(matches, expert_gates[0][:, :, None], 0.0), axis=1
    ) * retained.astype(f32)
    portion_all = lax.all_gather(portion, "fsdp", axis=0, tiled=True)
    own_expert = (names == me // copies).astype(f32)
    share = jnp.sum(portion_all * own_expert[None, :], axis=1, keepdims=True)

    def expert(weight_gate, weight_lift, weight_back, scale):
        gate = dot(second_all, weight_gate, ((1,), (0,)))
        lift = dot(second_all, weight_lift, ((1,), (0,)))
        raw = dot(upstream_all, weight_back, ((1,), (1,)))
        sigma = jax.nn.sigmoid(gate)
        silu = gate * sigma
        inner = silu * lift
        reach = jnp.sum(inner * raw, axis=1)
        inner = (inner * scale).astype(bf16)
        grad = raw * scale
        grad_gate = (grad * lift * sigma * (1.0 + gate * (1.0 - sigma))).astype(bf16)
        grad_lift = (grad * silu).astype(bf16)
        return inner, grad_gate, grad_lift, reach

    opening_all = jax.nn.sigmoid(dot(second_all, gate_vector, ((1,), (0,))))[:, None]
    s_gate, s_lift = shared_gate_up[:, 0], shared_gate_up[:, 1]
    inner_s, ga_s, gl_s, reach = expert(s_gate, s_lift, shared_down, opening_all)
    grad_s_down = dot(inner_s, upstream_all, ((0,), (0,)), bf16)
    grad_s_up = jnp.stack(
        [dot(second_all, ga_s, ((0,), (0,)), bf16), dot(second_all, gl_s, ((0,), (0,)), bf16)],
        axis=1,
    )
    e_gate, e_lift = weight_up[:, :hidden_own], weight_up[:, hidden_own:]
    inner_e, ga_e, gl_e, _ = expert(e_gate, e_lift, weight_down, share)

    grad_second_all = (
        dot(ga_s, s_gate, ((1,), (1,)))
        + dot(gl_s, s_lift, ((1,), (1,)))
        + dot(ga_e, e_gate, ((1,), (1,)))
        + dot(gl_e, e_lift, ((1,), (1,)))
    ).astype(bf16)
    grad_second = lax.psum_scatter(
        grad_second_all, "fsdp", scatter_dimension=0, tiled=True
    ).astype(f32)
    reach = lax.psum_scatter(reach, "fsdp", scatter_dimension=0, tiled=True)

    grad_e_down = dot(inner_e, upstream_all, ((0,), (0,)), bf16)
    grad_e_up = jnp.concatenate(
        [dot(second_all, ga_e, ((0,), (0,)), bf16), dot(second_all, gl_e, ((0,), (0,)), bf16)],
        axis=1,
    )
    grad_e_up = lax.all_to_all(
        grad_e_up.reshape(fsdp, width, 2 * hidden_own), "fsdp", 0, 0, tiled=True
    )
    grad_e_up = grad_e_up.reshape(EXPERTS, copies, width, 2, fsdp, piece)
    grad_e_up = grad_e_up.transpose(0, 2, 3, 4, 1, 5).reshape(EXPERTS, width, 2 * FF_EXPERT)
    grad_e_down = lax.all_to_all(
        grad_e_down.reshape(fsdp, piece, D), "fsdp", 0, 0, tiled=True
    ).reshape(EXPERTS, copies * piece, D)

    out_all = (
        dot(inner_s, shared_down, ((1,), (0,))) + dot(inner_e, weight_down, ((1,), (0,)))
    ).astype(bf16)
    out_part = lax.psum_scatter(out_all, "fsdp", scatter_dimension=0, tiled=True)
    output = (hidden + out_part.astype(f32)).astype(bf16)

    upstream = cotangent[0].astype(f32)
    opening = jax.nn.sigmoid(dot(second, gate_vector, ((1,), (0,))))
    grad_logit = reach * opening * (1.0 - opening)
    grad_second = grad_second + grad_logit[:, None] * gate_vector.astype(f32)[None, :]
    grad_gate_vector = jnp.sum(grad_logit[:, None] * second.astype(f32), axis=0)
    grad_hidden = upstream + norm_back(hidden, scale_two, gain_two, grad_second)
    grad_gain_two = jnp.sum(grad_second * hidden * scale_two, axis=0)
    grad_projected = grad_hidden.astype(bf16)
    grad_mixture = dot(grad_projected, weight_out, ((1,), (1,)), bf16)
    grad_heads = lax.all_to_all(
        grad_mixture.reshape(row_count, HEADS, HEAD_DIM), "seq", 1, 0, tiled=True
    )
    grad_out = dot(mixed_rows, grad_projected, ((0,), (0,)), bf16)
    grad_out = lax.psum_scatter(grad_out, "fsdp", scatter_dimension=0, tiled=True)

    grad_queries, grad_keys, grad_values = attend_back(
        queries, keys, values, documents, factor, logs, grad_heads
    )
    grad_joined = jnp.stack(
        [
            rotate_back(grad_queries.astype(bf16).astype(f32), cosine, sine),
            rotate_back(grad_keys.astype(bf16).astype(f32), cosine, sine),
            grad_values,
        ],
        axis=1,
    )
    grad_joined = grad_joined.reshape(length, 3 * heads * HEAD_DIM).astype(bf16)
    grad_normed_all = dot(grad_joined, weight_qkv, ((1,), (1,)))
    grad_gain_one = jnp.sum(grad_normed_all * normed_unit, axis=0)
    grad_normed = lax.psum_scatter(
        grad_normed_all.astype(bf16), "seq", scatter_dimension=0, tiled=True
    ).astype(f32)
    input_grad = (grad_hidden + norm_back(inputs, rms_scale(inputs), gain_one, grad_normed)).astype(
        bf16
    )

    grad_qkv = dot(normed, grad_joined, ((0,), (0,)), bf16)
    grad_qkv = lax.psum_scatter(grad_qkv, "fsdp", scatter_dimension=0, tiled=True)
    grad_qkv = lax.all_gather(grad_qkv.reshape(width, 3, heads * HEAD_DIM), "seq", axis=2)
    grad_qkv = grad_qkv.reshape(width, 3 * D).astype(f32)

    grad_bias = jnp.sum(grad_joined.astype(f32), axis=0).reshape(3, 1, heads * HEAD_DIM)
    own_heads = (jnp.arange(seq, dtype=jnp.int32) == place).astype(f32)
    grad_bias = (grad_bias * own_heads[None, :, None]).reshape(fsdp, 3 * D // fsdp)
    small = jnp.concatenate(
        [
            grad_gain_one.reshape(fsdp, width),
            grad_gain_two.reshape(fsdp, width),
            grad_gate_vector.reshape(fsdp, width),
            grad_bias,
        ],
        axis=1,
    )
    small = lax.psum(small, ("seq", "fsdp"))
    small = lax.dynamic_index_in_dim(small, me, 0, keepdims=False)

    return (
        output[None],
        input_grad[None],
        small[:width],
        grad_qkv,
        small[3 * width :],
        sum_seq(grad_out),
        small[width : 2 * width],
        sum_seq(grad_s_up),
        sum_seq(grad_s_down),
        small[2 * width : 3 * width],
        sum_seq(grad_e_up),
        sum_seq(grad_e_down),
    )


def solution(mesh):
    return jax.shard_map(
        on_device,
        mesh=mesh,
        in_specs=(
            P("fsdp", "seq", None),
            P("fsdp", None),
            P("fsdp", "seq", None),
            P("fsdp", "seq", None),
            P("fsdp"),
            P("fsdp", None),
            P("fsdp"),
            P("fsdp", None),
            P("fsdp"),
            P(None, None, "fsdp"),
            P("fsdp", None),
            P("fsdp"),
            P(None, "fsdp", None),
            P(None, "fsdp", None),
            P("fsdp", "seq", None),
        ),
        out_specs=(
            P("fsdp", "seq", None),
            P("fsdp", "seq", None),
            P("fsdp"),
            P("fsdp", None),
            P("fsdp"),
            P("fsdp", None),
            P("fsdp"),
            P(None, None, "fsdp"),
            P("fsdp", None),
            P("fsdp"),
            P(None, "fsdp", None),
            P(None, "fsdp", None),
        ),
        check_vma=False,
    )
```

```python
import functools
import math

import jax
import jax.numpy as jnp
from jax import lax
from jax.experimental import pallas as pl
from jax.experimental.pallas import tpu as pltpu
from jax.sharding import PartitionSpec as P

D = 2048
HEADS = 16
HEAD_DIM = 128
FF_EXPERT = 1408
TOP = 4
EXPERTS = 8
QBLOCK = 256
DOC_MOST = 512

EPSILON = 1e-06
THETA = 1000000.0

bf16 = jnp.bfloat16
f32 = jnp.float32


def dot(a, b, contract, kind=f32):
    return lax.dot_general(a, b, (contract, ((), ())), preferred_element_type=f32).astype(kind)


def rms_scale(values):
    return lax.rsqrt(jnp.mean(values * values, axis=-1, keepdims=True) + EPSILON)


def norm_back(values, scale, gain, grad):
    scaled = grad * gain
    centre = jnp.mean(scaled * values, axis=-1, keepdims=True)
    return scale * (scaled - values * (scale * scale) * centre)


def rope_tables(positions):
    steps_half = jnp.arange(HEAD_DIM // 2, dtype=jnp.int32).astype(f32)
    frequency = jnp.exp(steps_half * (-2.0 * math.log(THETA) / HEAD_DIM))
    angles = positions.astype(f32)[:, None] * frequency[None, :]
    angles = jnp.concatenate([angles, angles], axis=-1)
    return (jnp.cos(angles), jnp.sin(angles))


def rotate(rows, cosine, sine):
    middle = rows.shape[-1] // 2
    turned = jnp.concatenate([-rows[..., middle:], rows[..., :middle]], axis=-1)
    return rows * cosine[:, None, :] + turned * sine[:, None, :]


def rotate_back(rows, cosine, sine):
    middle = rows.shape[-1] // 2
    turned = rows * sine[:, None, :]
    turned = jnp.concatenate([turned[..., middle:], -turned[..., :middle]], axis=-1)
    return rows * cosine[:, None, :] + turned


def key_start(block):
    return max(0, block * QBLOCK - DOC_MOST)


def block_scores(block, queries, keys, documents, factor):
    first, start = block * QBLOCK, key_start(block)
    stop = first + QBLOCK
    scores = (
        jnp.einsum(
            "qhd,khd->hqk", queries[first:stop], keys[start:stop], preferred_element_type=f32
        )
        * factor
    )
    rows = first + jnp.arange(QBLOCK, dtype=jnp.int32)
    columns = start + jnp.arange(stop - start, dtype=jnp.int32)
    allowed = (rows[:, None] >= columns[None, :]) & (
        documents[first:stop, None] == documents[None, start:stop]
    )
    return jnp.where(allowed[None], scores, -1e30)


def attend(queries, keys, values, documents, factor):
    mixed, logs = [], []
    for block in range(queries.shape[0] // QBLOCK):
        start, stop = key_start(block), (block + 1) * QBLOCK
        scores = block_scores(block, queries, keys, documents, factor)
        top = jnp.max(scores, axis=-1, keepdims=True)
        weights = jnp.exp(scores - top)
        totals = jnp.sum(weights, axis=-1, keepdims=True)
        probability = (weights / totals).astype(bf16)
        mixed.append(
            jnp.einsum(
                "hqk,khd->qhd", probability, values[start:stop], preferred_element_type=f32
            ).astype(bf16)
        )
        logs.append(top + jnp.log(totals))
    return jnp.concatenate(mixed, axis=0), logs


def attend_back(queries, keys, values, documents, factor, logs, grads):
    length = queries.shape[0]
    grad_queries = []
    grad_keys = jnp.zeros(keys.shape, f32)
    grad_values = jnp.zeros(values.shape, f32)
    for block in range(length // QBLOCK):
        start, stop = key_start(block), (block + 1) * QBLOCK
        scores = block_scores(block, queries, keys, documents, factor)
        probability = jnp.exp(scores - logs[block])
        grad_block = grads[block * QBLOCK : stop]
        query_block = queries[block * QBLOCK : stop]
        grad_values = grad_values.at[start:stop].add(
            jnp.einsum(
                "hqk,qhd->khd", probability.astype(bf16), grad_block, preferred_element_type=f32
            )
        )
        grad_probability = jnp.einsum(
            "qhd,khd->hqk", grad_block, values[start:stop], preferred_element_type=f32
        )
        centre = jnp.sum(grad_probability * probability, axis=-1, keepdims=True)
        grad_scores = (probability * (grad_probability - centre)).astype(bf16)
        grad_queries.append(
            jnp.einsum("hqk,khd->qhd", grad_scores, keys[start:stop], preferred_element_type=f32)
            * factor
        )
        grad_keys = grad_keys.at[start:stop].add(
            jnp.einsum("hqk,qhd->khd", grad_scores, query_block, preferred_element_type=f32)
            * factor
        )
    return jnp.concatenate(grad_queries, axis=0), grad_keys, grad_values


def after(value, *earlier):
    return lax.optimization_barrier((value, earlier))[0]


def line_neighbours(place):
    middle = lax.rem(place + 1, 4) // 2
    low = 1 - place // 2
    partner = low * (1 - place) + (1 - low) * (5 - place)
    across = low * 2 + (1 - low) * 1
    return middle, partner, across


def flip(index, bits):
    result, step = 0, 1
    while step < 8:
        bit = lax.rem(index // step, 2)
        result = result + step * (1 - bit if bits & step else bit)
        step *= 2
    return result


SLOTS = 4
ORDER = (0, 1, 2, 4, 3, 5, 6, 7)
LEAVE = {2: ((2, 4), (3, 5)), 4: ((3, 5), (6, 7))}


def combine_kernel(plan, *refs):
    count = len(plan)
    sources, refs = refs[:count], refs[count:]
    results, refs = refs[:count], refs[count:]
    lands, refs = refs[:count], refs[count:]
    buffers, refs = refs[: 5 * count], refs[5 * count :]
    (land_send, land_recv, g_sem, a_send, a_recv, b_send, b_recv, c_send, c_recv) = refs[:9]
    out_sem, a_free, b_free = refs[9:]
    me, place = lax.axis_index("fsdp"), lax.axis_index("seq")
    middle, partner, across = line_neighbours(place)
    peers = [flip(me, k) for k in range(8)]

    barrier = pltpu.get_barrier_semaphore()
    swapping = any(swapped for swapped, _, _, _ in plan)
    if swapping:
        for k in range(1, 8):
            pl.semaphore_signal(
                barrier, device_id={"fsdp": peers[k]}, device_id_type=pl.DeviceIdType.MESH
            )
    pl.semaphore_signal(
        barrier, device_id={"seq": partner}, device_id_type=pl.DeviceIdType.MESH
    )

    @pl.when(middle == 1)
    def _():
        pl.semaphore_signal(
            barrier, device_id={"seq": across}, device_id_type=pl.DeviceIdType.MESH
        )

    pl.semaphore_wait(barrier, 1 + middle + (7 if swapping else 0))

    arrivals = {}
    for index, (swapped, rows, blocks, _) in enumerate(plan):
        if not swapped:
            continue
        here = pl.ds(pl.multiple_of(me * rows, 16), rows)
        for k in range(1, 8):
            there = pl.ds(pl.multiple_of(peers[k] * rows, 16), rows)
            copy = pltpu.make_async_remote_copy(
                src_ref=sources[index].at[there],
                dst_ref=lands[index].at[here],
                send_sem=land_send.at[index, k],
                recv_sem=land_recv.at[index, k],
                device_id={"fsdp": peers[k]},
                device_id_type=pl.DeviceIdType.MESH,
            )
            arrivals[index, k] = copy
            if k in (1, 2, 4):
                copy.start()

    chunks, starts = [], []
    for index, (swapped, rows, blocks, size) in enumerate(plan):
        starts.append(len(chunks))
        for block in range(blocks):
            base = (peers[ORDER[block]] if swapped else block) * rows
            for first in range(0, rows, size):
                chunks.append((index, block if first == 0 else None, base + first, size))
    total = len(chunks)

    def landed(c):
        index, block, _, _ = chunks[c]
        if not plan[index][0] or block is None:
            return
        if block > 0:
            arrivals[index, ORDER[block]].wait_recv()
        if block in LEAVE:
            left, leaving = LEAVE[block]
            for k in left:
                arrivals[index, k].wait_send()
            for k in leaving:
                arrivals[index, k].start()

    def place_of(c, ref_list):
        index, _, start, size = chunks[c]
        if isinstance(start, int):
            return ref_list[index].at[pl.ds(start, size)]
        return ref_list[index].at[pl.ds(pl.multiple_of(start, 16), size)]

    def held(c, which):
        return buffers[5 * chunks[c][0] + which].at[c % SLOTS]

    def given(c):
        index, _, _, size = chunks[c]
        away = plan[index][0] and size * (c - starts[index]) >= plan[index][1]
        return place_of(c, lands if away else sources)

    def inward(c):
        return pltpu.make_async_remote_copy(
            src_ref=given(c),
            dst_ref=held(c, 1),
            send_sem=a_send.at[c % SLOTS],
            recv_sem=a_recv.at[c % SLOTS],
            device_id={"seq": partner},
            device_id_type=pl.DeviceIdType.MESH,
        )

    def crossing(c):
        return pltpu.make_async_remote_copy(
            src_ref=held(c, 2),
            dst_ref=held(c, 3),
            send_sem=b_send.at[c % SLOTS],
            recv_sem=b_recv.at[c % SLOTS],
            device_id={"seq": across},
            device_id_type=pl.DeviceIdType.MESH,
        )

    def outward(c):
        return pltpu.make_async_remote_copy(
            src_ref=held(c, 4),
            dst_ref=place_of(c, results),
            send_sem=c_send.at[c % SLOTS],
            recv_sem=c_recv.at[c],
            device_id={"seq": partner},
            device_id_type=pl.DeviceIdType.MESH,
        )

    def fetch(c):
        return pltpu.make_async_copy(given(c), held(c, 0), g_sem.at[c % SLOTS])

    def keep(c):
        return pltpu.make_async_copy(held(c, 4), place_of(c, results), out_sem.at[c % SLOTS])

    @pl.when(middle == 0)
    def _():
        for c in range(total):
            landed(c)
            if c >= SLOTS:
                inward(c - SLOTS).wait_send()
                pl.semaphore_wait(a_free, 1)
            inward(c).start()
        for c in range(max(0, total - SLOTS), total):
            inward(c).wait_send()
        for c in range(total):
            outward(c).wait_recv()

    @pl.when(middle == 1)
    def _():
        for c in range(min(SLOTS, total)):
            landed(c)
            fetch(c).start()
        for i in range(total + 1):
            c = i
            if c < total:
                fetch(c).wait()
                inward(c).wait_recv()
                if c >= SLOTS:
                    crossing(c - SLOTS).wait_send()
                held(c, 2)[...] = (
                    held(c, 0)[...].astype(f32) + held(c, 1)[...].astype(f32)
                ).astype(bf16)
                if c + SLOTS < total:
                    pl.semaphore_signal(
                        a_free, device_id={"seq": partner}, device_id_type=pl.DeviceIdType.MESH
                    )
                if c >= SLOTS:
                    pl.semaphore_wait(b_free, 1)
                crossing(c).start()
                if c + SLOTS < total:
                    landed(c + SLOTS)
                    fetch(c + SLOTS).start()
            c = i - 1
            if c >= 0:
                crossing(c).wait_recv()
                if c >= SLOTS:
                    keep(c - SLOTS).wait()
                    outward(c - SLOTS).wait_send()
                held(c, 4)[...] = (
                    held(c, 2)[...].astype(f32) + held(c, 3)[...].astype(f32)
                ).astype(bf16)
                if c + SLOTS < total:
                    pl.semaphore_signal(
                        b_free, device_id={"seq": across}, device_id_type=pl.DeviceIdType.MESH
                    )
                outward(c).start()
                keep(c).start()
        for c in range(max(0, total - SLOTS), total):
            crossing(c).wait_send()
            keep(c).wait()
            outward(c).wait_send()

    for (_, k), copy in arrivals.items():
        if k in (1, 6, 7):
            copy.wait_send()


def combine(arrays, number):
    plan = []
    for value, swapped, size in arrays:
        rows = value.shape[0] // 8 if swapped else value.shape[0]
        plan.append((swapped, rows, 8 if swapped else 1, size))
    count = len(plan)
    total = sum(rows // size * blocks for _, rows, blocks, size in plan)
    shapes = [jax.ShapeDtypeStruct(value.shape, bf16) for value, _, _ in arrays]
    lands = [
        jax.ShapeDtypeStruct(value.shape if swapped else (16, 128), bf16)
        for value, swapped, _ in arrays
    ]
    buffers = [
        pltpu.VMEM((SLOTS, size, value.shape[1]), bf16)
        for value, _, size in arrays
        for _ in range(5)
    ]
    dma = pltpu.SemaphoreType.DMA
    moved = sum(value.size for value, _, _ in arrays)
    anywhere = pl.BlockSpec(memory_space=pl.ANY)
    return pl.pallas_call(
        functools.partial(combine_kernel, tuple(plan)),
        out_shape=shapes + lands,
        in_specs=[anywhere] * count,
        out_specs=[anywhere] * (2 * count),
        scratch_shapes=buffers
        + [
            dma((count, 8)),
            dma((count, 8)),
            dma((SLOTS,)),
            dma((SLOTS,)),
            dma((SLOTS,)),
            dma((SLOTS,)),
            dma((SLOTS,)),
            dma((SLOTS,)),
            dma((total,)),
            dma((SLOTS,)),
            pltpu.SemaphoreType.REGULAR,
            pltpu.SemaphoreType.REGULAR,
        ],
        compiler_params=pltpu.CompilerParams(
            collective_id=number, has_side_effects=True, vmem_limit_bytes=48 * 1024 * 1024
        ),
        cost_estimate=pl.CostEstimate(
            flops=2 * moved, bytes_accessed=200 * moved, transcendentals=0
        ),
        name="combine_%d" % number,
    )(*[value for value, _, _ in arrays])[:count]


def middle_kernel(joined, x, u, w_gate, w_lift, w_down, scale, inner, *outs):
    gate = jnp.dot(x[...], w_gate[...], preferred_element_type=f32)
    lift = jnp.dot(x[...], w_lift[...], preferred_element_type=f32)
    raw = lax.dot_general(
        u[...], w_down[...], (((1,), (1,)), ((), ())), preferred_element_type=f32
    )
    sigma = 1.0 / (1.0 + jnp.exp(-gate))
    silu = gate * sigma
    product = silu * lift
    outs[-1][...] = jnp.sum(product * raw, axis=1, keepdims=True)
    inner[...] = (product * scale[...]).astype(bf16)
    grad = raw * scale[...]
    grad_gate = (grad * lift * sigma * (1.0 + gate * (1.0 - sigma))).astype(bf16)
    grad_lift = (grad * silu).astype(bf16)
    if joined:
        width = grad_gate.shape[1]
        outs[0][:, :width] = grad_gate
        outs[0][:, width:] = grad_lift
    else:
        outs[0][...] = grad_gate
        outs[1][...] = grad_lift


def middle(x, u, w_gate, w_lift, w_down, scale):
    joined = w_lift is None
    rows, hidden = x.shape[0], w_down.shape[0]
    tile = 256
    whole = dict(pipeline_mode=pl.Buffered(1))
    grads = [hidden * 2] if joined else [hidden, hidden]
    return pl.pallas_call(
        functools.partial(middle_kernel, joined),
        grid=(rows // tile,),
        in_specs=[
            pl.BlockSpec((tile, D), lambda i: (i, 0)),
            pl.BlockSpec((tile, D), lambda i: (i, 0)),
            pl.BlockSpec((D, hidden), lambda i: (0, 0), **whole),
            pl.BlockSpec((D, hidden), lambda i: (0, 1 if joined else 0), **whole),
            pl.BlockSpec((hidden, D), lambda i: (0, 0), **whole),
            pl.BlockSpec((tile, 1), lambda i: (i, 0)),
        ],
        out_specs=[pl.BlockSpec((tile, w), lambda i: (i, 0)) for w in [hidden] + grads + [1]],
        out_shape=[jax.ShapeDtypeStruct((rows, w), bf16) for w in [hidden] + grads]
        + [jax.ShapeDtypeStruct((rows, 1), f32)],
        compiler_params=pltpu.CompilerParams(vmem_limit_bytes=52 * 1024 * 1024),
        cost_estimate=pl.CostEstimate(
            flops=6 * rows * D * hidden,
            bytes_accessed=2 * (2 * rows * D + 3 * hidden * D + 3 * rows * hidden),
            transcendentals=rows * hidden,
        ),
    )(x, u, w_gate, w_gate if joined else w_lift, w_down, scale)


def window(blocks, first, count, axis):
    size = blocks[0].shape[axis]
    return lax.dynamic_slice_in_dim(
        jnp.concatenate(blocks, axis=axis), first * size, count * size, axis
    )


def gather_seq(value):
    seq, place = lax.axis_size("seq"), lax.axis_index("seq")
    if seq != 4:
        return lax.all_gather(value, "seq", axis=0, tiled=True)
    lower, higher, up, down = [], [], value, value
    for hop in range(seq - 1):
        up = lax.ppermute(up, "seq", [(i, i + 1) for i in range(hop, seq - 1)])
        down = lax.ppermute(down, "seq", [(i + 1, i) for i in range(seq - 1 - hop)])
        lower.insert(0, up)
        higher.append(down)
    return window(lower + [value] + higher, seq - 1 - place, seq, 0)


def together(*values):
    return lax.optimization_barrier(values)


def exchange_seq(value, axis_out, axis_in):
    seq, place = lax.axis_size("seq"), lax.axis_index("seq")
    if seq != 4:
        return lax.all_to_all(value, "seq", axis_out, axis_in, tiled=True)
    size = value.shape[axis_out] // seq
    came = []
    for shift in range(seq):
        block = lax.dynamic_slice_in_dim(value, lax.rem(place + shift, seq) * size, size, axis_out)
        if shift:
            block = lax.ppermute(block, "seq", [(i, (i + shift) % seq) for i in range(seq)])
        came.append(block)
    order = [came[shift % seq] for shift in range(seq - 1, -seq, -1)]
    return window(order, seq - 1 - place, seq, axis_in)


def swap(value):
    return lax.all_to_all(value, "fsdp", 0, 0, tiled=True)


def scatter(value):
    size = lax.axis_size("fsdp")
    return jnp.sum(swap(value.reshape(size, -1, value.shape[-1])).astype(f32), axis=0)


def on_device(
    tokens,
    segments,
    expert_ids,
    expert_gates,
    attn_gain,
    qkv_weight,
    qkv_bias,
    out_weight,
    ffn_gain,
    shared_gate_up,
    shared_down,
    shared_gate,
    expert_gate_up,
    expert_down,
    cotangent,
):
    fsdp, seq = lax.axis_size("fsdp"), lax.axis_size("seq")
    me, place = lax.axis_index("fsdp"), lax.axis_index("seq")
    row_count, length = tokens.shape[1], segments.shape[1]
    heads = HEADS // seq
    group = heads * HEAD_DIM
    copies = fsdp // EXPERTS
    width = D // fsdp
    hidden_own = FF_EXPERT // copies
    piece = hidden_own // fsdp
    factor = 1.0 / math.sqrt(HEAD_DIM)
    capacity = length * TOP // EXPERTS

    all_tokens = gather_seq(tokens[0])
    own = [
        lax.dynamic_slice_in_dim(qkv_weight, part * D + place * group, group, 1)
        for part in range(3)
    ]
    vectors = jnp.concatenate([attn_gain, ffn_gain, shared_gate, qkv_bias])
    extra = -(-6 * width // (3 * group) // 16) * 16
    vectors = jnp.pad(vectors, (0, extra * 3 * group - 6 * width)).reshape(extra, 3 * group)
    gathered = lax.all_gather(
        jnp.concatenate([jnp.concatenate(own, axis=1), vectors], axis=0), "fsdp", axis=0
    )
    weight_qkv = gathered[:, :width].reshape(D, 3 * group)
    vectors = gathered[:, width:].reshape(fsdp, -1)
    gain_one = vectors[:, :width].reshape(D).astype(f32)
    gain_two = vectors[:, width : 2 * width].reshape(D).astype(f32)
    gate_vector = vectors[:, 2 * width : 3 * width].reshape(D)
    bias = vectors[:, 3 * width : 6 * width].reshape(3, seq, group)
    bias = lax.dynamic_index_in_dim(bias, place, 1, keepdims=False).reshape(-1).astype(f32)
    weight_out = lax.all_gather(out_weight, "fsdp", axis=0, tiled=True)
    upstream_all = lax.all_gather(cotangent[0], "fsdp", axis=0, tiled=True)

    up_sent = expert_gate_up.reshape(EXPERTS, width, 2, fsdp, copies, piece)
    up_sent = up_sent.transpose(0, 4, 1, 2, 3, 5).reshape(fsdp, width, 2 * hidden_own)
    down_sent = expert_down.reshape(fsdp, piece, D)
    if seq == 4:
        half = lax.rem(place, 2)
        fetched = swap(lax.dynamic_slice_in_dim(up_sent, half * (width // 2), width // 2, 1))
        given = lax.ppermute(fetched, "seq", [(0, 1), (1, 0), (2, 3), (3, 2)])
    else:
        fetched = given = swap(up_sent)

    x_all = all_tokens.astype(f32)
    normed_unit = x_all * rms_scale(x_all)
    normed = (normed_unit * gain_one).astype(bf16)
    cosine, sine = rope_tables(jnp.arange(length, dtype=jnp.int32))
    normed = after(normed, weight_qkv)
    joined = dot(normed, weight_qkv, ((1,), (0,))) + bias
    split = joined.reshape(length, 3, heads, HEAD_DIM)
    queries = rotate(split[:, 0], cosine, sine).astype(bf16)
    keys = rotate(split[:, 1], cosine, sine).astype(bf16)
    values = split[:, 2].astype(bf16)
    documents = segments[0]
    mixed, logs = attend(queries, keys, values, documents, factor)
    mixed_rows = exchange_seq(mixed.reshape(length, group), 0, 1)
    mixed_rows = after(mixed_rows, upstream_all)
    inputs = tokens[0].astype(f32)
    hidden = inputs + dot(mixed_rows, weight_out, ((1,), (0,)))
    scale_two = rms_scale(hidden)
    second = (hidden * scale_two * gain_two).astype(bf16)
    second_all = lax.all_gather(after(second, fetched), "fsdp", axis=0, tiled=True)

    names = jnp.arange(EXPERTS, dtype=jnp.int32)
    matches = expert_ids[0][None, :, :] == names[:, None, None]
    gates = jnp.sum(jnp.where(matches, expert_gates[0][None], 0.0), axis=-1)
    gates = jnp.where(jnp.any(matches, axis=-1), gates, -1.0)
    gates = lax.all_gather(after(gates.reshape(-1), second), ("seq", "fsdp"), axis=0)
    gates = gates.reshape(seq, fsdp, EXPERTS, row_count)
    gates = lax.dynamic_index_in_dim(gates, me // copies, 2, keepdims=False)
    gates = gates.transpose(1, 0, 2).reshape(fsdp, length)
    chosen = (gates >= 0.0).astype(jnp.int32)
    earlier = jnp.cumsum(chosen, axis=1) - chosen
    share = jnp.where((chosen > 0) & (earlier < capacity), gates, 0.0)
    share = lax.dynamic_slice_in_dim(share, place * row_count, row_count, 1).reshape(-1, 1)

    weight_down = swap(after(down_sent, second_all)).reshape(hidden_own, D)
    weight_up, fetched = after((given, fetched), second_all)
    if seq == 4:
        weight_up = jnp.concatenate(
            [jnp.where(half == 0, fetched, weight_up), jnp.where(half == 0, weight_up, fetched)],
            axis=1,
        )
    weight_up = weight_up.reshape(D, 2 * hidden_own)

    by_kernel = seq == 4 and fsdp == 8
    s_gate, s_lift = shared_gate_up[:, 0], shared_gate_up[:, 1]
    opening_all = jax.nn.sigmoid(dot(second_all, gate_vector, ((1,), (0,))))[:, None]
    inner_s, ga_s, gl_s, reach = middle(
        second_all, upstream_all, s_gate, s_lift, shared_down, opening_all
    )
    grad_s_down = dot(inner_s, upstream_all, ((0,), (0,)), bf16)
    grad_s_gate = dot(second_all, ga_s, ((0,), (0,)), bf16)
    grad_s_lift = dot(second_all, gl_s, ((0,), (0,)), bf16)

    held = after(second_all, grad_s_down, grad_s_gate, grad_s_lift)
    if hidden_own % 128 == 0:
        inner_e, grads_e, _ = middle(held, upstream_all, weight_up, None, weight_down, share)
    else:
        inner_e, ga_e, gl_e, _ = middle(
            held,
            upstream_all,
            weight_up[:, :hidden_own],
            weight_up[:, hidden_own:],
            weight_down,
            share,
        )
        grads_e = jnp.concatenate([ga_e, gl_e], axis=1)
    part = dot(inner_e, upstream_all, ((0,), (0,)), bf16)
    grad_e_down = part
    reach = jnp.sum(swap(after(reach.reshape(fsdp, row_count), part)), axis=0)

    grads_e, ga_s, gl_s = after((grads_e, ga_s, gl_s), part)
    grad_second_all = (
        dot(ga_s, s_gate, ((1,), (1,)))
        + dot(gl_s, s_lift, ((1,), (1,)))
        + dot(grads_e, weight_up, ((1,), (1,)))
    ).astype(bf16)
    grad_second = scatter(grad_second_all)

    grad_e_up = dot(second_all, after(grads_e, grad_second_all), ((0,), (0,)), bf16)

    inner_s, inner_e = after((inner_s, inner_e), grad_e_up)
    out_all = (
        dot(inner_s, shared_down, ((1,), (0,))) + dot(inner_e, weight_down, ((1,), (0,)))
    ).astype(bf16)

    if by_kernel:
        shared = after((grad_s_down, grad_s_gate, grad_s_lift), out_all)
        sum_s = combine([(shared[0], False, 64), (shared[1], False, 256), (shared[2], False, 256)], 2)
        out_all = after(out_all, *sum_s)
    else:
        sum_s = lax.psum((grad_s_down, grad_s_gate, grad_s_lift), "seq")

    grad_second, reach = after((grad_second, reach), out_all)
    upstream = cotangent[0].astype(f32)
    opening = jax.nn.sigmoid(dot(second, gate_vector, ((1,), (0,))))
    grad_logit = reach * opening * (1.0 - opening)
    grad_second = grad_second + grad_logit[:, None] * gate_vector.astype(f32)[None, :]
    grad_gate_vector = jnp.sum(grad_logit[:, None] * second.astype(f32), axis=0)
    grad_hidden = upstream + norm_back(hidden, scale_two, gain_two, grad_second)
    grad_gain_two = jnp.sum(grad_second * hidden * scale_two, axis=0)
    grad_projected = grad_hidden.astype(bf16)
    grad_mixture = dot(grad_projected, weight_out, ((1,), (1,)), bf16)
    grad_heads = exchange_seq(grad_mixture, 1, 0)
    grad_out = dot(mixed_rows, after(grad_projected, grad_mixture), ((0,), (0,)), bf16)

    grad_heads = after(grad_heads, grad_out)
    grad_queries, grad_keys, grad_values = attend_back(
        queries,
        keys,
        values,
        documents,
        factor,
        logs,
        grad_heads.reshape(length, heads, HEAD_DIM),
    )
    grad_joined = jnp.stack(
        [
            rotate_back(grad_queries.astype(bf16).astype(f32), cosine, sine),
            rotate_back(grad_keys.astype(bf16).astype(f32), cosine, sine),
            grad_values,
        ],
        axis=1,
    )
    grad_joined = grad_joined.reshape(length, 3 * group).astype(bf16)
    grad_normed_all = dot(grad_joined, weight_qkv, ((1,), (1,)))
    grad_gain_one = jnp.sum(grad_normed_all * normed_unit, axis=0)

    grad_qkv = dot(normed, grad_joined, ((0,), (0,)), bf16).reshape(fsdp, width, 3 * group)
    grad_bias = jnp.sum(grad_joined.astype(f32), axis=0).reshape(3, 1, group)
    own_heads = (jnp.arange(seq, dtype=jnp.int32) == place).astype(f32)
    grad_bias = (grad_bias * own_heads[None, :, None]).reshape(fsdp, 3 * width)
    rows = jnp.concatenate(
        [
            grad_gain_one.reshape(fsdp, width),
            grad_gain_two.reshape(fsdp, width),
            grad_gate_vector.reshape(fsdp, width),
            grad_bias,
        ],
        axis=1,
    ).astype(bf16)
    rows = jnp.pad(rows, ((0, 0), (0, extra * 3 * group - 6 * width)))
    rows = rows.reshape(fsdp, extra, 3 * group)
    grad_qkv = jnp.concatenate([grad_qkv, rows], axis=1)

    grad_out = scatter(grad_out).astype(bf16)
    grad_normed_all = grad_normed_all.astype(bf16)
    grad_e_up, grad_out, grad_qkv, grad_normed_all, out_all = together(
        grad_e_up, grad_out, grad_qkv, grad_normed_all, out_all
    )
    grad_qkv = lax.psum_scatter(
        grad_qkv.reshape(-1, 3 * group), "fsdp", scatter_dimension=0, tiled=True
    )
    grad_normed = lax.psum_scatter(grad_normed_all, "seq", scatter_dimension=0, tiled=True)
    out_part = lax.psum_scatter(out_all, "fsdp", scatter_dimension=0, tiled=True)
    if by_kernel:
        sum_e_up, sum_e_down, sum_out = combine(
            [(grad_e_up, True, 64), (grad_e_down, True, 176), (grad_out, False, 64)], 1
        )
        sum_e_up = sum_e_up.reshape(EXPERTS, width, 2 * FF_EXPERT)
        sum_e_down = sum_e_down.reshape(EXPERTS, piece, D)
    else:
        sum_e_up = swap(grad_e_up.reshape(fsdp, width, 2 * hidden_own))
        sum_e_down = swap(grad_e_down.reshape(fsdp, piece, D))
        sum_e_up, sum_e_down, sum_out = lax.psum((sum_e_up, sum_e_down, grad_out), "seq")
        sum_e_down = sum_e_down.reshape(EXPERTS, copies * piece, D)
        sum_e_up = sum_e_up.reshape(EXPERTS, copies, width, 2, fsdp, piece)
        sum_e_up = sum_e_up.transpose(0, 2, 3, 4, 1, 5).reshape(EXPERTS, width, 2 * FF_EXPERT)
    output = (hidden + out_part.astype(f32)).astype(bf16)
    grad_normed = grad_normed.astype(f32)
    grad_qkv = lax.all_gather(grad_qkv, "seq", axis=0)
    rows = jnp.sum(grad_qkv[:, width:].astype(f32), axis=0).reshape(-1)
    grad_qkv = jnp.concatenate(
        [
            grad_qkv[owner, :width, part * group : (part + 1) * group]
            for part in range(3)
            for owner in range(seq)
        ],
        axis=1,
    ).astype(f32)
    input_grad = (grad_hidden + norm_back(inputs, rms_scale(inputs), gain_one, grad_normed)).astype(
        bf16
    )
    sum_s_up = jnp.stack([sum_s[1], sum_s[2]], axis=1)

    return (
        output[None],
        input_grad[None],
        rows[:width],
        grad_qkv,
        rows[3 * width : 6 * width],
        sum_out.astype(f32),
        rows[width : 2 * width],
        sum_s_up.astype(f32),
        sum_s[0].astype(f32),
        rows[2 * width : 3 * width],
        sum_e_up.astype(f32),
        sum_e_down.astype(f32),
    )


def solution(mesh):
    return jax.shard_map(
        on_device,
        mesh=mesh,
        in_specs=(
            P("fsdp", "seq", None),
            P("fsdp", None),
            P("fsdp", "seq", None),
            P("fsdp", "seq", None),
            P("fsdp"),
            P("fsdp", None),
            P("fsdp"),
            P("fsdp", None),
            P("fsdp"),
            P(None, None, "fsdp"),
            P("fsdp", None),
            P("fsdp"),
            P(None, "fsdp", None),
            P(None, "fsdp", None),
            P("fsdp", "seq", None),
        ),
        out_specs=(
            P("fsdp", "seq", None),
            P("fsdp", "seq", None),
            P("fsdp"),
            P("fsdp", None),
            P("fsdp"),
            P("fsdp", None),
            P("fsdp"),
            P(None, None, "fsdp"),
            P("fsdp", None),
            P("fsdp"),
            P(None, "fsdp", None),
            P(None, "fsdp", None),
        ),
        check_vma=False,
    )
```

```python
import functools
import math

import jax
import jax.numpy as jnp
from jax import lax
from jax.experimental import pallas as pl
from jax.experimental.pallas import tpu as pltpu
from jax.sharding import PartitionSpec as P

D = 2048
HEADS = 16
HEAD_DIM = 128
FF_EXPERT = 1408
TOP = 4
EXPERTS = 8
QBLOCK = 256
DOC_MOST = 512

EPSILON = 1e-06
THETA = 1000000.0

bf16 = jnp.bfloat16
f32 = jnp.float32


def dot(a, b, contract, kind=f32):
    return lax.dot_general(a, b, (contract, ((), ())), preferred_element_type=f32).astype(kind)


def rms_scale(values):
    return lax.rsqrt(jnp.mean(values * values, axis=-1, keepdims=True) + EPSILON)


def norm_back(values, scale, gain, grad):
    scaled = grad * gain
    centre = jnp.mean(scaled * values, axis=-1, keepdims=True)
    return scale * (scaled - values * (scale * scale) * centre)


def rope_tables(positions):
    steps_half = jnp.arange(HEAD_DIM // 2, dtype=jnp.int32).astype(f32)
    frequency = jnp.exp(steps_half * (-2.0 * math.log(THETA) / HEAD_DIM))
    angles = positions.astype(f32)[:, None] * frequency[None, :]
    angles = jnp.concatenate([angles, angles], axis=-1)
    return (jnp.cos(angles), jnp.sin(angles))


def rotate(rows, cosine, sine):
    middle = rows.shape[-1] // 2
    turned = jnp.concatenate([-rows[..., middle:], rows[..., :middle]], axis=-1)
    return rows * cosine[:, None, :] + turned * sine[:, None, :]


def rotate_back(rows, cosine, sine):
    middle = rows.shape[-1] // 2
    turned = rows * sine[:, None, :]
    turned = jnp.concatenate([turned[..., middle:], -turned[..., :middle]], axis=-1)
    return rows * cosine[:, None, :] + turned


def key_start(block):
    return max(0, block * QBLOCK - DOC_MOST)


def block_scores(block, queries, keys, documents, factor):
    first, start = block * QBLOCK, key_start(block)
    stop = first + QBLOCK
    scores = (
        jnp.einsum(
            "qhd,khd->hqk", queries[first:stop], keys[start:stop], preferred_element_type=f32
        )
        * factor
    )
    rows = first + jnp.arange(QBLOCK, dtype=jnp.int32)
    columns = start + jnp.arange(stop - start, dtype=jnp.int32)
    allowed = (rows[:, None] >= columns[None, :]) & (
        documents[first:stop, None] == documents[None, start:stop]
    )
    return jnp.where(allowed[None], scores, -1e30)


def attend(queries, keys, values, documents, factor):
    mixed, logs = [], []
    for block in range(queries.shape[0] // QBLOCK):
        start, stop = key_start(block), (block + 1) * QBLOCK
        scores = block_scores(block, queries, keys, documents, factor)
        top = jnp.max(scores, axis=-1, keepdims=True)
        weights = jnp.exp(scores - top)
        totals = jnp.sum(weights, axis=-1, keepdims=True)
        probability = (weights / totals).astype(bf16)
        mixed.append(
            jnp.einsum(
                "hqk,khd->qhd", probability, values[start:stop], preferred_element_type=f32
            ).astype(bf16)
        )
        logs.append(top + jnp.log(totals))
    return jnp.concatenate(mixed, axis=0), logs


def attend_back(queries, keys, values, documents, factor, logs, grads):
    length = queries.shape[0]
    grad_queries = []
    grad_keys = jnp.zeros(keys.shape, f32)
    grad_values = jnp.zeros(values.shape, f32)
    for block in range(length // QBLOCK):
        start, stop = key_start(block), (block + 1) * QBLOCK
        scores = block_scores(block, queries, keys, documents, factor)
        probability = jnp.exp(scores - logs[block])
        grad_block = grads[block * QBLOCK : stop]
        query_block = queries[block * QBLOCK : stop]
        grad_values = grad_values.at[start:stop].add(
            jnp.einsum(
                "hqk,qhd->khd", probability.astype(bf16), grad_block, preferred_element_type=f32
            )
        )
        grad_probability = jnp.einsum(
            "qhd,khd->hqk", grad_block, values[start:stop], preferred_element_type=f32
        )
        centre = jnp.sum(grad_probability * probability, axis=-1, keepdims=True)
        grad_scores = (probability * (grad_probability - centre)).astype(bf16)
        grad_queries.append(
            jnp.einsum("hqk,khd->qhd", grad_scores, keys[start:stop], preferred_element_type=f32)
            * factor
        )
        grad_keys = grad_keys.at[start:stop].add(
            jnp.einsum("hqk,qhd->khd", grad_scores, query_block, preferred_element_type=f32)
            * factor
        )
    return jnp.concatenate(grad_queries, axis=0), grad_keys, grad_values


def after(value, *earlier):
    return lax.optimization_barrier((value, earlier))[0]


def line_neighbours(place):
    middle = lax.rem(place + 1, 4) // 2
    low = 1 - place // 2
    partner = low * (1 - place) + (1 - low) * (5 - place)
    across = low * 2 + (1 - low) * 1
    return middle, partner, across


def flip(index, bits):
    result, step = 0, 1
    while step < 8:
        bit = lax.rem(index // step, 2)
        result = result + step * (1 - bit if bits & step else bit)
        step *= 2
    return result


SLOTS = 4
ORDER = (0, 1, 2, 4, 3, 5, 6, 7)
LEAVE = {2: ((2, 4), (3, 5)), 4: ((3, 5), (6, 7))}


def combine_kernel(plan, *refs):
    count = len(plan)
    sources, refs = refs[:count], refs[count:]
    results, refs = refs[:count], refs[count:]
    lands, refs = refs[:count], refs[count:]
    buffers, refs = refs[: 5 * count], refs[5 * count :]
    (land_send, land_recv, g_sem, a_send, a_recv, b_send, b_recv, c_send, c_recv) = refs[:9]
    out_sem, a_free, b_free = refs[9:]
    me, place = lax.axis_index("fsdp"), lax.axis_index("seq")
    middle, partner, across = line_neighbours(place)
    peers = [flip(me, k) for k in range(8)]

    barrier = pltpu.get_barrier_semaphore()
    swapping = any(swapped for swapped, _, _, _ in plan)
    if swapping:
        for k in range(1, 8):
            pl.semaphore_signal(
                barrier, device_id={"fsdp": peers[k]}, device_id_type=pl.DeviceIdType.MESH
            )
    pl.semaphore_signal(
        barrier, device_id={"seq": partner}, device_id_type=pl.DeviceIdType.MESH
    )

    @pl.when(middle == 1)
    def _():
        pl.semaphore_signal(
            barrier, device_id={"seq": across}, device_id_type=pl.DeviceIdType.MESH
        )

    pl.semaphore_wait(barrier, 1 + middle + (7 if swapping else 0))

    arrivals = {}
    for index, (swapped, rows, blocks, _) in enumerate(plan):
        if not swapped:
            continue
        here = pl.ds(pl.multiple_of(me * rows, 16), rows)
        for k in range(1, 8):
            there = pl.ds(pl.multiple_of(peers[k] * rows, 16), rows)
            copy = pltpu.make_async_remote_copy(
                src_ref=sources[index].at[there],
                dst_ref=lands[index].at[here],
                send_sem=land_send.at[index, k],
                recv_sem=land_recv.at[index, k],
                device_id={"fsdp": peers[k]},
                device_id_type=pl.DeviceIdType.MESH,
            )
            arrivals[index, k] = copy
            if k in (1, 2, 4):
                copy.start()

    chunks, starts = [], []
    for index, (swapped, rows, blocks, size) in enumerate(plan):
        starts.append(len(chunks))
        for block in range(blocks):
            base = (peers[ORDER[block]] if swapped else block) * rows
            for first in range(0, rows, size):
                chunks.append((index, block if first == 0 else None, base + first, size))
    total = len(chunks)

    def landed(c):
        index, block, _, _ = chunks[c]
        if not plan[index][0] or block is None:
            return
        if block > 0:
            arrivals[index, ORDER[block]].wait_recv()
        if block in LEAVE:
            left, leaving = LEAVE[block]
            for k in left:
                arrivals[index, k].wait_send()
            for k in leaving:
                arrivals[index, k].start()

    def place_of(c, ref_list):
        index, _, start, size = chunks[c]
        if isinstance(start, int):
            return ref_list[index].at[pl.ds(start, size)]
        return ref_list[index].at[pl.ds(pl.multiple_of(start, 16), size)]

    def held(c, which):
        return buffers[5 * chunks[c][0] + which].at[c % SLOTS]

    def given(c):
        index, _, _, size = chunks[c]
        away = plan[index][0] and size * (c - starts[index]) >= plan[index][1]
        return place_of(c, lands if away else sources)

    def inward(c):
        return pltpu.make_async_remote_copy(
            src_ref=given(c),
            dst_ref=held(c, 1),
            send_sem=a_send.at[c % SLOTS],
            recv_sem=a_recv.at[c % SLOTS],
            device_id={"seq": partner},
            device_id_type=pl.DeviceIdType.MESH,
        )

    def crossing(c):
        return pltpu.make_async_remote_copy(
            src_ref=held(c, 2),
            dst_ref=held(c, 3),
            send_sem=b_send.at[c % SLOTS],
            recv_sem=b_recv.at[c % SLOTS],
            device_id={"seq": across},
            device_id_type=pl.DeviceIdType.MESH,
        )

    def outward(c):
        return pltpu.make_async_remote_copy(
            src_ref=held(c, 4),
            dst_ref=place_of(c, results),
            send_sem=c_send.at[c % SLOTS],
            recv_sem=c_recv.at[c],
            device_id={"seq": partner},
            device_id_type=pl.DeviceIdType.MESH,
        )

    def fetch(c):
        return pltpu.make_async_copy(given(c), held(c, 0), g_sem.at[c % SLOTS])

    def keep(c):
        return pltpu.make_async_copy(held(c, 4), place_of(c, results), out_sem.at[c % SLOTS])

    @pl.when(middle == 0)
    def _():
        for c in range(total):
            landed(c)
            if c >= SLOTS:
                inward(c - SLOTS).wait_send()
                pl.semaphore_wait(a_free, 1)
            inward(c).start()
        for c in range(max(0, total - SLOTS), total):
            inward(c).wait_send()
        for c in range(total):
            outward(c).wait_recv()

    @pl.when(middle == 1)
    def _():
        for c in range(min(SLOTS, total)):
            landed(c)
            fetch(c).start()
        for i in range(total + 1):
            c = i
            if c < total:
                fetch(c).wait()
                inward(c).wait_recv()
                if c >= SLOTS:
                    crossing(c - SLOTS).wait_send()
                held(c, 2)[...] = (
                    held(c, 0)[...].astype(f32) + held(c, 1)[...].astype(f32)
                ).astype(bf16)
                if c + SLOTS < total:
                    pl.semaphore_signal(
                        a_free, device_id={"seq": partner}, device_id_type=pl.DeviceIdType.MESH
                    )
                if c >= SLOTS:
                    pl.semaphore_wait(b_free, 1)
                crossing(c).start()
                if c + SLOTS < total:
                    landed(c + SLOTS)
                    fetch(c + SLOTS).start()
            c = i - 1
            if c >= 0:
                crossing(c).wait_recv()
                if c >= SLOTS:
                    keep(c - SLOTS).wait()
                    outward(c - SLOTS).wait_send()
                held(c, 4)[...] = (
                    held(c, 2)[...].astype(f32) + held(c, 3)[...].astype(f32)
                ).astype(bf16)
                if c + SLOTS < total:
                    pl.semaphore_signal(
                        b_free, device_id={"seq": across}, device_id_type=pl.DeviceIdType.MESH
                    )
                outward(c).start()
                keep(c).start()
        for c in range(max(0, total - SLOTS), total):
            crossing(c).wait_send()
            keep(c).wait()
            outward(c).wait_send()

    for (_, k), copy in arrivals.items():
        if k in (1, 6, 7):
            copy.wait_send()


def combine(arrays, number):
    plan = []
    for value, swapped, size in arrays:
        rows = value.shape[0] // 8 if swapped else value.shape[0]
        plan.append((swapped, rows, 8 if swapped else 1, size))
    count = len(plan)
    total = sum(rows // size * blocks for _, rows, blocks, size in plan)
    shapes = [jax.ShapeDtypeStruct(value.shape, bf16) for value, _, _ in arrays]
    lands = [
        jax.ShapeDtypeStruct(value.shape if swapped else (16, 128), bf16)
        for value, swapped, _ in arrays
    ]
    buffers = [
        pltpu.VMEM((SLOTS, size, value.shape[1]), bf16)
        for value, _, size in arrays
        for _ in range(5)
    ]
    dma = pltpu.SemaphoreType.DMA
    moved = sum(value.size for value, _, _ in arrays)
    anywhere = pl.BlockSpec(memory_space=pl.ANY)
    return pl.pallas_call(
        functools.partial(combine_kernel, tuple(plan)),
        out_shape=shapes + lands,
        in_specs=[anywhere] * count,
        out_specs=[anywhere] * (2 * count),
        scratch_shapes=buffers
        + [
            dma((count, 8)),
            dma((count, 8)),
            dma((SLOTS,)),
            dma((SLOTS,)),
            dma((SLOTS,)),
            dma((SLOTS,)),
            dma((SLOTS,)),
            dma((SLOTS,)),
            dma((total,)),
            dma((SLOTS,)),
            pltpu.SemaphoreType.REGULAR,
            pltpu.SemaphoreType.REGULAR,
        ],
        compiler_params=pltpu.CompilerParams(
            collective_id=number, has_side_effects=True, vmem_limit_bytes=48 * 1024 * 1024
        ),
        cost_estimate=pl.CostEstimate(
            flops=2 * moved, bytes_accessed=200 * moved, transcendentals=0
        ),
        name="combine_%d" % number,
    )(*[value for value, _, _ in arrays])[:count]


HOST_BLOCKS = 8


def feed_forward_kernel(*refs):
    sources, refs = refs[:3], refs[3:]
    tiles_in, refs = refs[:5], refs[5:]
    weights, refs = refs[:5], refs[5:]
    share, refs = refs[0], refs[1:]
    results, refs = refs[:3], refs[3:]
    tiles_out, refs = refs[:4], refs[4:]
    zg, za, zs, zb, zt = refs[:5]
    refs = refs[5:]
    held, refs = refs[:5], refs[5:]
    v_up, v_down, v_sg, v_sl, v_sd = held
    loaded, refs = refs[:5], refs[5:]
    v_x, v_u, v_ga, v_gl, v_in = loaded
    stored, refs = refs[:4], refs[4:]
    t_in, t_grads, t_second, t_out = stored
    (w_sem, l_sem, s_sem, g_sem, a_send, a_recv, b_send, b_recv, c_send, c_recv) = refs[:10]
    out_sem, a_free, b_free = refs[10:]
    place = lax.axis_index("seq")
    middle, partner, across = line_neighbours(place)
    tile = v_x.shape[1]
    hidden = v_down.shape[0]
    last = HOST_BLOCKS - 1

    for index in range(5):
        pltpu.make_async_copy(weights[index], held[index], w_sem.at[index]).start()

    barrier = pltpu.get_barrier_semaphore()
    pl.semaphore_signal(
        barrier, device_id={"seq": partner}, device_id_type=pl.DeviceIdType.MESH
    )

    @pl.when(middle == 1)
    def _():
        pl.semaphore_signal(
            barrier, device_id={"seq": across}, device_id_type=pl.DeviceIdType.MESH
        )

    pl.semaphore_wait(barrier, 1 + middle)

    def rows(o):
        return pl.ds(o * tile if isinstance(o, int) else pl.multiple_of(o * tile, tile), tile)

    def slot(o):
        return o % 2 if isinstance(o, int) else lax.rem(o, 2)

    def remote(source, target, sent, received, where):
        return pltpu.make_async_remote_copy(
            src_ref=source,
            dst_ref=target,
            send_sem=sent,
            recv_sem=received,
            device_id={"seq": where},
            device_id_type=pl.DeviceIdType.MESH,
        )

    def inward(o, a):
        i = slot(o)
        return remote(
            sources[a].at[rows(o)], za.at[i, a], a_send.at[i, a], a_recv.at[i, a], partner
        )

    def crossing(o, a):
        i = slot(o)
        return remote(zs.at[i, a], zb.at[i, a], b_send.at[i, a], b_recv.at[i, a], across)

    def outward(o, a):
        i = slot(o)
        return remote(
            zt.at[i, a], results[a].at[rows(o)], c_send.at[i, a], c_recv.at[o, a], partner
        )

    def fetch(o, a):
        i = slot(o)
        return pltpu.make_async_copy(sources[a].at[rows(o)], zg.at[i, a], g_sem.at[i, a])

    def keep(o, a):
        i = slot(o)
        return pltpu.make_async_copy(zt.at[i, a], results[a].at[rows(o)], out_sem.at[i, a])

    def load(o, index):
        i = slot(o)
        return pltpu.make_async_copy(
            tiles_in[index].at[rows(o)], loaded[index].at[i], l_sem.at[i, index]
        )

    def store(o, index):
        return pltpu.make_async_copy(stored[index], tiles_out[index].at[rows(o)], s_sem.at[index])

    for index in range(5):
        load(0, index).start()

    @pl.when(middle == 0)
    def _():
        for o in (0, 1):
            for a in range(3):
                inward(o, a).start()

    @pl.when(middle == 1)
    def _():
        for o in (0, 1):
            for a in range(3):
                fetch(o, a).start()

    for index in range(5):
        pltpu.make_async_copy(weights[index], held[index], w_sem.at[index]).wait()

    def add(left, right):
        return (left.astype(f32) + right.astype(f32)).astype(bf16)

    def end_step(o):
        @pl.when((o >= 1) & (o < last))
        def _():
            for a in range(3):
                inward(o - 1, a).wait_send()
                pl.semaphore_wait(a_free, 1)
                inward(o + 1, a).start()

    def middle_step(o):
        @pl.when(o <= last)
        def _():
            i = slot(o)
            for a in range(3):
                fetch(o, a).wait()
                inward(o, a).wait_recv()

                @pl.when(o >= 2)
                def _():
                    crossing(o - 2, a).wait_send()
                    pl.semaphore_wait(b_free, 1)

                zs[i, a] = add(zg[i, a], za[i, a])
                crossing(o, a).start()

                @pl.when(o + 2 <= last)
                def _():
                    pl.semaphore_signal(
                        a_free, device_id={"seq": partner}, device_id_type=pl.DeviceIdType.MESH
                    )
                    fetch(o + 2, a).start()

        @pl.when(o >= 1)
        def _():
            p = o - 1
            i = slot(p)
            for a in range(3):
                crossing(p, a).wait_recv()

                @pl.when(p >= 2)
                def _():
                    keep(p - 2, a).wait()
                    outward(p - 2, a).wait_send()

                zt[i, a] = add(zs[i, a], zb[i, a])

                @pl.when(p + 2 <= last)
                def _():
                    pl.semaphore_signal(
                        b_free, device_id={"seq": across}, device_id_type=pl.DeviceIdType.MESH
                    )

                outward(p, a).start()
                keep(p, a).start()

    def across_rows(left, right):
        return lax.dot_general(left, right, (((1,), (1,)), ((), ())), preferred_element_type=f32)

    def host(o):
        i = slot(o)
        for index in range(5):
            load(o, index).wait()

        @pl.when(o < last)
        def _():
            for index in range(5):
                load(o + 1, index).start()

        @pl.when(o >= 1)
        def _():
            for index in range(4):
                store(o - 1, index).wait()

        scale = share[rows(o), :]
        cut = hidden // 256 * 128
        for first, end in ((0, cut), (cut, hidden)):
            gate = jnp.dot(v_x[i], v_up[:, first:end], preferred_element_type=f32)
            lift = jnp.dot(
                v_x[i], v_up[:, hidden + first : hidden + end], preferred_element_type=f32
            )
            grad = across_rows(v_u[i], v_down[first:end, :]) * scale
            sigma = 1.0 / (1.0 + jnp.exp(-gate))
            silu = gate * sigma
            t_in[:, first:end] = (silu * lift * scale).astype(bf16)
            t_grads[:, first:end] = (
                grad * lift * sigma * (1.0 + gate * (1.0 - sigma))
            ).astype(bf16)
            t_grads[:, hidden + first : hidden + end] = (grad * silu).astype(bf16)
        for first in range(0, D, 512):
            end = first + 512
            t_second[:, first:end] = (
                across_rows(t_grads[...], v_up[first:end, :])
                + across_rows(v_ga[i], v_sg[first:end, :])
                + across_rows(v_gl[i], v_sl[first:end, :])
            ).astype(bf16)
            t_out[:, first:end] = (
                jnp.dot(t_in[...], v_down[:, first:end], preferred_element_type=f32)
                + jnp.dot(v_in[i], v_sd[:, first:end], preferred_element_type=f32)
            ).astype(bf16)
        for index in range(4):
            store(o, index).start()

    def step(o, carry):
        @pl.when(middle == 0)
        def _():
            end_step(o)

        @pl.when(middle == 1)
        def _():
            middle_step(o)

        @pl.when(o <= last)
        def _():
            host(o)

        return carry

    lax.fori_loop(0, HOST_BLOCKS + 1, step, 0)
    for index in range(4):
        store(last, index).wait()

    @pl.when(middle == 0)
    def _():
        for a in range(3):
            for o in (last - 1, last):
                inward(o, a).wait_send()
            for o in range(HOST_BLOCKS):
                outward(o, a).wait_recv()

    @pl.when(middle == 1)
    def _():
        for a in range(3):
            for o in (last - 1, last):
                crossing(o, a).wait_send()
                keep(o, a).wait()
                outward(o, a).wait_send()


def feed_forward(sums, tiles, weights, share, number):
    rows, cut = sums[0].shape
    tile = rows // HOST_BLOCKS
    hidden = weights[1].shape[0]
    dma = pltpu.SemaphoreType.DMA
    anywhere = pl.BlockSpec(memory_space=pl.ANY)
    outs = [hidden, 2 * hidden, D, D]
    return pl.pallas_call(
        feed_forward_kernel,
        out_shape=[jax.ShapeDtypeStruct((rows, cut), bf16)] * 3
        + [jax.ShapeDtypeStruct((rows, w), bf16) for w in outs],
        in_specs=[anywhere] * 13 + [pl.BlockSpec(memory_space=pltpu.VMEM)],
        out_specs=[anywhere] * 7,
        scratch_shapes=[pltpu.VMEM((2, 3, tile, cut), bf16)] * 5
        + [pltpu.VMEM(w.shape, bf16) for w in weights]
        + [pltpu.VMEM((2, tile, t.shape[1]), bf16) for t in tiles]
        + [pltpu.VMEM((tile, w), bf16) for w in outs]
        + [
            dma((5,)),
            dma((2, 5)),
            dma((4,)),
            dma((2, 3)),
            dma((2, 3)),
            dma((2, 3)),
            dma((2, 3)),
            dma((2, 3)),
            dma((2, 3)),
            dma((HOST_BLOCKS, 3)),
            dma((2, 3)),
            pltpu.SemaphoreType.REGULAR,
            pltpu.SemaphoreType.REGULAR,
        ],
        compiler_params=pltpu.CompilerParams(
            collective_id=number, has_side_effects=True, vmem_limit_bytes=60 * 1024 * 1024
        ),
        cost_estimate=pl.CostEstimate(
            flops=2 * rows * D * (6 * hidden + 3 * cut),
            bytes_accessed=800 * 1024 * 1024,
            transcendentals=rows * hidden,
        ),
    )(*sums, *tiles, *weights, share)


def middle_kernel(joined, x, u, w_gate, w_lift, w_down, scale, inner, *outs):
    gate = jnp.dot(x[...], w_gate[...], preferred_element_type=f32)
    lift = jnp.dot(x[...], w_lift[...], preferred_element_type=f32)
    raw = lax.dot_general(
        u[...], w_down[...], (((1,), (1,)), ((), ())), preferred_element_type=f32
    )
    sigma = 1.0 / (1.0 + jnp.exp(-gate))
    silu = gate * sigma
    product = silu * lift
    outs[-1][...] = jnp.sum(product * raw, axis=1, keepdims=True)
    inner[...] = (product * scale[...]).astype(bf16)
    grad = raw * scale[...]
    grad_gate = (grad * lift * sigma * (1.0 + gate * (1.0 - sigma))).astype(bf16)
    grad_lift = (grad * silu).astype(bf16)
    if joined:
        width = grad_gate.shape[1]
        outs[0][:, :width] = grad_gate
        outs[0][:, width:] = grad_lift
    else:
        outs[0][...] = grad_gate
        outs[1][...] = grad_lift


def middle(x, u, w_gate, w_lift, w_down, scale):
    joined = w_lift is None
    rows, hidden = x.shape[0], w_down.shape[0]
    tile = 256
    whole = dict(pipeline_mode=pl.Buffered(1))
    grads = [hidden * 2] if joined else [hidden, hidden]
    return pl.pallas_call(
        functools.partial(middle_kernel, joined),
        grid=(rows // tile,),
        in_specs=[
            pl.BlockSpec((tile, D), lambda i: (i, 0)),
            pl.BlockSpec((tile, D), lambda i: (i, 0)),
            pl.BlockSpec((D, hidden), lambda i: (0, 0), **whole),
            pl.BlockSpec((D, hidden), lambda i: (0, 1 if joined else 0), **whole),
            pl.BlockSpec((hidden, D), lambda i: (0, 0), **whole),
            pl.BlockSpec((tile, 1), lambda i: (i, 0)),
        ],
        out_specs=[pl.BlockSpec((tile, w), lambda i: (i, 0)) for w in [hidden] + grads + [1]],
        out_shape=[jax.ShapeDtypeStruct((rows, w), bf16) for w in [hidden] + grads]
        + [jax.ShapeDtypeStruct((rows, 1), f32)],
        compiler_params=pltpu.CompilerParams(vmem_limit_bytes=52 * 1024 * 1024),
        cost_estimate=pl.CostEstimate(
            flops=6 * rows * D * hidden,
            bytes_accessed=2 * (2 * rows * D + 3 * hidden * D + 3 * rows * hidden),
            transcendentals=rows * hidden,
        ),
    )(x, u, w_gate, w_gate if joined else w_lift, w_down, scale)


def window(blocks, first, count, axis):
    size = blocks[0].shape[axis]
    return lax.dynamic_slice_in_dim(
        jnp.concatenate(blocks, axis=axis), first * size, count * size, axis
    )


def gather_seq(value):
    seq, place = lax.axis_size("seq"), lax.axis_index("seq")
    if seq != 4:
        return lax.all_gather(value, "seq", axis=0, tiled=True)
    lower, higher, up, down = [], [], value, value
    for hop in range(seq - 1):
        up = lax.ppermute(up, "seq", [(i, i + 1) for i in range(hop, seq - 1)])
        down = lax.ppermute(down, "seq", [(i + 1, i) for i in range(seq - 1 - hop)])
        lower.insert(0, up)
        higher.append(down)
    return window(lower + [value] + higher, seq - 1 - place, seq, 0)


def together(*values):
    return lax.optimization_barrier(values)


def exchange_seq(value, axis_out, axis_in):
    seq, place = lax.axis_size("seq"), lax.axis_index("seq")
    if seq != 4:
        return lax.all_to_all(value, "seq", axis_out, axis_in, tiled=True)
    size = value.shape[axis_out] // seq
    came = []
    for shift in range(seq):
        block = lax.dynamic_slice_in_dim(value, lax.rem(place + shift, seq) * size, size, axis_out)
        if shift:
            block = lax.ppermute(block, "seq", [(i, (i + shift) % seq) for i in range(seq)])
        came.append(block)
    order = [came[shift % seq] for shift in range(seq - 1, -seq, -1)]
    return window(order, seq - 1 - place, seq, axis_in)


def swap(value):
    return lax.all_to_all(value, "fsdp", 0, 0, tiled=True)


def scatter(value):
    size = lax.axis_size("fsdp")
    return jnp.sum(swap(value.reshape(size, -1, value.shape[-1])).astype(f32), axis=0)


def on_device(
    tokens,
    segments,
    expert_ids,
    expert_gates,
    attn_gain,
    qkv_weight,
    qkv_bias,
    out_weight,
    ffn_gain,
    shared_gate_up,
    shared_down,
    shared_gate,
    expert_gate_up,
    expert_down,
    cotangent,
):
    fsdp, seq = lax.axis_size("fsdp"), lax.axis_size("seq")
    me, place = lax.axis_index("fsdp"), lax.axis_index("seq")
    row_count, length = tokens.shape[1], segments.shape[1]
    heads = HEADS // seq
    group = heads * HEAD_DIM
    copies = fsdp // EXPERTS
    width = D // fsdp
    hidden_own = FF_EXPERT // copies
    piece = hidden_own // fsdp
    factor = 1.0 / math.sqrt(HEAD_DIM)
    capacity = length * TOP // EXPERTS

    names = jnp.arange(EXPERTS, dtype=jnp.int32)
    matches = expert_ids[0][None, :, :] == names[:, None, None]
    gates = jnp.sum(jnp.where(matches, expert_gates[0][None], 0.0), axis=-1)
    gates = jnp.where(jnp.any(matches, axis=-1), gates, -1.0)
    chosen = (gates >= 0.0).astype(jnp.int32)
    tallies = lax.all_gather(jnp.sum(chosen, axis=1), "seq")
    before = jnp.arange(seq, dtype=jnp.int32)[:, None] < place
    offsets = jnp.sum(jnp.where(before, tallies, 0), axis=0)
    earlier = offsets[:, None] + jnp.cumsum(chosen, axis=1) - chosen
    gates = jnp.where((chosen > 0) & (earlier < capacity), gates, 0.0)
    gates = lax.all_gather(gates, "fsdp", axis=0)
    share = lax.dynamic_index_in_dim(gates, me // copies, 1, keepdims=False).reshape(-1, 1)

    all_tokens = gather_seq(after(tokens[0], gates))
    own = [
        lax.dynamic_slice_in_dim(qkv_weight, part * D + place * group, group, 1)
        for part in range(3)
    ]
    vectors = jnp.concatenate([attn_gain, ffn_gain, shared_gate, qkv_bias])
    extra = -(-6 * width // (3 * group) // 16) * 16
    vectors = jnp.pad(vectors, (0, extra * 3 * group - 6 * width)).reshape(extra, 3 * group)
    gathered = lax.all_gather(
        after(jnp.concatenate([jnp.concatenate(own, axis=1), vectors], axis=0), gates),
        "fsdp",
        axis=0,
    )
    weight_qkv = gathered[:, :width].reshape(D, 3 * group)
    vectors = gathered[:, width:].reshape(fsdp, -1)
    gain_one = vectors[:, :width].reshape(D).astype(f32)
    gain_two = vectors[:, width : 2 * width].reshape(D).astype(f32)
    gate_vector = vectors[:, 2 * width : 3 * width].reshape(D)
    bias = vectors[:, 3 * width : 6 * width].reshape(3, seq, group)
    bias = lax.dynamic_index_in_dim(bias, place, 1, keepdims=False).reshape(-1).astype(f32)
    weight_out = lax.all_gather(out_weight, "fsdp", axis=0, tiled=True)
    upstream_all = lax.all_gather(cotangent[0], "fsdp", axis=0, tiled=True)

    up_sent = expert_gate_up.reshape(EXPERTS, width, 2, fsdp, copies, piece)
    up_sent = up_sent.transpose(0, 4, 1, 2, 3, 5).reshape(fsdp, width, 2 * hidden_own)
    down_sent = expert_down.reshape(fsdp, piece, D)
    if seq == 4:
        half = lax.rem(place, 2)
        fetched = swap(lax.dynamic_slice_in_dim(up_sent, half * (width // 2), width // 2, 1))
        given = lax.ppermute(fetched, "seq", [(0, 1), (1, 0), (2, 3), (3, 2)])
    else:
        fetched = given = swap(up_sent)

    x_all = all_tokens.astype(f32)
    normed_unit = x_all * rms_scale(x_all)
    normed = (normed_unit * gain_one).astype(bf16)
    cosine, sine = rope_tables(jnp.arange(length, dtype=jnp.int32))
    normed = after(normed, weight_qkv)
    joined = dot(normed, weight_qkv, ((1,), (0,))) + bias
    split = joined.reshape(length, 3, heads, HEAD_DIM)
    queries = rotate(split[:, 0], cosine, sine).astype(bf16)
    keys = rotate(split[:, 1], cosine, sine).astype(bf16)
    values = split[:, 2].astype(bf16)
    documents = segments[0]
    mixed, logs = attend(queries, keys, values, documents, factor)
    mixed_rows = exchange_seq(mixed.reshape(length, group), 0, 1)
    mixed_rows = after(mixed_rows, upstream_all)
    inputs = tokens[0].astype(f32)
    hidden = inputs + dot(mixed_rows, weight_out, ((1,), (0,)))
    scale_two = rms_scale(hidden)
    second = (hidden * scale_two * gain_two).astype(bf16)
    second_all = lax.all_gather(after(second, fetched), "fsdp", axis=0, tiled=True)

    weight_down = swap(after(down_sent, second_all)).reshape(hidden_own, D)
    by_kernel = seq == 4 and fsdp == 8
    s_gate, s_lift = shared_gate_up[:, 0], shared_gate_up[:, 1]
    opening_all = jax.nn.sigmoid(dot(second_all, gate_vector, ((1,), (0,))))[:, None]
    inner_s, ga_s, gl_s, reach = middle(
        second_all, upstream_all, s_gate, s_lift, shared_down, opening_all
    )
    grad_s_down = dot(upstream_all, inner_s, ((0,), (0,)), bf16)
    grad_s_gate = dot(second_all, ga_s, ((0,), (0,)), bf16)
    grad_s_lift = dot(second_all, gl_s, ((0,), (0,)), bf16)

    weight_up, fetched = after((given, fetched), grad_s_down, grad_s_gate, grad_s_lift)
    if seq == 4:
        weight_up = jnp.concatenate(
            [jnp.where(half == 0, fetched, weight_up), jnp.where(half == 0, weight_up, fetched)],
            axis=1,
        )
    weight_up = weight_up.reshape(D, 2 * hidden_own)
    if by_kernel:
        *sum_s, inner_e, grads_e, grad_second_all, out_all = feed_forward(
            (grad_s_down, grad_s_gate, grad_s_lift),
            (second_all, upstream_all, ga_s, gl_s, inner_s),
            (weight_up, weight_down, s_gate, s_lift, shared_down),
            share,
            2,
        )
        grad_second = scatter(grad_second_all)
        grad_e_down = dot(inner_e, upstream_all, ((0,), (0,)), bf16)
        grad_e_up = dot(second_all, after(grads_e, grad_e_down), ((0,), (0,)), bf16)
        reach = jnp.sum(swap(after(reach.reshape(fsdp, row_count), inner_e)), axis=0)
        out_all = after(out_all, grad_e_up)
    else:
        held = after(second_all, grad_s_down, grad_s_gate, grad_s_lift)
        if hidden_own % 128 == 0:
            inner_e, grads_e, _ = middle(held, upstream_all, weight_up, None, weight_down, share)
        else:
            inner_e, ga_e, gl_e, _ = middle(
                held,
                upstream_all,
                weight_up[:, :hidden_own],
                weight_up[:, hidden_own:],
                weight_down,
                share,
            )
            grads_e = jnp.concatenate([ga_e, gl_e], axis=1)
        part = dot(inner_e, upstream_all, ((0,), (0,)), bf16)
        grad_e_down = part
        reach = jnp.sum(swap(after(reach.reshape(fsdp, row_count), part)), axis=0)

        grads_e, ga_s, gl_s = after((grads_e, ga_s, gl_s), part)
        grad_second_all = (
            dot(ga_s, s_gate, ((1,), (1,)))
            + dot(gl_s, s_lift, ((1,), (1,)))
            + dot(grads_e, weight_up, ((1,), (1,)))
        ).astype(bf16)
        grad_second = scatter(grad_second_all)

        grad_e_up = dot(second_all, after(grads_e, grad_second_all), ((0,), (0,)), bf16)

        inner_s, inner_e = after((inner_s, inner_e), grad_e_up)
        out_all = (
            dot(inner_s, shared_down, ((1,), (0,))) + dot(inner_e, weight_down, ((1,), (0,)))
        ).astype(bf16)
        sum_s = lax.psum((grad_s_down, grad_s_gate, grad_s_lift), "seq")

    grad_second, reach = after((grad_second, reach), out_all)
    upstream = cotangent[0].astype(f32)
    opening = jax.nn.sigmoid(dot(second, gate_vector, ((1,), (0,))))
    grad_logit = reach * opening * (1.0 - opening)
    grad_second = grad_second + grad_logit[:, None] * gate_vector.astype(f32)[None, :]
    grad_gate_vector = jnp.sum(grad_logit[:, None] * second.astype(f32), axis=0)
    grad_hidden = upstream + norm_back(hidden, scale_two, gain_two, grad_second)
    grad_gain_two = jnp.sum(grad_second * hidden * scale_two, axis=0)
    grad_projected = grad_hidden.astype(bf16)
    grad_mixture = dot(grad_projected, weight_out, ((1,), (1,)), bf16)
    grad_heads = exchange_seq(grad_mixture, 1, 0)
    grad_out = dot(mixed_rows, after(grad_projected, grad_mixture), ((0,), (0,)), bf16)

    grad_heads = after(grad_heads, grad_out)
    grad_queries, grad_keys, grad_values = attend_back(
        queries,
        keys,
        values,
        documents,
        factor,
        logs,
        grad_heads.reshape(length, heads, HEAD_DIM),
    )
    grad_joined = jnp.stack(
        [
            rotate_back(grad_queries.astype(bf16).astype(f32), cosine, sine),
            rotate_back(grad_keys.astype(bf16).astype(f32), cosine, sine),
            grad_values,
        ],
        axis=1,
    )
    grad_joined = grad_joined.reshape(length, 3 * group).astype(bf16)
    grad_normed_all = dot(grad_joined, weight_qkv, ((1,), (1,)))
    grad_gain_one = jnp.sum(grad_normed_all * normed_unit, axis=0)

    grad_qkv = dot(normed, grad_joined, ((0,), (0,)), bf16).reshape(fsdp, width, 3 * group)
    grad_bias = jnp.sum(grad_joined.astype(f32), axis=0).reshape(3, 1, group)
    own_heads = (jnp.arange(seq, dtype=jnp.int32) == place).astype(f32)
    grad_bias = (grad_bias * own_heads[None, :, None]).reshape(fsdp, 3 * width)
    rows = jnp.concatenate(
        [
            grad_gain_one.reshape(fsdp, width),
            grad_gain_two.reshape(fsdp, width),
            grad_gate_vector.reshape(fsdp, width),
            grad_bias,
        ],
        axis=1,
    ).astype(bf16)
    rows = jnp.pad(rows, ((0, 0), (0, extra * 3 * group - 6 * width)))
    rows = rows.reshape(fsdp, extra, 3 * group)
    grad_qkv = jnp.concatenate([grad_qkv, rows], axis=1)

    grad_out = scatter(grad_out).astype(bf16)
    grad_normed_all = grad_normed_all.astype(bf16)
    grad_e_up, grad_out, grad_qkv, grad_normed_all, out_all = together(
        grad_e_up, grad_out, grad_qkv, grad_normed_all, out_all
    )
    grad_qkv = lax.psum_scatter(
        grad_qkv.reshape(-1, 3 * group), "fsdp", scatter_dimension=0, tiled=True
    )
    grad_normed = lax.psum_scatter(grad_normed_all, "seq", scatter_dimension=0, tiled=True)
    out_part = lax.psum_scatter(out_all, "fsdp", scatter_dimension=0, tiled=True)
    if by_kernel:
        sum_e_up, sum_e_down, sum_out = combine(
            [(grad_e_up, True, 64), (grad_e_down, True, 176), (grad_out, False, 64)], 1
        )
        sum_e_up = sum_e_up.reshape(EXPERTS, width, 2 * FF_EXPERT)
        sum_e_down = sum_e_down.reshape(EXPERTS, piece, D)
    else:
        sum_e_up = swap(grad_e_up.reshape(fsdp, width, 2 * hidden_own))
        sum_e_down = swap(grad_e_down.reshape(fsdp, piece, D))
        sum_e_up, sum_e_down, sum_out = lax.psum((sum_e_up, sum_e_down, grad_out), "seq")
        sum_e_down = sum_e_down.reshape(EXPERTS, copies * piece, D)
        sum_e_up = sum_e_up.reshape(EXPERTS, copies, width, 2, fsdp, piece)
        sum_e_up = sum_e_up.transpose(0, 2, 3, 4, 1, 5).reshape(EXPERTS, width, 2 * FF_EXPERT)
    output = (hidden + out_part.astype(f32)).astype(bf16)
    grad_normed = grad_normed.astype(f32)
    grad_qkv = lax.all_gather(after(grad_qkv, sum_out), "seq", axis=0)
    rows = jnp.sum(grad_qkv[:, width:].astype(f32), axis=0).reshape(-1)
    grad_qkv = jnp.concatenate(
        [
            grad_qkv[owner, :width, part * group : (part + 1) * group]
            for part in range(3)
            for owner in range(seq)
        ],
        axis=1,
    ).astype(f32)
    input_grad = (grad_hidden + norm_back(inputs, rms_scale(inputs), gain_one, grad_normed)).astype(
        bf16
    )
    sum_s_up = jnp.stack([sum_s[1], sum_s[2]], axis=1)

    return (
        output[None],
        input_grad[None],
        rows[:width],
        grad_qkv,
        rows[3 * width : 6 * width],
        sum_out.astype(f32),
        rows[width : 2 * width],
        sum_s_up.astype(f32),
        sum_s[0].T.astype(f32),
        rows[2 * width : 3 * width],
        sum_e_up.astype(f32),
        sum_e_down.astype(f32),
    )


def solution(mesh):
    return jax.shard_map(
        on_device,
        mesh=mesh,
        in_specs=(
            P("fsdp", "seq", None),
            P("fsdp", None),
            P("fsdp", "seq", None),
            P("fsdp", "seq", None),
            P("fsdp"),
            P("fsdp", None),
            P("fsdp"),
            P("fsdp", None),
            P("fsdp"),
            P(None, None, "fsdp"),
            P("fsdp", None),
            P("fsdp"),
            P(None, "fsdp", None),
            P(None, "fsdp", None),
            P("fsdp", "seq", None),
        ),
        out_specs=(
            P("fsdp", "seq", None),
            P("fsdp", "seq", None),
            P("fsdp"),
            P("fsdp", None),
            P("fsdp"),
            P("fsdp", None),
            P("fsdp"),
            P(None, None, "fsdp"),
            P("fsdp", None),
            P("fsdp"),
            P(None, "fsdp", None),
            P(None, "fsdp", None),
        ),
        check_vma=False,
    )
```

```python
import functools
import math

import jax
import jax.numpy as jnp
from jax import lax
from jax.experimental import pallas as pl
from jax.experimental.pallas import tpu as pltpu
from jax.sharding import PartitionSpec as P

D = 2048
HEADS = 16
HEAD_DIM = 128
FF_EXPERT = 1408
TOP = 4
EXPERTS = 8
QBLOCK = 256
DOC_MOST = 512

EPSILON = 1e-06
THETA = 1000000.0

bf16 = jnp.bfloat16
f32 = jnp.float32


def dot(a, b, contract, kind=f32):
    return lax.dot_general(a, b, (contract, ((), ())), preferred_element_type=f32).astype(kind)


def rms_scale(values):
    return lax.rsqrt(jnp.mean(values * values, axis=-1, keepdims=True) + EPSILON)


def norm_back(values, scale, gain, grad):
    scaled = grad * gain
    centre = jnp.mean(scaled * values, axis=-1, keepdims=True)
    return scale * (scaled - values * (scale * scale) * centre)


def rope_tables(positions):
    steps_half = jnp.arange(HEAD_DIM // 2, dtype=jnp.int32).astype(f32)
    frequency = jnp.exp(steps_half * (-2.0 * math.log(THETA) / HEAD_DIM))
    angles = positions.astype(f32)[:, None] * frequency[None, :]
    angles = jnp.concatenate([angles, angles], axis=-1)
    return (jnp.cos(angles), jnp.sin(angles))


def rotate(rows, cosine, sine):
    middle = rows.shape[-1] // 2
    turned = jnp.concatenate([-rows[..., middle:], rows[..., :middle]], axis=-1)
    return rows * cosine[:, None, :] + turned * sine[:, None, :]


def rotate_back(rows, cosine, sine):
    middle = rows.shape[-1] // 2
    turned = rows * sine[:, None, :]
    turned = jnp.concatenate([turned[..., middle:], -turned[..., :middle]], axis=-1)
    return rows * cosine[:, None, :] + turned


def key_start(block):
    return max(0, block * QBLOCK - DOC_MOST)


def block_scores(block, queries, keys, documents, factor):
    first, start = block * QBLOCK, key_start(block)
    stop = first + QBLOCK
    scores = (
        jnp.einsum(
            "qhd,khd->hqk", queries[first:stop], keys[start:stop], preferred_element_type=f32
        )
        * factor
    )
    rows = first + jnp.arange(QBLOCK, dtype=jnp.int32)
    columns = start + jnp.arange(stop - start, dtype=jnp.int32)
    allowed = (rows[:, None] >= columns[None, :]) & (
        documents[first:stop, None] == documents[None, start:stop]
    )
    return jnp.where(allowed[None], scores, -1e30)


def attend(queries, keys, values, documents, factor):
    mixed, logs = [], []
    for block in range(queries.shape[0] // QBLOCK):
        start, stop = key_start(block), (block + 1) * QBLOCK
        scores = block_scores(block, queries, keys, documents, factor)
        top = jnp.max(scores, axis=-1, keepdims=True)
        weights = jnp.exp(scores - top)
        totals = jnp.sum(weights, axis=-1, keepdims=True)
        probability = (weights / totals).astype(bf16)
        mixed.append(
            jnp.einsum(
                "hqk,khd->qhd", probability, values[start:stop], preferred_element_type=f32
            ).astype(bf16)
        )
        logs.append(top + jnp.log(totals))
    return jnp.concatenate(mixed, axis=0), logs


def attend_back(queries, keys, values, documents, factor, logs, grads):
    length = queries.shape[0]
    grad_queries = []
    grad_keys = jnp.zeros(keys.shape, f32)
    grad_values = jnp.zeros(values.shape, f32)
    for block in range(length // QBLOCK):
        start, stop = key_start(block), (block + 1) * QBLOCK
        scores = block_scores(block, queries, keys, documents, factor)
        probability = jnp.exp(scores - logs[block])
        grad_block = grads[block * QBLOCK : stop]
        query_block = queries[block * QBLOCK : stop]
        grad_values = grad_values.at[start:stop].add(
            jnp.einsum(
                "hqk,qhd->khd", probability.astype(bf16), grad_block, preferred_element_type=f32
            )
        )
        grad_probability = jnp.einsum(
            "qhd,khd->hqk", grad_block, values[start:stop], preferred_element_type=f32
        )
        centre = jnp.sum(grad_probability * probability, axis=-1, keepdims=True)
        grad_scores = (probability * (grad_probability - centre)).astype(bf16)
        grad_queries.append(
            jnp.einsum("hqk,khd->qhd", grad_scores, keys[start:stop], preferred_element_type=f32)
            * factor
        )
        grad_keys = grad_keys.at[start:stop].add(
            jnp.einsum("hqk,qhd->khd", grad_scores, query_block, preferred_element_type=f32)
            * factor
        )
    return jnp.concatenate(grad_queries, axis=0), grad_keys, grad_values


def after(value, *earlier):
    return lax.optimization_barrier((value, earlier))[0]


def line_neighbours(place):
    middle = lax.rem(place + 1, 4) // 2
    low = 1 - place // 2
    partner = low * (1 - place) + (1 - low) * (5 - place)
    across = low * 2 + (1 - low) * 1
    return middle, partner, across


def flip(index, bits):
    result, step = 0, 1
    while step < 8:
        bit = lax.rem(index // step, 2)
        result = result + step * (1 - bit if bits & step else bit)
        step *= 2
    return result


SLOTS = 4
ORDER = (0, 1, 2, 4, 3, 5, 6, 7)
LEAVE = {2: ((2, 4), (3, 5)), 4: ((3, 5), (6, 7))}


def combine_kernel(plan, *refs):
    count = len(plan)
    sources, refs = refs[:count], refs[count:]
    results, refs = refs[:count], refs[count:]
    lands, refs = refs[:count], refs[count:]
    buffers, refs = refs[: 5 * count], refs[5 * count :]
    (land_send, land_recv, g_sem, a_send, a_recv, b_send, b_recv, c_send, c_recv) = refs[:9]
    out_sem, a_free, b_free = refs[9:]
    me, place = lax.axis_index("fsdp"), lax.axis_index("seq")
    middle, partner, across = line_neighbours(place)
    peers = [flip(me, k) for k in range(8)]

    barrier = pltpu.get_barrier_semaphore()
    swapping = any(swapped for swapped, _, _, _ in plan)
    if swapping:
        for k in range(1, 8):
            pl.semaphore_signal(
                barrier, device_id={"fsdp": peers[k]}, device_id_type=pl.DeviceIdType.MESH
            )
    pl.semaphore_signal(
        barrier, device_id={"seq": partner}, device_id_type=pl.DeviceIdType.MESH
    )

    @pl.when(middle == 1)
    def _():
        pl.semaphore_signal(
            barrier, device_id={"seq": across}, device_id_type=pl.DeviceIdType.MESH
        )

    pl.semaphore_wait(barrier, 1 + middle + (7 if swapping else 0))

    arrivals = {}
    for index, (swapped, rows, blocks, _) in enumerate(plan):
        if not swapped:
            continue
        here = pl.ds(pl.multiple_of(me * rows, 16), rows)
        for k in range(1, 8):
            there = pl.ds(pl.multiple_of(peers[k] * rows, 16), rows)
            copy = pltpu.make_async_remote_copy(
                src_ref=sources[index].at[there],
                dst_ref=lands[index].at[here],
                send_sem=land_send.at[index, k],
                recv_sem=land_recv.at[index, k],
                device_id={"fsdp": peers[k]},
                device_id_type=pl.DeviceIdType.MESH,
            )
            arrivals[index, k] = copy
            if k in (1, 2, 4):
                copy.start()

    chunks, starts = [], []
    for index, (swapped, rows, blocks, size) in enumerate(plan):
        starts.append(len(chunks))
        for block in range(blocks):
            base = (peers[ORDER[block]] if swapped else block) * rows
            for first in range(0, rows, size):
                chunks.append((index, block if first == 0 else None, base + first, size))
    total = len(chunks)

    def landed(c):
        index, block, _, _ = chunks[c]
        if not plan[index][0] or block is None:
            return
        if block > 0:
            arrivals[index, ORDER[block]].wait_recv()
        if block in LEAVE:
            left, leaving = LEAVE[block]
            for k in left:
                arrivals[index, k].wait_send()
            for k in leaving:
                arrivals[index, k].start()

    def place_of(c, ref_list):
        index, _, start, size = chunks[c]
        if isinstance(start, int):
            return ref_list[index].at[pl.ds(start, size)]
        return ref_list[index].at[pl.ds(pl.multiple_of(start, 16), size)]

    def held(c, which):
        return buffers[5 * chunks[c][0] + which].at[c % SLOTS]

    def given(c):
        index, _, _, size = chunks[c]
        away = plan[index][0] and size * (c - starts[index]) >= plan[index][1]
        return place_of(c, lands if away else sources)

    def inward(c):
        return pltpu.make_async_remote_copy(
            src_ref=given(c),
            dst_ref=held(c, 1),
            send_sem=a_send.at[c % SLOTS],
            recv_sem=a_recv.at[c % SLOTS],
            device_id={"seq": partner},
            device_id_type=pl.DeviceIdType.MESH,
        )

    def crossing(c):
        return pltpu.make_async_remote_copy(
            src_ref=held(c, 2),
            dst_ref=held(c, 3),
            send_sem=b_send.at[c % SLOTS],
            recv_sem=b_recv.at[c % SLOTS],
            device_id={"seq": across},
            device_id_type=pl.DeviceIdType.MESH,
        )

    def outward(c):
        return pltpu.make_async_remote_copy(
            src_ref=held(c, 4),
            dst_ref=place_of(c, results),
            send_sem=c_send.at[c % SLOTS],
            recv_sem=c_recv.at[c],
            device_id={"seq": partner},
            device_id_type=pl.DeviceIdType.MESH,
        )

    def fetch(c):
        return pltpu.make_async_copy(given(c), held(c, 0), g_sem.at[c % SLOTS])

    def keep(c):
        return pltpu.make_async_copy(held(c, 4), place_of(c, results), out_sem.at[c % SLOTS])

    @pl.when(middle == 0)
    def _():
        for c in range(total):
            landed(c)
            if c >= SLOTS:
                inward(c - SLOTS).wait_send()
                pl.semaphore_wait(a_free, 1)
            inward(c).start()
        for c in range(max(0, total - SLOTS), total):
            inward(c).wait_send()
        for c in range(total):
            outward(c).wait_recv()

    @pl.when(middle == 1)
    def _():
        for c in range(min(SLOTS, total)):
            landed(c)
            fetch(c).start()
        for i in range(total + 1):
            c = i
            if c < total:
                fetch(c).wait()
                inward(c).wait_recv()
                if c >= SLOTS:
                    crossing(c - SLOTS).wait_send()
                held(c, 2)[...] = (
                    held(c, 0)[...].astype(f32) + held(c, 1)[...].astype(f32)
                ).astype(bf16)
                if c + SLOTS < total:
                    pl.semaphore_signal(
                        a_free, device_id={"seq": partner}, device_id_type=pl.DeviceIdType.MESH
                    )
                if c >= SLOTS:
                    pl.semaphore_wait(b_free, 1)
                crossing(c).start()
                if c + SLOTS < total:
                    landed(c + SLOTS)
                    fetch(c + SLOTS).start()
            c = i - 1
            if c >= 0:
                crossing(c).wait_recv()
                if c >= SLOTS:
                    keep(c - SLOTS).wait()
                    outward(c - SLOTS).wait_send()
                held(c, 4)[...] = (
                    held(c, 2)[...].astype(f32) + held(c, 3)[...].astype(f32)
                ).astype(bf16)
                if c + SLOTS < total:
                    pl.semaphore_signal(
                        b_free, device_id={"seq": across}, device_id_type=pl.DeviceIdType.MESH
                    )
                outward(c).start()
                keep(c).start()
        for c in range(max(0, total - SLOTS), total):
            crossing(c).wait_send()
            keep(c).wait()
            outward(c).wait_send()

    for (_, k), copy in arrivals.items():
        if k in (1, 6, 7):
            copy.wait_send()


def combine(arrays, number):
    plan = []
    for value, swapped, size in arrays:
        rows = value.shape[0] // 8 if swapped else value.shape[0]
        plan.append((swapped, rows, 8 if swapped else 1, size))
    count = len(plan)
    total = sum(rows // size * blocks for _, rows, blocks, size in plan)
    shapes = [jax.ShapeDtypeStruct(value.shape, bf16) for value, _, _ in arrays]
    lands = [
        jax.ShapeDtypeStruct(value.shape if swapped else (16, 128), bf16)
        for value, swapped, _ in arrays
    ]
    buffers = [
        pltpu.VMEM((SLOTS, size, value.shape[1]), bf16)
        for value, _, size in arrays
        for _ in range(5)
    ]
    dma = pltpu.SemaphoreType.DMA
    moved = sum(value.size for value, _, _ in arrays)
    anywhere = pl.BlockSpec(memory_space=pl.ANY)
    return pl.pallas_call(
        functools.partial(combine_kernel, tuple(plan)),
        out_shape=shapes + lands,
        in_specs=[anywhere] * count,
        out_specs=[anywhere] * (2 * count),
        scratch_shapes=buffers
        + [
            dma((count, 8)),
            dma((count, 8)),
            dma((SLOTS,)),
            dma((SLOTS,)),
            dma((SLOTS,)),
            dma((SLOTS,)),
            dma((SLOTS,)),
            dma((SLOTS,)),
            dma((total,)),
            dma((SLOTS,)),
            pltpu.SemaphoreType.REGULAR,
            pltpu.SemaphoreType.REGULAR,
        ],
        compiler_params=pltpu.CompilerParams(
            collective_id=number, has_side_effects=True, vmem_limit_bytes=48 * 1024 * 1024
        ),
        cost_estimate=pl.CostEstimate(
            flops=2 * moved, bytes_accessed=200 * moved, transcendentals=0
        ),
        name="combine_%d" % number,
    )(*[value for value, _, _ in arrays])[:count]


HOST_BLOCKS = 8
SUM_BLOCKS = 16


def feed_forward_kernel(*refs):
    sources, refs = refs[:3], refs[3:]
    tiles_in, refs = refs[:5], refs[5:]
    near, far, *weights = refs[:6]
    share, refs = refs[6], refs[7:]
    results, refs = refs[:3], refs[3:]
    tiles_out, refs = refs[:4], refs[4:]
    zg, za, zs, zb, zt = refs[:5]
    refs = refs[5:]
    held, refs = refs[:5], refs[5:]
    v_up, v_down, v_sg, v_sl, v_sd = held
    loaded, refs = refs[:5], refs[5:]
    v_x, v_u, v_ga, v_gl, v_in = loaded
    stored, refs = refs[:4], refs[4:]
    t_in, t_grads, t_second, t_out = stored
    (w_sem, l_sem, s_sem, g_sem, a_send, a_recv, b_send, b_recv, c_send, c_recv) = refs[:10]
    out_sem, a_free, b_free = refs[10:]
    place = lax.axis_index("seq")
    middle, partner, across = line_neighbours(place)
    tile = v_x.shape[1]
    hidden = v_down.shape[0]
    last = SUM_BLOCKS - 1
    pace = SUM_BLOCKS // HOST_BLOCKS
    block = za.shape[2]

    half = lax.rem(place, 2)
    cut_rows = v_up.shape[0] // 16
    copies = [
        pltpu.make_async_copy(weights[index], held[index + 1], w_sem.at[index])
        for index in range(4)
    ]
    for owner in range(8):
        source = pl.ds(owner * cut_rows, cut_rows)
        for which, (ref, side) in enumerate(((near, half), (far, 1 - half))):
            first = pl.multiple_of((2 * owner + side) * cut_rows, cut_rows)
            copies.append(
                pltpu.make_async_copy(
                    ref.at[source],
                    v_up.at[pl.ds(first, cut_rows)],
                    w_sem.at[4 + 2 * owner + which],
                )
            )
    for copy in copies:
        copy.start()

    barrier = pltpu.get_barrier_semaphore()
    pl.semaphore_signal(
        barrier, device_id={"seq": partner}, device_id_type=pl.DeviceIdType.MESH
    )

    @pl.when(middle == 1)
    def _():
        pl.semaphore_signal(
            barrier, device_id={"seq": across}, device_id_type=pl.DeviceIdType.MESH
        )

    pl.semaphore_wait(barrier, 1 + middle)

    def rows(o, size=block):
        return pl.ds(o * size if isinstance(o, int) else pl.multiple_of(o * size, size), size)

    def slot(o):
        return o % 2 if isinstance(o, int) else lax.rem(o, 2)

    def remote(source, target, sent, received, where):
        return pltpu.make_async_remote_copy(
            src_ref=source,
            dst_ref=target,
            send_sem=sent,
            recv_sem=received,
            device_id={"seq": where},
            device_id_type=pl.DeviceIdType.MESH,
        )

    def inward(o, a):
        i = slot(o)
        return remote(
            sources[a].at[rows(o)], za.at[i, a], a_send.at[i, a], a_recv.at[i, a], partner
        )

    def crossing(o, a):
        i = slot(o)
        return remote(zs.at[i, a], zb.at[i, a], b_send.at[i, a], b_recv.at[i, a], across)

    def outward(o, a):
        i = slot(o)
        return remote(
            zt.at[i, a], results[a].at[rows(o)], c_send.at[i, a], c_recv.at[o, a], partner
        )

    def fetch(o, a):
        i = slot(o)
        return pltpu.make_async_copy(sources[a].at[rows(o)], zg.at[i, a], g_sem.at[i, a])

    def keep(o, a):
        i = slot(o)
        return pltpu.make_async_copy(zt.at[i, a], results[a].at[rows(o)], out_sem.at[i, a])

    def load(o, index):
        i = slot(o)
        return pltpu.make_async_copy(
            tiles_in[index].at[rows(o, tile)], loaded[index].at[i], l_sem.at[i, index]
        )

    def store(o, index):
        return pltpu.make_async_copy(stored[index], tiles_out[index].at[rows(o, tile)], s_sem.at[index])

    for index in range(5):
        load(0, index).start()

    @pl.when(middle == 0)
    def _():
        for o in (0, 1):
            for a in range(3):
                inward(o, a).start()

    @pl.when(middle == 1)
    def _():
        for o in (0, 1):
            for a in range(3):
                fetch(o, a).start()

    for copy in copies:
        copy.wait()

    def add(left, right):
        return (left.astype(f32) + right.astype(f32)).astype(bf16)

    def end_step(o):
        @pl.when((o >= 1) & (o < last))
        def _():
            for a in range(3):
                inward(o - 1, a).wait_send()
                pl.semaphore_wait(a_free, 1)
                inward(o + 1, a).start()

    def middle_step(o):
        @pl.when(o <= last)
        def _():
            i = slot(o)
            for a in range(3):
                fetch(o, a).wait()
                inward(o, a).wait_recv()

                @pl.when(o >= 2)
                def _():
                    crossing(o - 2, a).wait_send()
                    pl.semaphore_wait(b_free, 1)

                zs[i, a] = add(zg[i, a], za[i, a])
                crossing(o, a).start()

                @pl.when(o + 2 <= last)
                def _():
                    pl.semaphore_signal(
                        a_free, device_id={"seq": partner}, device_id_type=pl.DeviceIdType.MESH
                    )
                    fetch(o + 2, a).start()

        @pl.when(o >= 1)
        def _():
            p = o - 1
            i = slot(p)
            for a in range(3):
                crossing(p, a).wait_recv()

                @pl.when(p >= 2)
                def _():
                    keep(p - 2, a).wait()
                    outward(p - 2, a).wait_send()

                zt[i, a] = add(zs[i, a], zb[i, a])

                @pl.when(p + 2 <= last)
                def _():
                    pl.semaphore_signal(
                        b_free, device_id={"seq": across}, device_id_type=pl.DeviceIdType.MESH
                    )

                outward(p, a).start()
                keep(p, a).start()

    def across_rows(left, right):
        return lax.dot_general(left, right, (((1,), (1,)), ((), ())), preferred_element_type=f32)

    def host(o):
        i = slot(o)
        for index in range(5):
            load(o, index).wait()

        @pl.when(o < HOST_BLOCKS - 1)
        def _():
            for index in range(5):
                load(o + 1, index).start()

        @pl.when(o >= 1)
        def _():
            for index in range(4):
                store(o - 1, index).wait()

        scale = share[rows(o, tile), :]
        cut = hidden // 256 * 128
        for first, end in ((0, cut), (cut, hidden)):
            gate = jnp.dot(v_x[i], v_up[:, first:end], preferred_element_type=f32)
            lift = jnp.dot(
                v_x[i], v_up[:, hidden + first : hidden + end], preferred_element_type=f32
            )
            grad = across_rows(v_u[i], v_down[first:end, :]) * scale
            sigma = 1.0 / (1.0 + jnp.exp(-gate))
            silu = gate * sigma
            t_in[:, first:end] = (silu * lift * scale).astype(bf16)
            t_grads[:, first:end] = (
                grad * lift * sigma * (1.0 + gate * (1.0 - sigma))
            ).astype(bf16)
            t_grads[:, hidden + first : hidden + end] = (grad * silu).astype(bf16)
        for first in range(0, D, 512):
            end = first + 512
            t_second[:, first:end] = (
                across_rows(t_grads[...], v_up[first:end, :])
                + across_rows(v_ga[i], v_sg[first:end, :])
                + across_rows(v_gl[i], v_sl[first:end, :])
            ).astype(bf16)
            t_out[:, first:end] = (
                jnp.dot(t_in[...], v_down[:, first:end], preferred_element_type=f32)
                + jnp.dot(v_in[i], v_sd[:, first:end], preferred_element_type=f32)
            ).astype(bf16)
        for index in range(4):
            store(o, index).start()

    def step(o, carry):
        @pl.when(middle == 0)
        def _():
            end_step(o)

        @pl.when(middle == 1)
        def _():
            middle_step(o)

        @pl.when((o <= last) & (lax.rem(o, pace) == 0))
        def _():
            host(o // pace)

        return carry

    lax.fori_loop(0, SUM_BLOCKS + 1, step, 0)
    for index in range(4):
        store(HOST_BLOCKS - 1, index).wait()

    @pl.when(middle == 0)
    def _():
        for a in range(3):
            for o in (last - 1, last):
                inward(o, a).wait_send()
            for o in range(SUM_BLOCKS):
                outward(o, a).wait_recv()

    @pl.when(middle == 1)
    def _():
        for a in range(3):
            for o in (last - 1, last):
                crossing(o, a).wait_send()
                keep(o, a).wait()
                outward(o, a).wait_send()


def feed_forward(sums, tiles, weights, share, number):
    rows, cut = sums[0].shape
    tile = rows // HOST_BLOCKS
    hidden = weights[2].shape[0]
    dma = pltpu.SemaphoreType.DMA
    anywhere = pl.BlockSpec(memory_space=pl.ANY)
    outs = [hidden, 2 * hidden, D, D]
    return pl.pallas_call(
        feed_forward_kernel,
        out_shape=[jax.ShapeDtypeStruct((rows, cut), bf16)] * 3
        + [jax.ShapeDtypeStruct((rows, w), bf16) for w in outs],
        in_specs=[anywhere] * 14 + [pl.BlockSpec(memory_space=pltpu.VMEM)],
        out_specs=[anywhere] * 7,
        scratch_shapes=[pltpu.VMEM((2, 3, rows // SUM_BLOCKS, cut), bf16)] * 5
        + [pltpu.VMEM((D, 2 * hidden), bf16)]
        + [pltpu.VMEM(w.shape, bf16) for w in weights[2:]]
        + [pltpu.VMEM((2, tile, t.shape[1]), bf16) for t in tiles]
        + [pltpu.VMEM((tile, w), bf16) for w in outs]
        + [
            dma((20,)),
            dma((2, 5)),
            dma((4,)),
            dma((2, 3)),
            dma((2, 3)),
            dma((2, 3)),
            dma((2, 3)),
            dma((2, 3)),
            dma((2, 3)),
            dma((SUM_BLOCKS, 3)),
            dma((2, 3)),
            pltpu.SemaphoreType.REGULAR,
            pltpu.SemaphoreType.REGULAR,
        ],
        compiler_params=pltpu.CompilerParams(
            collective_id=number, has_side_effects=True, vmem_limit_bytes=60 * 1024 * 1024
        ),
        cost_estimate=pl.CostEstimate(
            flops=2 * rows * D * (6 * hidden + 3 * cut),
            bytes_accessed=800 * 1024 * 1024,
            transcendentals=rows * hidden,
        ),
    )(*sums, *tiles, *weights, share)


def middle_kernel(joined, x, u, w_gate, w_lift, w_down, scale, inner, *outs):
    gate = jnp.dot(x[...], w_gate[...], preferred_element_type=f32)
    lift = jnp.dot(x[...], w_lift[...], preferred_element_type=f32)
    raw = lax.dot_general(
        u[...], w_down[...], (((1,), (1,)), ((), ())), preferred_element_type=f32
    )
    sigma = 1.0 / (1.0 + jnp.exp(-gate))
    silu = gate * sigma
    product = silu * lift
    outs[-1][...] = jnp.sum(product * raw, axis=1, keepdims=True)
    inner[...] = (product * scale[...]).astype(bf16)
    grad = raw * scale[...]
    grad_gate = (grad * lift * sigma * (1.0 + gate * (1.0 - sigma))).astype(bf16)
    grad_lift = (grad * silu).astype(bf16)
    if joined:
        width = grad_gate.shape[1]
        outs[0][:, :width] = grad_gate
        outs[0][:, width:] = grad_lift
    else:
        outs[0][...] = grad_gate
        outs[1][...] = grad_lift


def middle(x, u, w_gate, w_lift, w_down, scale):
    joined = w_lift is None
    rows, hidden = x.shape[0], w_down.shape[0]
    tile = 256
    whole = dict(pipeline_mode=pl.Buffered(1))
    grads = [hidden * 2] if joined else [hidden, hidden]
    return pl.pallas_call(
        functools.partial(middle_kernel, joined),
        grid=(rows // tile,),
        in_specs=[
            pl.BlockSpec((tile, D), lambda i: (i, 0)),
            pl.BlockSpec((tile, D), lambda i: (i, 0)),
            pl.BlockSpec((D, hidden), lambda i: (0, 0), **whole),
            pl.BlockSpec((D, hidden), lambda i: (0, 1 if joined else 0), **whole),
            pl.BlockSpec((hidden, D), lambda i: (0, 0), **whole),
            pl.BlockSpec((tile, 1), lambda i: (i, 0)),
        ],
        out_specs=[pl.BlockSpec((tile, w), lambda i: (i, 0)) for w in [hidden] + grads + [1]],
        out_shape=[jax.ShapeDtypeStruct((rows, w), bf16) for w in [hidden] + grads]
        + [jax.ShapeDtypeStruct((rows, 1), f32)],
        compiler_params=pltpu.CompilerParams(vmem_limit_bytes=52 * 1024 * 1024),
        cost_estimate=pl.CostEstimate(
            flops=6 * rows * D * hidden,
            bytes_accessed=2 * (2 * rows * D + 3 * hidden * D + 3 * rows * hidden),
            transcendentals=rows * hidden,
        ),
    )(x, u, w_gate, w_gate if joined else w_lift, w_down, scale)


def window(blocks, first, count, axis):
    size = blocks[0].shape[axis]
    return lax.dynamic_slice_in_dim(
        jnp.concatenate(blocks, axis=axis), first * size, count * size, axis
    )


def gather_seq(value):
    seq, place = lax.axis_size("seq"), lax.axis_index("seq")
    if seq != 4:
        return lax.all_gather(value, "seq", axis=0, tiled=True)
    lower, higher, up, down = [], [], value, value
    for hop in range(seq - 1):
        up = lax.ppermute(up, "seq", [(i, i + 1) for i in range(hop, seq - 1)])
        down = lax.ppermute(down, "seq", [(i + 1, i) for i in range(seq - 1 - hop)])
        lower.insert(0, up)
        higher.append(down)
    return window(lower + [value] + higher, seq - 1 - place, seq, 0)


def together(*values):
    return lax.optimization_barrier(values)


def exchange_seq(value, axis_out, axis_in):
    seq, place = lax.axis_size("seq"), lax.axis_index("seq")
    if seq != 4:
        return lax.all_to_all(value, "seq", axis_out, axis_in, tiled=True)
    size = value.shape[axis_out] // seq
    came = []
    for shift in range(seq):
        block = lax.dynamic_slice_in_dim(value, lax.rem(place + shift, seq) * size, size, axis_out)
        if shift:
            block = lax.ppermute(block, "seq", [(i, (i + shift) % seq) for i in range(seq)])
        came.append(block)
    order = [came[shift % seq] for shift in range(seq - 1, -seq, -1)]
    return window(order, seq - 1 - place, seq, axis_in)


def swap(value):
    return lax.all_to_all(value, "fsdp", 0, 0, tiled=True)


def sum_fsdp(value):
    return lax.psum_scatter(value, "fsdp", scatter_dimension=0, tiled=True)


def on_device(
    tokens,
    segments,
    expert_ids,
    expert_gates,
    attn_gain,
    qkv_weight,
    qkv_bias,
    out_weight,
    ffn_gain,
    shared_gate_up,
    shared_down,
    shared_gate,
    expert_gate_up,
    expert_down,
    cotangent,
):
    fsdp, seq = lax.axis_size("fsdp"), lax.axis_size("seq")
    me, place = lax.axis_index("fsdp"), lax.axis_index("seq")
    row_count, length = tokens.shape[1], segments.shape[1]
    heads = HEADS // seq
    group = heads * HEAD_DIM
    copies = fsdp // EXPERTS
    width = D // fsdp
    hidden_own = FF_EXPERT // copies
    piece = hidden_own // fsdp
    factor = 1.0 / math.sqrt(HEAD_DIM)
    capacity = length * TOP // EXPERTS

    names = jnp.arange(EXPERTS, dtype=jnp.int32)
    matches = expert_ids[0][None, :, :] == names[:, None, None]
    gates = jnp.sum(jnp.where(matches, expert_gates[0][None], 0.0), axis=-1)
    gates = jnp.where(jnp.any(matches, axis=-1), gates, -1.0)
    chosen = (gates >= 0.0).astype(jnp.int32)
    tallies = lax.all_gather(jnp.sum(chosen, axis=1), "seq")
    before = jnp.arange(seq, dtype=jnp.int32)[:, None] < place
    offsets = jnp.sum(jnp.where(before, tallies, 0), axis=0)
    earlier = offsets[:, None] + jnp.cumsum(chosen, axis=1) - chosen
    gates = jnp.where((chosen > 0) & (earlier < capacity), gates, 0.0)
    gates = lax.all_gather(gates, "fsdp", axis=0)
    share = lax.dynamic_index_in_dim(gates, me // copies, 1, keepdims=False).reshape(-1, 1)

    all_tokens = gather_seq(tokens[0])
    own = [
        lax.dynamic_slice_in_dim(qkv_weight, part * D + place * group, group, 1)
        for part in range(3)
    ]
    vectors = jnp.concatenate([attn_gain, ffn_gain, shared_gate, qkv_bias])
    extra = -(-6 * width // (3 * group) // 16) * 16
    vectors = jnp.pad(vectors, (0, extra * 3 * group - 6 * width)).reshape(extra, 3 * group)
    gathered = lax.all_gather(
        after(jnp.concatenate([jnp.concatenate(own, axis=1), vectors], axis=0), gates),
        "fsdp",
        axis=0,
    )
    weight_qkv = gathered[:, :width].reshape(D, 3 * group)
    vectors = gathered[:, width:].reshape(fsdp, -1)
    gain_one = vectors[:, :width].reshape(D).astype(f32)
    gain_two = vectors[:, width : 2 * width].reshape(D).astype(f32)
    gate_vector = vectors[:, 2 * width : 3 * width].reshape(D)
    bias = vectors[:, 3 * width : 6 * width].reshape(3, seq, group)
    bias = lax.dynamic_index_in_dim(bias, place, 1, keepdims=False).reshape(-1).astype(f32)
    weight_out = lax.all_gather(out_weight, "fsdp", axis=0, tiled=True)
    upstream_all = lax.all_gather(cotangent[0], "fsdp", axis=0, tiled=True)

    up_sent = expert_gate_up.reshape(EXPERTS, width, 2, fsdp, copies, piece)
    up_sent = up_sent.transpose(0, 4, 1, 2, 3, 5).reshape(fsdp, width, 2 * hidden_own)
    down_sent = expert_down.reshape(fsdp, piece, D)
    if seq == 4:
        half = lax.rem(place, 2)
        fetched = swap(lax.dynamic_slice_in_dim(up_sent, half * (width // 2), width // 2, 1))
        given = lax.ppermute(fetched, "seq", [(0, 1), (1, 0), (2, 3), (3, 2)])
    else:
        fetched = given = swap(up_sent)

    x_all = all_tokens.astype(f32)
    normed_unit = x_all * rms_scale(x_all)
    normed = (normed_unit * gain_one).astype(bf16)
    cosine, sine = rope_tables(jnp.arange(length, dtype=jnp.int32))
    normed = after(normed, weight_qkv)
    joined = dot(normed, weight_qkv, ((1,), (0,))) + bias
    split = joined.reshape(length, 3, heads, HEAD_DIM)
    queries = rotate(split[:, 0], cosine, sine).astype(bf16)
    keys = rotate(split[:, 1], cosine, sine).astype(bf16)
    values = split[:, 2].astype(bf16)
    documents = segments[0]
    mixed, logs = attend(queries, keys, values, documents, factor)
    mixed_rows = exchange_seq(mixed.reshape(length, group), 0, 1)
    mixed_rows = after(mixed_rows, upstream_all)
    inputs = tokens[0].astype(f32)
    hidden = inputs + dot(mixed_rows, weight_out, ((1,), (0,)))
    scale_two = rms_scale(hidden)
    second = (hidden * scale_two * gain_two).astype(bf16)
    second_all = lax.all_gather(after(second, fetched), "fsdp", axis=0, tiled=True)

    weight_down = swap(after(down_sent, second_all)).reshape(hidden_own, D)
    by_kernel = seq == 4 and fsdp == 8
    s_gate, s_lift = shared_gate_up[:, 0], shared_gate_up[:, 1]
    opening_all = jax.nn.sigmoid(dot(second_all, gate_vector, ((1,), (0,))))[:, None]
    inner_s, ga_s, gl_s, reach = middle(
        second_all, upstream_all, s_gate, s_lift, shared_down, opening_all
    )
    grad_s_down = dot(upstream_all, inner_s, ((0,), (0,)), bf16)
    grad_s_gate = dot(second_all, ga_s, ((0,), (0,)), bf16)
    grad_s_lift = dot(second_all, gl_s, ((0,), (0,)), bf16)

    given, fetched = after((given, fetched), grad_s_down, grad_s_gate, grad_s_lift)
    if by_kernel:
        *sum_s, inner_e, grads_e, grad_second_all, out_all = feed_forward(
            (grad_s_down, grad_s_gate, grad_s_lift),
            (second_all, upstream_all, ga_s, gl_s, inner_s),
            (
                fetched.reshape(D // 2, -1),
                given.reshape(D // 2, -1),
                weight_down,
                s_gate,
                s_lift,
                shared_down,
            ),
            share,
            2,
        )
        grad_second = sum_fsdp(grad_second_all)
        grad_e_down = dot(inner_e, upstream_all, ((0,), (0,)), bf16)
        grad_e_up = dot(second_all, after(grads_e, grad_e_down), ((0,), (0,)), bf16)
        reach = jnp.sum(swap(after(reach.reshape(fsdp, row_count), inner_e)), axis=0)
        out_all = after(out_all, grad_e_up)
    else:
        weight_up = given
        if seq == 4:
            weight_up = jnp.concatenate(
                [jnp.where(half == 0, fetched, given), jnp.where(half == 0, given, fetched)],
                axis=1,
            )
        weight_up = weight_up.reshape(D, 2 * hidden_own)
        held = after(second_all, grad_s_down, grad_s_gate, grad_s_lift)
        if hidden_own % 128 == 0:
            inner_e, grads_e, _ = middle(held, upstream_all, weight_up, None, weight_down, share)
        else:
            inner_e, ga_e, gl_e, _ = middle(
                held,
                upstream_all,
                weight_up[:, :hidden_own],
                weight_up[:, hidden_own:],
                weight_down,
                share,
            )
            grads_e = jnp.concatenate([ga_e, gl_e], axis=1)
        part = dot(inner_e, upstream_all, ((0,), (0,)), bf16)
        grad_e_down = part
        reach = jnp.sum(swap(after(reach.reshape(fsdp, row_count), part)), axis=0)

        grads_e, ga_s, gl_s = after((grads_e, ga_s, gl_s), part)
        grad_second_all = (
            dot(ga_s, s_gate, ((1,), (1,)))
            + dot(gl_s, s_lift, ((1,), (1,)))
            + dot(grads_e, weight_up, ((1,), (1,)))
        ).astype(bf16)
        grad_second = sum_fsdp(grad_second_all)

        grad_e_up = dot(second_all, after(grads_e, grad_second_all), ((0,), (0,)), bf16)

        inner_s, inner_e = after((inner_s, inner_e), grad_e_up)
        out_all = (
            dot(inner_s, shared_down, ((1,), (0,))) + dot(inner_e, weight_down, ((1,), (0,)))
        ).astype(bf16)
        sum_s = lax.psum((grad_s_down, grad_s_gate, grad_s_lift), "seq")

    grad_second, reach = after((grad_second, reach), out_all)
    upstream = cotangent[0].astype(f32)
    opening = jax.nn.sigmoid(dot(second, gate_vector, ((1,), (0,))))
    grad_logit = reach * opening * (1.0 - opening)
    grad_second = grad_second.astype(f32) + grad_logit[:, None] * gate_vector.astype(f32)[None, :]
    grad_gate_vector = jnp.sum(grad_logit[:, None] * second.astype(f32), axis=0)
    grad_hidden = upstream + norm_back(hidden, scale_two, gain_two, grad_second)
    grad_gain_two = jnp.sum(grad_second * hidden * scale_two, axis=0)
    grad_projected = grad_hidden.astype(bf16)
    grad_mixture = dot(grad_projected, weight_out, ((1,), (1,)), bf16)
    grad_heads = exchange_seq(grad_mixture, 1, 0)
    grad_out = dot(mixed_rows, after(grad_projected, grad_mixture), ((0,), (0,)), bf16)

    grad_heads = after(grad_heads, grad_out)
    grad_queries, grad_keys, grad_values = attend_back(
        queries,
        keys,
        values,
        documents,
        factor,
        logs,
        grad_heads.reshape(length, heads, HEAD_DIM),
    )
    grad_joined = jnp.stack(
        [
            rotate_back(grad_queries.astype(bf16).astype(f32), cosine, sine),
            rotate_back(grad_keys.astype(bf16).astype(f32), cosine, sine),
            grad_values,
        ],
        axis=1,
    )
    grad_joined = grad_joined.reshape(length, 3 * group).astype(bf16)
    grad_normed_all = dot(grad_joined, weight_qkv, ((1,), (1,)))
    grad_gain_one = jnp.sum(grad_normed_all * normed_unit, axis=0)

    grad_qkv = dot(normed, grad_joined, ((0,), (0,)), bf16).reshape(fsdp, width, 3 * group)
    grad_bias = jnp.sum(grad_joined.astype(f32), axis=0).reshape(3, 1, group)
    own_heads = (jnp.arange(seq, dtype=jnp.int32) == place).astype(f32)
    grad_bias = (grad_bias * own_heads[None, :, None]).reshape(fsdp, 3 * width)
    rows = jnp.concatenate(
        [
            grad_gain_one.reshape(fsdp, width),
            grad_gain_two.reshape(fsdp, width),
            grad_gate_vector.reshape(fsdp, width),
            grad_bias,
        ],
        axis=1,
    ).astype(bf16)
    rows = jnp.pad(rows, ((0, 0), (0, extra * 3 * group - 6 * width)))
    rows = rows.reshape(fsdp, extra, 3 * group)
    grad_qkv = jnp.concatenate([grad_qkv, rows], axis=1)

    grad_out = sum_fsdp(grad_out)
    grad_normed_all = grad_normed_all.astype(bf16)
    grad_e_up, grad_out, grad_qkv, grad_normed_all, out_all = together(
        grad_e_up, grad_out, grad_qkv, grad_normed_all, out_all
    )
    grad_qkv = lax.psum_scatter(
        grad_qkv.reshape(-1, 3 * group), "fsdp", scatter_dimension=0, tiled=True
    )
    grad_normed = lax.psum_scatter(grad_normed_all, "seq", scatter_dimension=0, tiled=True)
    out_part = lax.psum_scatter(out_all, "fsdp", scatter_dimension=0, tiled=True)
    if by_kernel:
        sum_e_up, sum_e_down, sum_out = combine(
            [(grad_e_up, True, 64), (grad_e_down, True, 176), (grad_out, False, 64)], 1
        )
        sum_e_up = sum_e_up.reshape(EXPERTS, width, 2 * FF_EXPERT)
        sum_e_down = sum_e_down.reshape(EXPERTS, piece, D)
    else:
        sum_e_up = swap(grad_e_up.reshape(fsdp, width, 2 * hidden_own))
        sum_e_down = swap(grad_e_down.reshape(fsdp, piece, D))
        sum_e_up, sum_e_down, sum_out = lax.psum((sum_e_up, sum_e_down, grad_out), "seq")
        sum_e_down = sum_e_down.reshape(EXPERTS, copies * piece, D)
        sum_e_up = sum_e_up.reshape(EXPERTS, copies, width, 2, fsdp, piece)
        sum_e_up = sum_e_up.transpose(0, 2, 3, 4, 1, 5).reshape(EXPERTS, width, 2 * FF_EXPERT)
    output = (hidden + out_part.astype(f32)).astype(bf16)
    grad_normed = grad_normed.astype(f32)
    grad_qkv = lax.all_gather(after(grad_qkv, sum_out), "seq", axis=0)
    rows = jnp.sum(grad_qkv[:, width:].astype(f32), axis=0).reshape(-1)
    grad_qkv = jnp.concatenate(
        [
            grad_qkv[owner, :width, part * group : (part + 1) * group]
            for part in range(3)
            for owner in range(seq)
        ],
        axis=1,
    ).astype(f32)
    input_grad = (grad_hidden + norm_back(inputs, rms_scale(inputs), gain_one, grad_normed)).astype(
        bf16
    )
    sum_s_up = jnp.stack([sum_s[1], sum_s[2]], axis=1)

    return (
        output[None],
        input_grad[None],
        rows[:width],
        grad_qkv,
        rows[3 * width : 6 * width],
        sum_out.astype(f32),
        rows[width : 2 * width],
        sum_s_up.astype(f32),
        sum_s[0].T.astype(f32),
        rows[2 * width : 3 * width],
        sum_e_up.astype(f32),
        sum_e_down.astype(f32),
    )


def solution(mesh):
    return jax.shard_map(
        on_device,
        mesh=mesh,
        in_specs=(
            P("fsdp", "seq", None),
            P("fsdp", None),
            P("fsdp", "seq", None),
            P("fsdp", "seq", None),
            P("fsdp"),
            P("fsdp", None),
            P("fsdp"),
            P("fsdp", None),
            P("fsdp"),
            P(None, None, "fsdp"),
            P("fsdp", None),
            P("fsdp"),
            P(None, "fsdp", None),
            P(None, "fsdp", None),
            P("fsdp", "seq", None),
        ),
        out_specs=(
            P("fsdp", "seq", None),
            P("fsdp", "seq", None),
            P("fsdp"),
            P("fsdp", None),
            P("fsdp"),
            P("fsdp", None),
            P("fsdp"),
            P(None, None, "fsdp"),
            P("fsdp", None),
            P("fsdp"),
            P(None, "fsdp", None),
            P(None, "fsdp", None),
        ),
        check_vma=False,
    )
```

```python
import functools
import math

import jax
import jax.numpy as jnp
from jax import lax
from jax.experimental import pallas as pl
from jax.experimental.pallas import tpu as pltpu
from jax.sharding import PartitionSpec as P

D = 2048
HEADS = 16
HEAD_DIM = 128
FF_EXPERT = 1408
TOP = 4
EXPERTS = 8
QBLOCK = 256
DOC_MOST = 512

EPSILON = 1e-06
THETA = 1000000.0

bf16 = jnp.bfloat16
f32 = jnp.float32


def dot(a, b, contract, kind=f32):
    return lax.dot_general(a, b, (contract, ((), ())), preferred_element_type=f32).astype(kind)


def rms_scale(values):
    return lax.rsqrt(jnp.mean(values * values, axis=-1, keepdims=True) + EPSILON)


def norm_back(values, scale, gain, grad):
    scaled = grad * gain
    centre = jnp.mean(scaled * values, axis=-1, keepdims=True)
    return scale * (scaled - values * (scale * scale) * centre)


def rope_tables(positions):
    steps_half = jnp.arange(HEAD_DIM // 2, dtype=jnp.int32).astype(f32)
    frequency = jnp.exp(steps_half * (-2.0 * math.log(THETA) / HEAD_DIM))
    angles = positions.astype(f32)[:, None] * frequency[None, :]
    angles = jnp.concatenate([angles, angles], axis=-1)
    return (jnp.cos(angles), jnp.sin(angles))


def rotate(rows, cosine, sine):
    middle = rows.shape[-1] // 2
    turned = jnp.concatenate([-rows[..., middle:], rows[..., :middle]], axis=-1)
    return rows * cosine[:, None, :] + turned * sine[:, None, :]


def rotate_back(rows, cosine, sine):
    middle = rows.shape[-1] // 2
    turned = rows * sine[:, None, :]
    turned = jnp.concatenate([turned[..., middle:], -turned[..., :middle]], axis=-1)
    return rows * cosine[:, None, :] + turned


def key_start(block):
    return max(0, block * QBLOCK - DOC_MOST)


def block_scores(block, queries, keys, documents, factor):
    first, start = block * QBLOCK, key_start(block)
    stop = first + QBLOCK
    scores = (
        jnp.einsum(
            "qhd,khd->hqk", queries[first:stop], keys[start:stop], preferred_element_type=f32
        )
        * factor
    )
    rows = first + jnp.arange(QBLOCK, dtype=jnp.int32)
    columns = start + jnp.arange(stop - start, dtype=jnp.int32)
    allowed = (rows[:, None] >= columns[None, :]) & (
        documents[first:stop, None] == documents[None, start:stop]
    )
    return jnp.where(allowed[None], scores, -1e30)


def attend(queries, keys, values, documents, factor):
    mixed, logs = [], []
    for block in range(queries.shape[0] // QBLOCK):
        start, stop = key_start(block), (block + 1) * QBLOCK
        scores = block_scores(block, queries, keys, documents, factor)
        top = jnp.max(scores, axis=-1, keepdims=True)
        weights = jnp.exp(scores - top)
        totals = jnp.sum(weights, axis=-1, keepdims=True)
        probability = (weights / totals).astype(bf16)
        mixed.append(
            jnp.einsum(
                "hqk,khd->qhd", probability, values[start:stop], preferred_element_type=f32
            ).astype(bf16)
        )
        logs.append(top + jnp.log(totals))
    return jnp.concatenate(mixed, axis=0), logs


def attend_back(queries, keys, values, documents, factor, logs, grads):
    length = queries.shape[0]
    grad_queries = []
    grad_keys = jnp.zeros(keys.shape, f32)
    grad_values = jnp.zeros(values.shape, f32)
    for block in range(length // QBLOCK):
        start, stop = key_start(block), (block + 1) * QBLOCK
        scores = block_scores(block, queries, keys, documents, factor)
        probability = jnp.exp(scores - logs[block])
        grad_block = grads[block * QBLOCK : stop]
        query_block = queries[block * QBLOCK : stop]
        grad_values = grad_values.at[start:stop].add(
            jnp.einsum(
                "hqk,qhd->khd", probability.astype(bf16), grad_block, preferred_element_type=f32
            )
        )
        grad_probability = jnp.einsum(
            "qhd,khd->hqk", grad_block, values[start:stop], preferred_element_type=f32
        )
        centre = jnp.sum(grad_probability * probability, axis=-1, keepdims=True)
        grad_scores = (probability * (grad_probability - centre)).astype(bf16)
        grad_queries.append(
            jnp.einsum("hqk,khd->qhd", grad_scores, keys[start:stop], preferred_element_type=f32)
            * factor
        )
        grad_keys = grad_keys.at[start:stop].add(
            jnp.einsum("hqk,qhd->khd", grad_scores, query_block, preferred_element_type=f32)
            * factor
        )
    return jnp.concatenate(grad_queries, axis=0), grad_keys, grad_values


def after(value, *earlier):
    return lax.optimization_barrier((value, earlier))[0]


def line_neighbours(place):
    middle = lax.rem(place + 1, 4) // 2
    low = 1 - place // 2
    partner = low * (1 - place) + (1 - low) * (5 - place)
    across = low * 2 + (1 - low) * 1
    return middle, partner, across


def flip(index, bits):
    result, step = 0, 1
    while step < 8:
        bit = lax.rem(index // step, 2)
        result = result + step * (1 - bit if bits & step else bit)
        step *= 2
    return result


SLOTS = 4
ORDER = (0, 1, 2, 4, 3, 5, 6, 7)
LEAVE = {2: ((2, 4), (3, 5)), 4: ((3, 5), (6, 7))}


def combine_kernel(plan, *refs):
    count = len(plan)
    sources, refs = refs[:count], refs[count:]
    results, refs = refs[:count], refs[count:]
    lands, refs = refs[:count], refs[count:]
    buffers, refs = refs[: 5 * count], refs[5 * count :]
    (land_send, land_recv, g_sem, a_send, a_recv, b_send, b_recv, c_send, c_recv) = refs[:9]
    out_sem, a_free, b_free = refs[9:]
    me, place = lax.axis_index("fsdp"), lax.axis_index("seq")
    middle, partner, across = line_neighbours(place)
    peers = [flip(me, k) for k in range(8)]

    barrier = pltpu.get_barrier_semaphore()
    swapping = any(swapped for swapped, _, _, _ in plan)
    if swapping:
        for k in range(1, 8):
            pl.semaphore_signal(
                barrier, device_id={"fsdp": peers[k]}, device_id_type=pl.DeviceIdType.MESH
            )
    pl.semaphore_signal(
        barrier, device_id={"seq": partner}, device_id_type=pl.DeviceIdType.MESH
    )

    @pl.when(middle == 1)
    def _():
        pl.semaphore_signal(
            barrier, device_id={"seq": across}, device_id_type=pl.DeviceIdType.MESH
        )

    pl.semaphore_wait(barrier, 1 + middle + (7 if swapping else 0))

    arrivals = {}
    for index, (swapped, rows, blocks, _) in enumerate(plan):
        if not swapped:
            continue
        here = pl.ds(pl.multiple_of(me * rows, 16), rows)
        for k in range(1, 8):
            there = pl.ds(pl.multiple_of(peers[k] * rows, 16), rows)
            copy = pltpu.make_async_remote_copy(
                src_ref=sources[index].at[there],
                dst_ref=lands[index].at[here],
                send_sem=land_send.at[index, k],
                recv_sem=land_recv.at[index, k],
                device_id={"fsdp": peers[k]},
                device_id_type=pl.DeviceIdType.MESH,
            )
            arrivals[index, k] = copy
            if k in (1, 2, 4):
                copy.start()

    chunks, starts = [], []
    for index, (swapped, rows, blocks, size) in enumerate(plan):
        starts.append(len(chunks))
        for block in range(blocks):
            base = (peers[ORDER[block]] if swapped else block) * rows
            for first in range(0, rows, size):
                chunks.append((index, block if first == 0 else None, base + first, size))
    total = len(chunks)

    def landed(c):
        index, block, _, _ = chunks[c]
        if not plan[index][0] or block is None:
            return
        if block > 0:
            arrivals[index, ORDER[block]].wait_recv()
        if block in LEAVE:
            left, leaving = LEAVE[block]
            for k in left:
                arrivals[index, k].wait_send()
            for k in leaving:
                arrivals[index, k].start()

    def place_of(c, ref_list):
        index, _, start, size = chunks[c]
        if isinstance(start, int):
            return ref_list[index].at[pl.ds(start, size)]
        return ref_list[index].at[pl.ds(pl.multiple_of(start, 16), size)]

    def held(c, which):
        return buffers[5 * chunks[c][0] + which].at[c % SLOTS]

    def given(c):
        index, _, _, size = chunks[c]
        away = plan[index][0] and size * (c - starts[index]) >= plan[index][1]
        return place_of(c, lands if away else sources)

    def inward(c):
        return pltpu.make_async_remote_copy(
            src_ref=given(c),
            dst_ref=held(c, 1),
            send_sem=a_send.at[c % SLOTS],
            recv_sem=a_recv.at[c % SLOTS],
            device_id={"seq": partner},
            device_id_type=pl.DeviceIdType.MESH,
        )

    def crossing(c):
        return pltpu.make_async_remote_copy(
            src_ref=held(c, 2),
            dst_ref=held(c, 3),
            send_sem=b_send.at[c % SLOTS],
            recv_sem=b_recv.at[c % SLOTS],
            device_id={"seq": across},
            device_id_type=pl.DeviceIdType.MESH,
        )

    def outward(c):
        return pltpu.make_async_remote_copy(
            src_ref=held(c, 4),
            dst_ref=place_of(c, results),
            send_sem=c_send.at[c % SLOTS],
            recv_sem=c_recv.at[c],
            device_id={"seq": partner},
            device_id_type=pl.DeviceIdType.MESH,
        )

    def fetch(c):
        return pltpu.make_async_copy(given(c), held(c, 0), g_sem.at[c % SLOTS])

    def keep(c):
        return pltpu.make_async_copy(held(c, 4), place_of(c, results), out_sem.at[c % SLOTS])

    @pl.when(middle == 0)
    def _():
        for c in range(total):
            landed(c)
            if c >= SLOTS:
                inward(c - SLOTS).wait_send()
                pl.semaphore_wait(a_free, 1)
            inward(c).start()
        for c in range(max(0, total - SLOTS), total):
            inward(c).wait_send()
        for c in range(total):
            outward(c).wait_recv()

    @pl.when(middle == 1)
    def _():
        for c in range(min(SLOTS, total)):
            landed(c)
            fetch(c).start()
        for i in range(total + 1):
            c = i
            if c < total:
                fetch(c).wait()
                inward(c).wait_recv()
                if c >= SLOTS:
                    crossing(c - SLOTS).wait_send()
                held(c, 2)[...] = (
                    held(c, 0)[...].astype(f32) + held(c, 1)[...].astype(f32)
                ).astype(bf16)
                if c + SLOTS < total:
                    pl.semaphore_signal(
                        a_free, device_id={"seq": partner}, device_id_type=pl.DeviceIdType.MESH
                    )
                if c >= SLOTS:
                    pl.semaphore_wait(b_free, 1)
                crossing(c).start()
                if c + SLOTS < total:
                    landed(c + SLOTS)
                    fetch(c + SLOTS).start()
            c = i - 1
            if c >= 0:
                crossing(c).wait_recv()
                if c >= SLOTS:
                    keep(c - SLOTS).wait()
                    outward(c - SLOTS).wait_send()
                held(c, 4)[...] = (
                    held(c, 2)[...].astype(f32) + held(c, 3)[...].astype(f32)
                ).astype(bf16)
                if c + SLOTS < total:
                    pl.semaphore_signal(
                        b_free, device_id={"seq": across}, device_id_type=pl.DeviceIdType.MESH
                    )
                outward(c).start()
                keep(c).start()
        for c in range(max(0, total - SLOTS), total):
            crossing(c).wait_send()
            keep(c).wait()
            outward(c).wait_send()

    for (_, k), copy in arrivals.items():
        if k in (1, 6, 7):
            copy.wait_send()


def combine(arrays, number):
    plan = []
    for value, swapped, size in arrays:
        rows = value.shape[0] // 8 if swapped else value.shape[0]
        plan.append((swapped, rows, 8 if swapped else 1, size))
    count = len(plan)
    total = sum(rows // size * blocks for _, rows, blocks, size in plan)
    shapes = [jax.ShapeDtypeStruct(value.shape, bf16) for value, _, _ in arrays]
    lands = [
        jax.ShapeDtypeStruct(value.shape if swapped else (16, 128), bf16)
        for value, swapped, _ in arrays
    ]
    buffers = [
        pltpu.VMEM((SLOTS, size, value.shape[1]), bf16)
        for value, _, size in arrays
        for _ in range(5)
    ]
    dma = pltpu.SemaphoreType.DMA
    moved = sum(value.size for value, _, _ in arrays)
    anywhere = pl.BlockSpec(memory_space=pl.ANY)
    return pl.pallas_call(
        functools.partial(combine_kernel, tuple(plan)),
        out_shape=shapes + lands,
        in_specs=[anywhere] * count,
        out_specs=[anywhere] * (2 * count),
        scratch_shapes=buffers
        + [
            dma((count, 8)),
            dma((count, 8)),
            dma((SLOTS,)),
            dma((SLOTS,)),
            dma((SLOTS,)),
            dma((SLOTS,)),
            dma((SLOTS,)),
            dma((SLOTS,)),
            dma((total,)),
            dma((SLOTS,)),
            pltpu.SemaphoreType.REGULAR,
            pltpu.SemaphoreType.REGULAR,
        ],
        compiler_params=pltpu.CompilerParams(
            collective_id=number, has_side_effects=True, vmem_limit_bytes=48 * 1024 * 1024
        ),
        cost_estimate=pl.CostEstimate(
            flops=2 * moved, bytes_accessed=200 * moved, transcendentals=0
        ),
        name="combine_%d" % number,
    )(*[value for value, _, _ in arrays])[:count]


HOST_BLOCKS = 8
SUM_BLOCKS = 16


def feed_forward_kernel(*refs):
    sources, refs = refs[:3], refs[3:]
    tiles_in, refs = refs[:5], refs[5:]
    near, far, *weights = refs[:6]
    share, refs = refs[6], refs[7:]
    results, refs = refs[:3], refs[3:]
    tiles_out, refs = refs[:4], refs[4:]
    zg, za, zs, zb, zt = refs[:5]
    refs = refs[5:]
    held, refs = refs[:5], refs[5:]
    v_up, v_down, v_sg, v_sl, v_sd = held
    loaded, refs = refs[:5], refs[5:]
    v_x, v_u, v_ga, v_gl, v_in = loaded
    stored, refs = refs[:4], refs[4:]
    t_in, t_grads, t_second, t_out = stored
    (w_sem, l_sem, s_sem, g_sem, a_send, a_recv, b_send, b_recv, c_send, c_recv) = refs[:10]
    out_sem, a_free, b_free = refs[10:]
    place = lax.axis_index("seq")
    middle, partner, across = line_neighbours(place)
    tile = v_x.shape[1]
    hidden = v_down.shape[0]
    last = SUM_BLOCKS - 1
    pace = SUM_BLOCKS // HOST_BLOCKS
    block = za.shape[2]

    half = lax.rem(place, 2)
    cut_rows = v_up.shape[0] // 16
    copies = [
        pltpu.make_async_copy(weights[index], held[index + 1], w_sem.at[index])
        for index in range(4)
    ]
    for owner in range(8):
        source = pl.ds(owner * cut_rows, cut_rows)
        for which, (ref, side) in enumerate(((near, half), (far, 1 - half))):
            first = pl.multiple_of((2 * owner + side) * cut_rows, cut_rows)
            copies.append(
                pltpu.make_async_copy(
                    ref.at[source],
                    v_up.at[pl.ds(first, cut_rows)],
                    w_sem.at[4 + 2 * owner + which],
                )
            )
    for copy in copies:
        copy.start()

    barrier = pltpu.get_barrier_semaphore()
    pl.semaphore_signal(
        barrier, device_id={"seq": partner}, device_id_type=pl.DeviceIdType.MESH
    )

    @pl.when(middle == 1)
    def _():
        pl.semaphore_signal(
            barrier, device_id={"seq": across}, device_id_type=pl.DeviceIdType.MESH
        )

    pl.semaphore_wait(barrier, 1 + middle)

    def rows(o, size=block):
        return pl.ds(o * size if isinstance(o, int) else pl.multiple_of(o * size, size), size)

    def slot(o):
        return o % 2 if isinstance(o, int) else lax.rem(o, 2)

    def remote(source, target, sent, received, where):
        return pltpu.make_async_remote_copy(
            src_ref=source,
            dst_ref=target,
            send_sem=sent,
            recv_sem=received,
            device_id={"seq": where},
            device_id_type=pl.DeviceIdType.MESH,
        )

    def inward(o, a):
        i = slot(o)
        return remote(
            sources[a].at[rows(o)], za.at[i, a], a_send.at[i, a], a_recv.at[i, a], partner
        )

    def crossing(o, a):
        i = slot(o)
        return remote(zs.at[i, a], zb.at[i, a], b_send.at[i, a], b_recv.at[i, a], across)

    def outward(o, a):
        i = slot(o)
        return remote(
            zt.at[i, a], results[a].at[rows(o)], c_send.at[i, a], c_recv.at[o, a], partner
        )

    def fetch(o, a):
        i = slot(o)
        return pltpu.make_async_copy(sources[a].at[rows(o)], zg.at[i, a], g_sem.at[i, a])

    def keep(o, a):
        i = slot(o)
        return pltpu.make_async_copy(zt.at[i, a], results[a].at[rows(o)], out_sem.at[i, a])

    def load(o, index):
        i = slot(o)
        return pltpu.make_async_copy(
            tiles_in[index].at[rows(o, tile)], loaded[index].at[i], l_sem.at[i, index]
        )

    def store(o, index):
        return pltpu.make_async_copy(stored[index], tiles_out[index].at[rows(o, tile)], s_sem.at[index])

    for index in range(5):
        load(0, index).start()

    @pl.when(middle == 0)
    def _():
        for o in (0, 1):
            for a in range(3):
                inward(o, a).start()

    @pl.when(middle == 1)
    def _():
        for o in (0, 1):
            for a in range(3):
                fetch(o, a).start()

    for copy in copies:
        copy.wait()

    def add(left, right):
        return (left.astype(f32) + right.astype(f32)).astype(bf16)

    def end_step(o):
        @pl.when((o >= 1) & (o < last))
        def _():
            for a in range(3):
                inward(o - 1, a).wait_send()
                pl.semaphore_wait(a_free, 1)
                inward(o + 1, a).start()

    def middle_step(o):
        @pl.when(o <= last)
        def _():
            i = slot(o)
            for a in range(3):
                fetch(o, a).wait()
                inward(o, a).wait_recv()

                @pl.when(o >= 2)
                def _():
                    crossing(o - 2, a).wait_send()
                    pl.semaphore_wait(b_free, 1)

                zs[i, a] = add(zg[i, a], za[i, a])
                crossing(o, a).start()

                @pl.when(o + 2 <= last)
                def _():
                    pl.semaphore_signal(
                        a_free, device_id={"seq": partner}, device_id_type=pl.DeviceIdType.MESH
                    )
                    fetch(o + 2, a).start()

        @pl.when(o >= 1)
        def _():
            p = o - 1
            i = slot(p)
            for a in range(3):
                crossing(p, a).wait_recv()

                @pl.when(p >= 2)
                def _():
                    keep(p - 2, a).wait()
                    outward(p - 2, a).wait_send()

                zt[i, a] = add(zs[i, a], zb[i, a])

                @pl.when(p + 2 <= last)
                def _():
                    pl.semaphore_signal(
                        b_free, device_id={"seq": across}, device_id_type=pl.DeviceIdType.MESH
                    )

                outward(p, a).start()
                keep(p, a).start()

    def across_rows(left, right):
        return lax.dot_general(left, right, (((1,), (1,)), ((), ())), preferred_element_type=f32)

    def host(o):
        i = slot(o)
        for index in range(5):
            load(o, index).wait()

        @pl.when(o < HOST_BLOCKS - 1)
        def _():
            for index in range(5):
                load(o + 1, index).start()

        @pl.when(o >= 1)
        def _():
            for index in range(4):
                store(o - 1, index).wait()

        scale = share[rows(o, tile), :]
        cut = hidden // 256 * 128
        for first, end in ((0, cut), (cut, hidden)):
            gate = jnp.dot(v_x[i], v_up[:, first:end], preferred_element_type=f32)
            lift = jnp.dot(
                v_x[i], v_up[:, hidden + first : hidden + end], preferred_element_type=f32
            )
            grad = across_rows(v_u[i], v_down[first:end, :]) * scale
            sigma = 1.0 / (1.0 + jnp.exp(-gate))
            silu = gate * sigma
            t_in[:, first:end] = (silu * lift * scale).astype(bf16)
            t_grads[:, first:end] = (
                grad * lift * sigma * (1.0 + gate * (1.0 - sigma))
            ).astype(bf16)
            t_grads[:, hidden + first : hidden + end] = (grad * silu).astype(bf16)
        for first in range(0, D, 512):
            end = first + 512
            t_second[:, first:end] = (
                across_rows(t_grads[...], v_up[first:end, :])
                + across_rows(v_ga[i], v_sg[first:end, :])
                + across_rows(v_gl[i], v_sl[first:end, :])
            ).astype(bf16)
            t_out[:, first:end] = (
                jnp.dot(t_in[...], v_down[:, first:end], preferred_element_type=f32)
                + jnp.dot(v_in[i], v_sd[:, first:end], preferred_element_type=f32)
            ).astype(bf16)
        for index in range(4):
            store(o, index).start()

    def step(o, carry):
        @pl.when(middle == 0)
        def _():
            end_step(o)

        @pl.when(middle == 1)
        def _():
            middle_step(o)

        @pl.when((o <= last) & (lax.rem(o, pace) == 0))
        def _():
            host(o // pace)

        return carry

    lax.fori_loop(0, SUM_BLOCKS + 1, step, 0)
    for index in range(4):
        store(HOST_BLOCKS - 1, index).wait()

    @pl.when(middle == 0)
    def _():
        for a in range(3):
            for o in (last - 1, last):
                inward(o, a).wait_send()
            for o in range(SUM_BLOCKS):
                outward(o, a).wait_recv()

    @pl.when(middle == 1)
    def _():
        for a in range(3):
            for o in (last - 1, last):
                crossing(o, a).wait_send()
                keep(o, a).wait()
                outward(o, a).wait_send()


def feed_forward(sums, tiles, weights, share, number):
    rows, cut = sums[0].shape
    tile = rows // HOST_BLOCKS
    hidden = weights[2].shape[0]
    dma = pltpu.SemaphoreType.DMA
    anywhere = pl.BlockSpec(memory_space=pl.ANY)
    outs = [hidden, 2 * hidden, D, D]
    return pl.pallas_call(
        feed_forward_kernel,
        out_shape=[jax.ShapeDtypeStruct((rows, cut), bf16)] * 3
        + [jax.ShapeDtypeStruct((rows, w), bf16) for w in outs],
        in_specs=[anywhere] * 14 + [pl.BlockSpec(memory_space=pltpu.VMEM)],
        out_specs=[anywhere] * 7,
        scratch_shapes=[pltpu.VMEM((2, 3, rows // SUM_BLOCKS, cut), bf16)] * 5
        + [pltpu.VMEM((D, 2 * hidden), bf16)]
        + [pltpu.VMEM(w.shape, bf16) for w in weights[2:]]
        + [pltpu.VMEM((2, tile, t.shape[1]), bf16) for t in tiles]
        + [pltpu.VMEM((tile, w), bf16) for w in outs]
        + [
            dma((20,)),
            dma((2, 5)),
            dma((4,)),
            dma((2, 3)),
            dma((2, 3)),
            dma((2, 3)),
            dma((2, 3)),
            dma((2, 3)),
            dma((2, 3)),
            dma((SUM_BLOCKS, 3)),
            dma((2, 3)),
            pltpu.SemaphoreType.REGULAR,
            pltpu.SemaphoreType.REGULAR,
        ],
        compiler_params=pltpu.CompilerParams(
            collective_id=number, has_side_effects=True, vmem_limit_bytes=60 * 1024 * 1024
        ),
        cost_estimate=pl.CostEstimate(
            flops=2 * rows * D * (6 * hidden + 3 * cut),
            bytes_accessed=800 * 1024 * 1024,
            transcendentals=rows * hidden,
        ),
    )(*sums, *tiles, *weights, share)


def middle_kernel(joined, ahead, x, u, w_gate, w_lift, w_down, scale, inner, *outs):
    gate = jnp.dot(x[...], w_gate[...], preferred_element_type=f32)
    lift = jnp.dot(x[...], w_lift[...], preferred_element_type=f32)
    if ahead:
        raw = u[...]
    else:
        raw = lax.dot_general(
            u[...], w_down[...], (((1,), (1,)), ((), ())), preferred_element_type=f32
        )
    sigma = 1.0 / (1.0 + jnp.exp(-gate))
    silu = gate * sigma
    product = silu * lift
    outs[-1][...] = jnp.sum(product * raw, axis=1, keepdims=True)
    inner[...] = (product * scale[...]).astype(bf16)
    grad = raw * scale[...]
    grad_gate = (grad * lift * sigma * (1.0 + gate * (1.0 - sigma))).astype(bf16)
    grad_lift = (grad * silu).astype(bf16)
    if joined:
        width = grad_gate.shape[1]
        outs[0][:, :width] = grad_gate
        outs[0][:, width:] = grad_lift
    else:
        outs[0][...] = grad_gate
        outs[1][...] = grad_lift


def middle(x, u, w_gate, w_lift, w_down, scale):
    joined = w_lift is None
    rows, hidden = x.shape[0], w_down.shape[0]
    ahead = u.shape[1] == hidden
    tile = 256
    whole = dict(pipeline_mode=pl.Buffered(1))
    grads = [hidden * 2] if joined else [hidden, hidden]
    return pl.pallas_call(
        functools.partial(middle_kernel, joined, ahead),
        grid=(rows // tile,),
        in_specs=[
            pl.BlockSpec((tile, D), lambda i: (i, 0)),
            pl.BlockSpec((tile, u.shape[1]), lambda i: (i, 0)),
            pl.BlockSpec((D, hidden), lambda i: (0, 0), **whole),
            pl.BlockSpec((D, hidden), lambda i: (0, 1 if joined else 0), **whole),
            pl.BlockSpec((16 if ahead else hidden, D), lambda i: (0, 0), **whole),
            pl.BlockSpec((tile, 1), lambda i: (i, 0)),
        ],
        out_specs=[pl.BlockSpec((tile, w), lambda i: (i, 0)) for w in [hidden] + grads + [1]],
        out_shape=[jax.ShapeDtypeStruct((rows, w), bf16) for w in [hidden] + grads]
        + [jax.ShapeDtypeStruct((rows, 1), f32)],
        compiler_params=pltpu.CompilerParams(vmem_limit_bytes=52 * 1024 * 1024),
        cost_estimate=pl.CostEstimate(
            flops=6 * rows * D * hidden,
            bytes_accessed=2 * (2 * rows * D + 3 * hidden * D + 3 * rows * hidden),
            transcendentals=rows * hidden,
        ),
    )(x, u, w_gate, w_gate if joined else w_lift, w_down, scale)


def window(blocks, first, count, axis):
    size = blocks[0].shape[axis]
    return lax.dynamic_slice_in_dim(
        jnp.concatenate(blocks, axis=axis), first * size, count * size, axis
    )


def gather_seq(value):
    seq, place = lax.axis_size("seq"), lax.axis_index("seq")
    if seq != 4:
        return lax.all_gather(value, "seq", axis=0, tiled=True)
    lower, higher, up, down = [], [], value, value
    for hop in range(seq - 1):
        up = lax.ppermute(up, "seq", [(i, i + 1) for i in range(hop, seq - 1)])
        down = lax.ppermute(down, "seq", [(i + 1, i) for i in range(seq - 1 - hop)])
        lower.insert(0, up)
        higher.append(down)
    return window(lower + [value] + higher, seq - 1 - place, seq, 0)


def together(*values):
    return lax.optimization_barrier(values)


def exchange_seq(value, axis_out, axis_in):
    seq, place = lax.axis_size("seq"), lax.axis_index("seq")
    if seq != 4:
        return lax.all_to_all(value, "seq", axis_out, axis_in, tiled=True)
    size = value.shape[axis_out] // seq
    came = []
    for shift in range(seq):
        block = lax.dynamic_slice_in_dim(value, lax.rem(place + shift, seq) * size, size, axis_out)
        if shift:
            block = lax.ppermute(block, "seq", [(i, (i + shift) % seq) for i in range(seq)])
        came.append(block)
    order = [came[shift % seq] for shift in range(seq - 1, -seq, -1)]
    return window(order, seq - 1 - place, seq, axis_in)


def swap(value):
    return lax.all_to_all(value, "fsdp", 0, 0, tiled=True)


def sum_fsdp(value):
    return lax.psum_scatter(value, "fsdp", scatter_dimension=0, tiled=True)


def on_device(
    tokens,
    segments,
    expert_ids,
    expert_gates,
    attn_gain,
    qkv_weight,
    qkv_bias,
    out_weight,
    ffn_gain,
    shared_gate_up,
    shared_down,
    shared_gate,
    expert_gate_up,
    expert_down,
    cotangent,
):
    fsdp, seq = lax.axis_size("fsdp"), lax.axis_size("seq")
    me, place = lax.axis_index("fsdp"), lax.axis_index("seq")
    row_count, length = tokens.shape[1], segments.shape[1]
    heads = HEADS // seq
    group = heads * HEAD_DIM
    copies = fsdp // EXPERTS
    width = D // fsdp
    hidden_own = FF_EXPERT // copies
    piece = hidden_own // fsdp
    factor = 1.0 / math.sqrt(HEAD_DIM)
    capacity = length * TOP // EXPERTS

    names = jnp.arange(EXPERTS, dtype=jnp.int32)
    matches = expert_ids[0][None, :, :] == names[:, None, None]
    gates = jnp.sum(jnp.where(matches, expert_gates[0][None], 0.0), axis=-1)
    gates = jnp.where(jnp.any(matches, axis=-1), gates, -1.0)
    chosen = (gates >= 0.0).astype(jnp.int32)
    tallies = lax.all_gather(jnp.sum(chosen, axis=1), "seq")
    before = jnp.arange(seq, dtype=jnp.int32)[:, None] < place
    offsets = jnp.sum(jnp.where(before, tallies, 0), axis=0)
    earlier = offsets[:, None] + jnp.cumsum(chosen, axis=1) - chosen
    gates = jnp.where((chosen > 0) & (earlier < capacity), gates, 0.0)
    vectors = jnp.concatenate([attn_gain, ffn_gain, shared_gate, qkv_bias]).astype(f32)
    small = lax.all_gather(jnp.concatenate([gates.reshape(-1), vectors]), "fsdp", axis=0)
    gates = small[:, : EXPERTS * row_count].reshape(fsdp, EXPERTS, row_count)
    share = lax.dynamic_index_in_dim(gates, me // copies, 1, keepdims=False).reshape(-1, 1)
    vectors = small[:, EXPERTS * row_count :]
    gain_one = vectors[:, :width].reshape(D)
    gain_two = vectors[:, width : 2 * width].reshape(D)
    gate_vector = vectors[:, 2 * width : 3 * width].reshape(D).astype(bf16)
    bias = vectors[:, 3 * width : 6 * width].reshape(3, seq, group)
    bias = lax.dynamic_index_in_dim(bias, place, 1, keepdims=False).reshape(-1)

    all_tokens = gather_seq(tokens[0])
    own = [
        lax.dynamic_slice_in_dim(qkv_weight, part * D + place * group, group, 1)
        for part in range(3)
    ]
    extra = -(-6 * width // (3 * group) // 16) * 16
    weight_qkv = lax.all_gather(
        after(jnp.concatenate(own, axis=1), small), "fsdp", axis=0, tiled=True
    )
    weight_out = lax.all_gather(out_weight, "fsdp", axis=0, tiled=True)
    upstream_all = lax.all_gather(cotangent[0], "fsdp", axis=0, tiled=True)

    up_sent = expert_gate_up.reshape(EXPERTS, width, 2, fsdp, copies, piece)
    up_sent = up_sent.transpose(0, 4, 1, 2, 3, 5).reshape(fsdp, width, 2 * hidden_own)
    down_sent = expert_down.reshape(fsdp, piece, D)
    if seq == 4:
        half = lax.rem(place, 2)
        fetched = swap(lax.dynamic_slice_in_dim(up_sent, half * (width // 2), width // 2, 1))
        given = lax.ppermute(fetched, "seq", [(0, 1), (1, 0), (2, 3), (3, 2)])
    else:
        fetched = given = swap(up_sent)

    x_all = all_tokens.astype(f32)
    normed_unit = x_all * rms_scale(x_all)
    normed = (normed_unit * gain_one).astype(bf16)
    cosine, sine = rope_tables(jnp.arange(length, dtype=jnp.int32))
    normed = after(normed, weight_qkv)
    joined = dot(normed, weight_qkv, ((1,), (0,))) + bias
    split = joined.reshape(length, 3, heads, HEAD_DIM)
    queries = rotate(split[:, 0], cosine, sine).astype(bf16)
    keys = rotate(split[:, 1], cosine, sine).astype(bf16)
    values = split[:, 2].astype(bf16)
    documents = segments[0]
    mixed, logs = attend(queries, keys, values, documents, factor)
    mixed_rows = exchange_seq(mixed.reshape(length, group), 0, 1)
    inputs = tokens[0].astype(f32)
    hidden = inputs + dot(mixed_rows, weight_out, ((1,), (0,)))
    scale_two = rms_scale(hidden)
    second = (hidden * scale_two * gain_two).astype(bf16)
    second_all = lax.all_gather(after(second, fetched, upstream_all), "fsdp", axis=0, tiled=True)

    weight_down = swap(after(down_sent, second_all)).reshape(hidden_own, D)
    by_kernel = seq == 4 and fsdp == 8
    s_gate, s_lift = shared_gate_up[:, 0], shared_gate_up[:, 1]
    opening_all = jax.nn.sigmoid(dot(second_all, gate_vector, ((1,), (0,))))[:, None]
    raw_s = dot(after(upstream_all, second), shared_down, ((1,), (1,)))
    inner_s, ga_s, gl_s, reach = middle(
        second_all, raw_s, s_gate, s_lift, shared_down, opening_all
    )
    grad_s_down = dot(upstream_all, inner_s, ((0,), (0,)), bf16)
    grad_s_gate = dot(second_all, ga_s, ((0,), (0,)), bf16)
    grad_s_lift = dot(second_all, gl_s, ((0,), (0,)), bf16)

    given, fetched = after((given, fetched), grad_s_down, grad_s_gate, grad_s_lift)
    if by_kernel:
        *sum_s, inner_e, grads_e, grad_second_all, out_all = feed_forward(
            (grad_s_down, grad_s_gate, grad_s_lift),
            (second_all, upstream_all, ga_s, gl_s, inner_s),
            (
                fetched.reshape(D // 2, -1),
                given.reshape(D // 2, -1),
                weight_down,
                s_gate,
                s_lift,
                shared_down,
            ),
            share,
            2,
        )
        grad_second = sum_fsdp(grad_second_all)
        grad_e_down = dot(inner_e, upstream_all, ((0,), (0,)), bf16)
        grad_e_up = dot(second_all, after(grads_e, grad_e_down), ((0,), (0,)), bf16)
        reach = jnp.sum(swap(after(reach.reshape(fsdp, row_count), inner_e)), axis=0)
        out_all = after(out_all, grad_e_up)
    else:
        weight_up = given
        if seq == 4:
            weight_up = jnp.concatenate(
                [jnp.where(half == 0, fetched, given), jnp.where(half == 0, given, fetched)],
                axis=1,
            )
        weight_up = weight_up.reshape(D, 2 * hidden_own)
        held = after(second_all, grad_s_down, grad_s_gate, grad_s_lift)
        if hidden_own % 128 == 0:
            inner_e, grads_e, _ = middle(held, upstream_all, weight_up, None, weight_down, share)
        else:
            inner_e, ga_e, gl_e, _ = middle(
                held,
                upstream_all,
                weight_up[:, :hidden_own],
                weight_up[:, hidden_own:],
                weight_down,
                share,
            )
            grads_e = jnp.concatenate([ga_e, gl_e], axis=1)
        part = dot(inner_e, upstream_all, ((0,), (0,)), bf16)
        grad_e_down = part
        reach = jnp.sum(swap(after(reach.reshape(fsdp, row_count), part)), axis=0)

        grads_e, ga_s, gl_s = after((grads_e, ga_s, gl_s), part)
        grad_second_all = (
            dot(ga_s, s_gate, ((1,), (1,)))
            + dot(gl_s, s_lift, ((1,), (1,)))
            + dot(grads_e, weight_up, ((1,), (1,)))
        ).astype(bf16)
        grad_second = sum_fsdp(grad_second_all)

        grad_e_up = dot(second_all, after(grads_e, grad_second_all), ((0,), (0,)), bf16)

        inner_s, inner_e = after((inner_s, inner_e), grad_e_up)
        out_all = (
            dot(inner_s, shared_down, ((1,), (0,))) + dot(inner_e, weight_down, ((1,), (0,)))
        ).astype(bf16)
        sum_s = lax.psum((grad_s_down, grad_s_gate, grad_s_lift), "seq")

    grad_second, reach = after((grad_second, reach), out_all)
    upstream = cotangent[0].astype(f32)
    opening = jax.nn.sigmoid(dot(second, gate_vector, ((1,), (0,))))
    grad_logit = reach * opening * (1.0 - opening)
    grad_second = grad_second.astype(f32) + grad_logit[:, None] * gate_vector.astype(f32)[None, :]
    grad_gate_vector = jnp.sum(grad_logit[:, None] * second.astype(f32), axis=0)
    grad_hidden = upstream + norm_back(hidden, scale_two, gain_two, grad_second)
    grad_gain_two = jnp.sum(grad_second * hidden * scale_two, axis=0)
    grad_projected = grad_hidden.astype(bf16)
    grad_mixture = dot(grad_projected, weight_out, ((1,), (1,)), bf16)
    grad_heads = exchange_seq(grad_mixture, 1, 0)
    grad_out = dot(mixed_rows, after(grad_projected, grad_mixture), ((0,), (0,)), bf16)

    grad_heads = after(grad_heads, grad_out)
    grad_queries, grad_keys, grad_values = attend_back(
        queries,
        keys,
        values,
        documents,
        factor,
        logs,
        grad_heads.reshape(length, heads, HEAD_DIM),
    )
    grad_joined = jnp.stack(
        [
            rotate_back(grad_queries.astype(bf16).astype(f32), cosine, sine),
            rotate_back(grad_keys.astype(bf16).astype(f32), cosine, sine),
            grad_values,
        ],
        axis=1,
    )
    grad_joined = grad_joined.reshape(length, 3 * group).astype(bf16)
    grad_normed_all = dot(grad_joined, weight_qkv, ((1,), (1,)))
    grad_gain_one = jnp.sum(grad_normed_all * normed_unit, axis=0)

    grad_qkv = dot(normed, grad_joined, ((0,), (0,)), bf16).reshape(fsdp, width, 3 * group)
    grad_bias = jnp.sum(grad_joined.astype(f32), axis=0).reshape(3, 1, group)
    own_heads = (jnp.arange(seq, dtype=jnp.int32) == place).astype(f32)
    grad_bias = (grad_bias * own_heads[None, :, None]).reshape(fsdp, 3 * width)
    rows = jnp.concatenate(
        [
            grad_gain_one.reshape(fsdp, width),
            grad_gain_two.reshape(fsdp, width),
            grad_gate_vector.reshape(fsdp, width),
            grad_bias,
        ],
        axis=1,
    ).astype(bf16)
    rows = jnp.pad(rows, ((0, 0), (0, extra * 3 * group - 6 * width)))
    rows = rows.reshape(fsdp, extra, 3 * group)
    grad_qkv = jnp.concatenate([grad_qkv, rows], axis=1)

    grad_out = sum_fsdp(grad_out)
    grad_normed_all = grad_normed_all.astype(bf16)
    grad_e_up, grad_out, grad_qkv, grad_normed_all, out_all = together(
        grad_e_up, grad_out, grad_qkv, grad_normed_all, out_all
    )
    grad_qkv = lax.psum_scatter(
        grad_qkv.reshape(-1, 3 * group), "fsdp", scatter_dimension=0, tiled=True
    )
    grad_normed = lax.psum_scatter(grad_normed_all, "seq", scatter_dimension=0, tiled=True)
    out_part = lax.psum_scatter(out_all, "fsdp", scatter_dimension=0, tiled=True)
    if by_kernel:
        sum_e_up, sum_e_down, sum_out = combine(
            [(grad_e_up, True, 64), (grad_e_down, True, 176), (grad_out, False, 64)], 1
        )
        sum_e_up = sum_e_up.reshape(EXPERTS, width, 2 * FF_EXPERT)
        sum_e_down = sum_e_down.reshape(EXPERTS, piece, D)
    else:
        sum_e_up = swap(grad_e_up.reshape(fsdp, width, 2 * hidden_own))
        sum_e_down = swap(grad_e_down.reshape(fsdp, piece, D))
        sum_e_up, sum_e_down, sum_out = lax.psum((sum_e_up, sum_e_down, grad_out), "seq")
        sum_e_down = sum_e_down.reshape(EXPERTS, copies * piece, D)
        sum_e_up = sum_e_up.reshape(EXPERTS, copies, width, 2, fsdp, piece)
        sum_e_up = sum_e_up.transpose(0, 2, 3, 4, 1, 5).reshape(EXPERTS, width, 2 * FF_EXPERT)
    output = (hidden + out_part.astype(f32)).astype(bf16)
    grad_normed = grad_normed.astype(f32)
    grad_qkv = lax.all_gather(after(grad_qkv, sum_out), "seq", axis=0)
    rows = jnp.sum(grad_qkv[:, width:].astype(f32), axis=0).reshape(-1)
    grad_qkv = jnp.concatenate(
        [
            grad_qkv[owner, :width, part * group : (part + 1) * group]
            for part in range(3)
            for owner in range(seq)
        ],
        axis=1,
    ).astype(f32)
    input_grad = (grad_hidden + norm_back(inputs, rms_scale(inputs), gain_one, grad_normed)).astype(
        bf16
    )
    sum_s_up = jnp.stack([sum_s[1], sum_s[2]], axis=1)

    return (
        output[None],
        input_grad[None],
        rows[:width],
        grad_qkv,
        rows[3 * width : 6 * width],
        sum_out.astype(f32),
        rows[width : 2 * width],
        sum_s_up.astype(f32),
        sum_s[0].T.astype(f32),
        rows[2 * width : 3 * width],
        sum_e_up.astype(f32),
        sum_e_down.astype(f32),
    )


def solution(mesh):
    return jax.shard_map(
        on_device,
        mesh=mesh,
        in_specs=(
            P("fsdp", "seq", None),
            P("fsdp", None),
            P("fsdp", "seq", None),
            P("fsdp", "seq", None),
            P("fsdp"),
            P("fsdp", None),
            P("fsdp"),
            P("fsdp", None),
            P("fsdp"),
            P(None, None, "fsdp"),
            P("fsdp", None),
            P("fsdp"),
            P(None, "fsdp", None),
            P(None, "fsdp", None),
            P("fsdp", "seq", None),
        ),
        out_specs=(
            P("fsdp", "seq", None),
            P("fsdp", "seq", None),
            P("fsdp"),
            P("fsdp", None),
            P("fsdp"),
            P("fsdp", None),
            P("fsdp"),
            P(None, None, "fsdp"),
            P("fsdp", None),
            P("fsdp"),
            P(None, "fsdp", None),
            P(None, "fsdp", None),
        ),
        check_vma=False,
    )
```

```python
import functools
import math

import jax
import jax.numpy as jnp
from jax import lax
from jax.experimental import pallas as pl
from jax.experimental.pallas import tpu as pltpu
from jax.sharding import PartitionSpec as P

D = 2048
HEADS = 16
HEAD_DIM = 128
FF_EXPERT = 1408
TOP = 4
EXPERTS = 8
QBLOCK = 256
DOC_MOST = 512

EPSILON = 1e-06
THETA = 1000000.0

bf16 = jnp.bfloat16
f32 = jnp.float32


def dot(a, b, contract, kind=f32):
    return lax.dot_general(a, b, (contract, ((), ())), preferred_element_type=f32).astype(kind)


def rms_scale(values):
    return lax.rsqrt(jnp.mean(values * values, axis=-1, keepdims=True) + EPSILON)


def norm_back(values, scale, gain, grad):
    scaled = grad * gain
    centre = jnp.mean(scaled * values, axis=-1, keepdims=True)
    return scale * (scaled - values * (scale * scale) * centre)


def rope_tables(positions):
    steps_half = jnp.arange(HEAD_DIM // 2, dtype=jnp.int32).astype(f32)
    frequency = jnp.exp(steps_half * (-2.0 * math.log(THETA) / HEAD_DIM))
    angles = positions.astype(f32)[:, None] * frequency[None, :]
    angles = jnp.concatenate([angles, angles], axis=-1)
    return (jnp.cos(angles), jnp.sin(angles))


def rotate(rows, cosine, sine):
    middle = rows.shape[-1] // 2
    turned = jnp.concatenate([-rows[..., middle:], rows[..., :middle]], axis=-1)
    return rows * cosine[:, None, :] + turned * sine[:, None, :]


def rotate_back(rows, cosine, sine):
    middle = rows.shape[-1] // 2
    turned = rows * sine[:, None, :]
    turned = jnp.concatenate([turned[..., middle:], -turned[..., :middle]], axis=-1)
    return rows * cosine[:, None, :] + turned


def key_start(block):
    return max(0, block * QBLOCK - DOC_MOST)


def block_scores(block, queries, keys, documents, factor):
    first, start = block * QBLOCK, key_start(block)
    stop = first + QBLOCK
    scores = (
        jnp.einsum(
            "qhd,khd->hqk", queries[first:stop], keys[start:stop], preferred_element_type=f32
        )
        * factor
    )
    rows = first + jnp.arange(QBLOCK, dtype=jnp.int32)
    columns = start + jnp.arange(stop - start, dtype=jnp.int32)
    allowed = (rows[:, None] >= columns[None, :]) & (
        documents[first:stop, None] == documents[None, start:stop]
    )
    return jnp.where(allowed[None], scores, -1e30)


def attend(queries, keys, values, documents, factor):
    mixed, logs = [], []
    for block in range(queries.shape[0] // QBLOCK):
        start, stop = key_start(block), (block + 1) * QBLOCK
        scores = block_scores(block, queries, keys, documents, factor)
        top = jnp.max(scores, axis=-1, keepdims=True)
        weights = jnp.exp(scores - top)
        totals = jnp.sum(weights, axis=-1, keepdims=True)
        probability = (weights / totals).astype(bf16)
        mixed.append(
            jnp.einsum(
                "hqk,khd->qhd", probability, values[start:stop], preferred_element_type=f32
            ).astype(bf16)
        )
        logs.append(top + jnp.log(totals))
    return jnp.concatenate(mixed, axis=0), logs


def attend_back(queries, keys, values, documents, factor, logs, grads):
    length = queries.shape[0]
    grad_queries = []
    grad_keys = jnp.zeros(keys.shape, f32)
    grad_values = jnp.zeros(values.shape, f32)
    for block in range(length // QBLOCK):
        start, stop = key_start(block), (block + 1) * QBLOCK
        scores = block_scores(block, queries, keys, documents, factor)
        probability = jnp.exp(scores - logs[block])
        grad_block = grads[block * QBLOCK : stop]
        query_block = queries[block * QBLOCK : stop]
        grad_values = grad_values.at[start:stop].add(
            jnp.einsum(
                "hqk,qhd->khd", probability.astype(bf16), grad_block, preferred_element_type=f32
            )
        )
        grad_probability = jnp.einsum(
            "qhd,khd->hqk", grad_block, values[start:stop], preferred_element_type=f32
        )
        centre = jnp.sum(grad_probability * probability, axis=-1, keepdims=True)
        grad_scores = (probability * (grad_probability - centre)).astype(bf16)
        grad_queries.append(
            jnp.einsum("hqk,khd->qhd", grad_scores, keys[start:stop], preferred_element_type=f32)
            * factor
        )
        grad_keys = grad_keys.at[start:stop].add(
            jnp.einsum("hqk,qhd->khd", grad_scores, query_block, preferred_element_type=f32)
            * factor
        )
    return jnp.concatenate(grad_queries, axis=0), grad_keys, grad_values


def after(value, *earlier):
    return lax.optimization_barrier((value, earlier))[0]


def line_neighbours(place):
    middle = lax.rem(place + 1, 4) // 2
    low = 1 - place // 2
    partner = low * (1 - place) + (1 - low) * (5 - place)
    across = low * 2 + (1 - low) * 1
    return middle, partner, across


def flip(index, bits):
    result, step = 0, 1
    while step < 8:
        bit = lax.rem(index // step, 2)
        result = result + step * (1 - bit if bits & step else bit)
        step *= 2
    return result


SLOTS = 4
ORDER = (0, 1, 2, 4, 3, 5, 6, 7)
LEAVE = {2: ((2, 4), (3, 5)), 4: ((3, 5), (6, 7))}


def combine_kernel(plan, *refs):
    count = len(plan)
    sources, refs = refs[:count], refs[count:]
    results, refs = refs[:count], refs[count:]
    lands, refs = refs[:count], refs[count:]
    buffers, refs = refs[: 5 * count], refs[5 * count :]
    (land_send, land_recv, g_sem, a_send, a_recv, b_send, b_recv, c_send, c_recv) = refs[:9]
    out_sem, a_free, b_free = refs[9:]
    me, place = lax.axis_index("fsdp"), lax.axis_index("seq")
    middle, partner, across = line_neighbours(place)
    peers = [flip(me, k) for k in range(8)]

    barrier = pltpu.get_barrier_semaphore()
    swapping = any(swapped for swapped, _, _, _ in plan)
    if swapping:
        for k in range(1, 8):
            pl.semaphore_signal(
                barrier, device_id={"fsdp": peers[k]}, device_id_type=pl.DeviceIdType.MESH
            )
    pl.semaphore_signal(
        barrier, device_id={"seq": partner}, device_id_type=pl.DeviceIdType.MESH
    )

    @pl.when(middle == 1)
    def _():
        pl.semaphore_signal(
            barrier, device_id={"seq": across}, device_id_type=pl.DeviceIdType.MESH
        )

    pl.semaphore_wait(barrier, 1 + middle + (7 if swapping else 0))

    arrivals = {}
    for index, (swapped, rows, blocks, _) in enumerate(plan):
        if not swapped:
            continue
        here = pl.ds(pl.multiple_of(me * rows, 16), rows)
        for k in range(1, 8):
            there = pl.ds(pl.multiple_of(peers[k] * rows, 16), rows)
            copy = pltpu.make_async_remote_copy(
                src_ref=sources[index].at[there],
                dst_ref=lands[index].at[here],
                send_sem=land_send.at[index, k],
                recv_sem=land_recv.at[index, k],
                device_id={"fsdp": peers[k]},
                device_id_type=pl.DeviceIdType.MESH,
            )
            arrivals[index, k] = copy
            if k in (1, 2, 4):
                copy.start()

    chunks, starts = [], []
    for index, (swapped, rows, blocks, size) in enumerate(plan):
        starts.append(len(chunks))
        for block in range(blocks):
            base = (peers[ORDER[block]] if swapped else block) * rows
            for first in range(0, rows, size):
                chunks.append((index, block if first == 0 else None, base + first, size))
    total = len(chunks)

    def landed(c):
        index, block, _, _ = chunks[c]
        if not plan[index][0] or block is None:
            return
        if block > 0:
            arrivals[index, ORDER[block]].wait_recv()
        if index > 0:
            for k in (3, 5, 6, 7) if block == 0 else ():
                arrivals[index, k].start()
        elif block in LEAVE:
            left, leaving = LEAVE[block]
            for k in left:
                arrivals[index, k].wait_send()
            for k in leaving:
                arrivals[index, k].start()

    def place_of(c, ref_list):
        index, _, start, size = chunks[c]
        if isinstance(start, int):
            return ref_list[index].at[pl.ds(start, size)]
        return ref_list[index].at[pl.ds(pl.multiple_of(start, 16), size)]

    def held(c, which):
        return buffers[5 * chunks[c][0] + which].at[c % SLOTS]

    def given(c):
        index, _, _, size = chunks[c]
        away = plan[index][0] and size * (c - starts[index]) >= plan[index][1]
        return place_of(c, lands if away else sources)

    def inward(c):
        return pltpu.make_async_remote_copy(
            src_ref=given(c),
            dst_ref=held(c, 1),
            send_sem=a_send.at[c % SLOTS],
            recv_sem=a_recv.at[c % SLOTS],
            device_id={"seq": partner},
            device_id_type=pl.DeviceIdType.MESH,
        )

    def crossing(c):
        return pltpu.make_async_remote_copy(
            src_ref=held(c, 2),
            dst_ref=held(c, 3),
            send_sem=b_send.at[c % SLOTS],
            recv_sem=b_recv.at[c % SLOTS],
            device_id={"seq": across},
            device_id_type=pl.DeviceIdType.MESH,
        )

    def outward(c):
        return pltpu.make_async_remote_copy(
            src_ref=held(c, 4),
            dst_ref=place_of(c, results),
            send_sem=c_send.at[c % SLOTS],
            recv_sem=c_recv.at[c],
            device_id={"seq": partner},
            device_id_type=pl.DeviceIdType.MESH,
        )

    def fetch(c):
        return pltpu.make_async_copy(given(c), held(c, 0), g_sem.at[c % SLOTS])

    def keep(c):
        return pltpu.make_async_copy(held(c, 4), place_of(c, results), out_sem.at[c % SLOTS])

    @pl.when(middle == 0)
    def _():
        for c in range(total):
            landed(c)
            if c >= SLOTS:
                inward(c - SLOTS).wait_send()
                pl.semaphore_wait(a_free, 1)
            inward(c).start()
        for c in range(max(0, total - SLOTS), total):
            inward(c).wait_send()
        for c in range(total):
            outward(c).wait_recv()

    @pl.when(middle == 1)
    def _():
        for c in range(min(SLOTS, total)):
            landed(c)
            fetch(c).start()
        for i in range(total + 1):
            c = i
            if c < total:
                fetch(c).wait()
                inward(c).wait_recv()
                if c >= SLOTS:
                    crossing(c - SLOTS).wait_send()
                held(c, 2)[...] = (
                    held(c, 0)[...].astype(f32) + held(c, 1)[...].astype(f32)
                ).astype(bf16)
                if c + SLOTS < total:
                    pl.semaphore_signal(
                        a_free, device_id={"seq": partner}, device_id_type=pl.DeviceIdType.MESH
                    )
                if c >= SLOTS:
                    pl.semaphore_wait(b_free, 1)
                crossing(c).start()
                if c + SLOTS < total:
                    landed(c + SLOTS)
                    fetch(c + SLOTS).start()
            c = i - 1
            if c >= 0:
                crossing(c).wait_recv()
                if c >= SLOTS:
                    keep(c - SLOTS).wait()
                    outward(c - SLOTS).wait_send()
                held(c, 4)[...] = (
                    held(c, 2)[...].astype(f32) + held(c, 3)[...].astype(f32)
                ).astype(bf16)
                if c + SLOTS < total:
                    pl.semaphore_signal(
                        b_free, device_id={"seq": across}, device_id_type=pl.DeviceIdType.MESH
                    )
                outward(c).start()
                keep(c).start()
        for c in range(max(0, total - SLOTS), total):
            crossing(c).wait_send()
            keep(c).wait()
            outward(c).wait_send()

    for (index, k), copy in arrivals.items():
        if index > 0 or k in (1, 6, 7):
            copy.wait_send()


def combine(arrays, number):
    plan = []
    for value, swapped, size in arrays:
        rows = value.shape[0] // 8 if swapped else value.shape[0]
        plan.append((swapped, rows, 8 if swapped else 1, size))
    count = len(plan)
    total = sum(rows // size * blocks for _, rows, blocks, size in plan)
    shapes = [jax.ShapeDtypeStruct(value.shape, bf16) for value, _, _ in arrays]
    lands = [
        jax.ShapeDtypeStruct(value.shape if swapped else (16, 128), bf16)
        for value, swapped, _ in arrays
    ]
    buffers = [
        pltpu.VMEM((SLOTS, size, value.shape[1]), bf16)
        for value, _, size in arrays
        for _ in range(5)
    ]
    dma = pltpu.SemaphoreType.DMA
    moved = sum(value.size for value, _, _ in arrays)
    anywhere = pl.BlockSpec(memory_space=pl.ANY)
    return pl.pallas_call(
        functools.partial(combine_kernel, tuple(plan)),
        out_shape=shapes + lands,
        in_specs=[anywhere] * count,
        out_specs=[anywhere] * (2 * count),
        scratch_shapes=buffers
        + [
            dma((count, 8)),
            dma((count, 8)),
            dma((SLOTS,)),
            dma((SLOTS,)),
            dma((SLOTS,)),
            dma((SLOTS,)),
            dma((SLOTS,)),
            dma((SLOTS,)),
            dma((total,)),
            dma((SLOTS,)),
            pltpu.SemaphoreType.REGULAR,
            pltpu.SemaphoreType.REGULAR,
        ],
        compiler_params=pltpu.CompilerParams(
            collective_id=number, has_side_effects=True, vmem_limit_bytes=48 * 1024 * 1024
        ),
        cost_estimate=pl.CostEstimate(
            flops=2 * moved, bytes_accessed=200 * moved, transcendentals=0
        ),
        name="combine_%d" % number,
    )(*[value for value, _, _ in arrays])[:count]


HOST_BLOCKS = 8
SUM_BLOCKS = 16


def feed_forward_kernel(*refs):
    sources, refs = refs[:3], refs[3:]
    tiles_in, refs = refs[:5], refs[5:]
    near, far, *weights = refs[:6]
    share, refs = refs[6], refs[7:]
    results, refs = refs[:3], refs[3:]
    tiles_out, refs = refs[:4], refs[4:]
    zg, za, zs, zb, zt = refs[:5]
    refs = refs[5:]
    held, refs = refs[:5], refs[5:]
    v_up, v_down, v_sg, v_sl, v_sd = held
    loaded, refs = refs[:5], refs[5:]
    v_x, v_u, v_ga, v_gl, v_in = loaded
    stored, refs = refs[:4], refs[4:]
    t_in, t_grads, t_second, t_out = stored
    (w_sem, l_sem, s_sem, g_sem, a_send, a_recv, b_send, b_recv, c_send, c_recv) = refs[:10]
    out_sem, a_free, b_free = refs[10:]
    place = lax.axis_index("seq")
    middle, partner, across = line_neighbours(place)
    tile = v_x.shape[1]
    hidden = v_down.shape[0]
    last = SUM_BLOCKS - 1
    pace = SUM_BLOCKS // HOST_BLOCKS
    block = za.shape[2]

    half = lax.rem(place, 2)
    cut_rows = v_up.shape[0] // 16
    copies = [
        pltpu.make_async_copy(weights[index], held[index + 1], w_sem.at[index])
        for index in range(4)
    ]
    for owner in range(8):
        source = pl.ds(owner * cut_rows, cut_rows)
        for which, (ref, side) in enumerate(((near, half), (far, 1 - half))):
            first = pl.multiple_of((2 * owner + side) * cut_rows, cut_rows)
            copies.append(
                pltpu.make_async_copy(
                    ref.at[source],
                    v_up.at[pl.ds(first, cut_rows)],
                    w_sem.at[4 + 2 * owner + which],
                )
            )
    for copy in copies:
        copy.start()

    barrier = pltpu.get_barrier_semaphore()
    pl.semaphore_signal(
        barrier, device_id={"seq": partner}, device_id_type=pl.DeviceIdType.MESH
    )

    @pl.when(middle == 1)
    def _():
        pl.semaphore_signal(
            barrier, device_id={"seq": across}, device_id_type=pl.DeviceIdType.MESH
        )

    pl.semaphore_wait(barrier, 1 + middle)

    def rows(o, size=block):
        return pl.ds(o * size if isinstance(o, int) else pl.multiple_of(o * size, size), size)

    def slot(o):
        return o % 2 if isinstance(o, int) else lax.rem(o, 2)

    def remote(source, target, sent, received, where):
        return pltpu.make_async_remote_copy(
            src_ref=source,
            dst_ref=target,
            send_sem=sent,
            recv_sem=received,
            device_id={"seq": where},
            device_id_type=pl.DeviceIdType.MESH,
        )

    def inward(o, a):
        i = slot(o)
        return remote(
            sources[a].at[rows(o)], za.at[i, a], a_send.at[i, a], a_recv.at[i, a], partner
        )

    def crossing(o, a):
        i = slot(o)
        return remote(zs.at[i, a], zb.at[i, a], b_send.at[i, a], b_recv.at[i, a], across)

    def outward(o, a):
        i = slot(o)
        return remote(
            zt.at[i, a], results[a].at[rows(o)], c_send.at[i, a], c_recv.at[o, a], partner
        )

    def fetch(o, a):
        i = slot(o)
        return pltpu.make_async_copy(sources[a].at[rows(o)], zg.at[i, a], g_sem.at[i, a])

    def keep(o, a):
        i = slot(o)
        return pltpu.make_async_copy(zt.at[i, a], results[a].at[rows(o)], out_sem.at[i, a])

    def load(o, index):
        i = slot(o)
        return pltpu.make_async_copy(
            tiles_in[index].at[rows(o, tile)], loaded[index].at[i], l_sem.at[i, index]
        )

    def store(o, index):
        return pltpu.make_async_copy(stored[index], tiles_out[index].at[rows(o, tile)], s_sem.at[index])

    for index in range(5):
        load(0, index).start()

    @pl.when(middle == 0)
    def _():
        for o in (0, 1):
            for a in range(3):
                inward(o, a).start()

    @pl.when(middle == 1)
    def _():
        for o in (0, 1):
            for a in range(3):
                fetch(o, a).start()

    for copy in copies:
        copy.wait()

    def add(left, right):
        return (left.astype(f32) + right.astype(f32)).astype(bf16)

    def end_step(o):
        @pl.when((o >= 1) & (o < last))
        def _():
            for a in range(3):
                inward(o - 1, a).wait_send()
                pl.semaphore_wait(a_free, 1)
                inward(o + 1, a).start()

    def middle_step(o):
        @pl.when(o <= last)
        def _():
            i = slot(o)
            for a in range(3):
                fetch(o, a).wait()
                inward(o, a).wait_recv()

                @pl.when(o >= 2)
                def _():
                    crossing(o - 2, a).wait_send()
                    pl.semaphore_wait(b_free, 1)

                zs[i, a] = add(zg[i, a], za[i, a])
                crossing(o, a).start()

                @pl.when(o + 2 <= last)
                def _():
                    pl.semaphore_signal(
                        a_free, device_id={"seq": partner}, device_id_type=pl.DeviceIdType.MESH
                    )
                    fetch(o + 2, a).start()

        @pl.when(o >= 1)
        def _():
            p = o - 1
            i = slot(p)
            for a in range(3):
                crossing(p, a).wait_recv()

                @pl.when(p >= 2)
                def _():
                    keep(p - 2, a).wait()
                    outward(p - 2, a).wait_send()

                zt[i, a] = add(zs[i, a], zb[i, a])

                @pl.when(p + 2 <= last)
                def _():
                    pl.semaphore_signal(
                        b_free, device_id={"seq": across}, device_id_type=pl.DeviceIdType.MESH
                    )

                outward(p, a).start()
                keep(p, a).start()

    def across_rows(left, right):
        return lax.dot_general(left, right, (((1,), (1,)), ((), ())), preferred_element_type=f32)

    def host(o):
        i = slot(o)
        for index in range(5):
            load(o, index).wait()

        @pl.when(o < HOST_BLOCKS - 1)
        def _():
            for index in range(5):
                load(o + 1, index).start()

        @pl.when(o >= 1)
        def _():
            for index in range(4):
                store(o - 1, index).wait()

        scale = share[rows(o, tile), :]
        cut = hidden // 256 * 128
        for first, end in ((0, cut), (cut, hidden)):
            gate = jnp.dot(v_x[i], v_up[:, first:end], preferred_element_type=f32)
            lift = jnp.dot(
                v_x[i], v_up[:, hidden + first : hidden + end], preferred_element_type=f32
            )
            grad = across_rows(v_u[i], v_down[first:end, :]) * scale
            sigma = 1.0 / (1.0 + jnp.exp(-gate))
            silu = gate * sigma
            t_in[:, first:end] = (silu * lift * scale).astype(bf16)
            t_grads[:, first:end] = (
                grad * lift * sigma * (1.0 + gate * (1.0 - sigma))
            ).astype(bf16)
            t_grads[:, hidden + first : hidden + end] = (grad * silu).astype(bf16)
        for first in range(0, D, 512):
            end = first + 512
            t_second[:, first:end] = (
                across_rows(t_grads[...], v_up[first:end, :])
                + across_rows(v_ga[i], v_sg[first:end, :])
                + across_rows(v_gl[i], v_sl[first:end, :])
            ).astype(bf16)
            t_out[:, first:end] = (
                jnp.dot(t_in[...], v_down[:, first:end], preferred_element_type=f32)
                + jnp.dot(v_in[i], v_sd[:, first:end], preferred_element_type=f32)
            ).astype(bf16)
        for index in range(4):
            store(o, index).start()

    def step(o, carry):
        @pl.when(middle == 0)
        def _():
            end_step(o)

        @pl.when(middle == 1)
        def _():
            middle_step(o)

        @pl.when((o <= last) & (lax.rem(o, pace) == 0))
        def _():
            host(o // pace)

        return carry

    lax.fori_loop(0, SUM_BLOCKS + 1, step, 0)
    for index in range(4):
        store(HOST_BLOCKS - 1, index).wait()

    @pl.when(middle == 0)
    def _():
        for a in range(3):
            for o in (last - 1, last):
                inward(o, a).wait_send()
            for o in range(SUM_BLOCKS):
                outward(o, a).wait_recv()

    @pl.when(middle == 1)
    def _():
        for a in range(3):
            for o in (last - 1, last):
                crossing(o, a).wait_send()
                keep(o, a).wait()
                outward(o, a).wait_send()


def feed_forward(sums, tiles, weights, share, number):
    rows, cut = sums[0].shape
    tile = rows // HOST_BLOCKS
    hidden = weights[2].shape[0]
    dma = pltpu.SemaphoreType.DMA
    anywhere = pl.BlockSpec(memory_space=pl.ANY)
    outs = [hidden, 2 * hidden, D, D]
    return pl.pallas_call(
        feed_forward_kernel,
        out_shape=[jax.ShapeDtypeStruct((rows, cut), bf16)] * 3
        + [jax.ShapeDtypeStruct((rows, w), bf16) for w in outs],
        in_specs=[anywhere] * 14 + [pl.BlockSpec(memory_space=pltpu.VMEM)],
        out_specs=[anywhere] * 7,
        scratch_shapes=[pltpu.VMEM((2, 3, rows // SUM_BLOCKS, cut), bf16)] * 5
        + [pltpu.VMEM((D, 2 * hidden), bf16)]
        + [pltpu.VMEM(w.shape, bf16) for w in weights[2:]]
        + [pltpu.VMEM((2, tile, t.shape[1]), bf16) for t in tiles]
        + [pltpu.VMEM((tile, w), bf16) for w in outs]
        + [
            dma((20,)),
            dma((2, 5)),
            dma((4,)),
            dma((2, 3)),
            dma((2, 3)),
            dma((2, 3)),
            dma((2, 3)),
            dma((2, 3)),
            dma((2, 3)),
            dma((SUM_BLOCKS, 3)),
            dma((2, 3)),
            pltpu.SemaphoreType.REGULAR,
            pltpu.SemaphoreType.REGULAR,
        ],
        compiler_params=pltpu.CompilerParams(
            collective_id=number, has_side_effects=True, vmem_limit_bytes=60 * 1024 * 1024
        ),
        cost_estimate=pl.CostEstimate(
            flops=2 * rows * D * (6 * hidden + 3 * cut),
            bytes_accessed=800 * 1024 * 1024,
            transcendentals=rows * hidden,
        ),
    )(*sums, *tiles, *weights, share)


def middle_kernel(joined, ahead, x, u, w_gate, w_lift, w_down, scale, inner, *outs):
    gate = jnp.dot(x[...], w_gate[...], preferred_element_type=f32)
    lift = jnp.dot(x[...], w_lift[...], preferred_element_type=f32)
    if ahead:
        raw = u[...]
    else:
        raw = lax.dot_general(
            u[...], w_down[...], (((1,), (1,)), ((), ())), preferred_element_type=f32
        )
    sigma = 1.0 / (1.0 + jnp.exp(-gate))
    silu = gate * sigma
    product = silu * lift
    outs[-1][...] = jnp.sum(product * raw, axis=1, keepdims=True)
    inner[...] = (product * scale[...]).astype(bf16)
    grad = raw * scale[...]
    grad_gate = (grad * lift * sigma * (1.0 + gate * (1.0 - sigma))).astype(bf16)
    grad_lift = (grad * silu).astype(bf16)
    if joined:
        width = grad_gate.shape[1]
        outs[0][:, :width] = grad_gate
        outs[0][:, width:] = grad_lift
    else:
        outs[0][...] = grad_gate
        outs[1][...] = grad_lift


def middle(x, u, w_gate, w_lift, w_down, scale):
    joined = w_lift is None
    rows, hidden = x.shape[0], w_down.shape[0]
    ahead = u.shape[1] == hidden
    tile = 256
    whole = dict(pipeline_mode=pl.Buffered(1))
    grads = [hidden * 2] if joined else [hidden, hidden]
    return pl.pallas_call(
        functools.partial(middle_kernel, joined, ahead),
        grid=(rows // tile,),
        in_specs=[
            pl.BlockSpec((tile, D), lambda i: (i, 0)),
            pl.BlockSpec((tile, u.shape[1]), lambda i: (i, 0)),
            pl.BlockSpec((D, hidden), lambda i: (0, 0), **whole),
            pl.BlockSpec((D, hidden), lambda i: (0, 1 if joined else 0), **whole),
            pl.BlockSpec((16 if ahead else hidden, D), lambda i: (0, 0), **whole),
            pl.BlockSpec((tile, 1), lambda i: (i, 0)),
        ],
        out_specs=[pl.BlockSpec((tile, w), lambda i: (i, 0)) for w in [hidden] + grads + [1]],
        out_shape=[jax.ShapeDtypeStruct((rows, w), bf16) for w in [hidden] + grads]
        + [jax.ShapeDtypeStruct((rows, 1), f32)],
        compiler_params=pltpu.CompilerParams(vmem_limit_bytes=52 * 1024 * 1024),
        cost_estimate=pl.CostEstimate(
            flops=6 * rows * D * hidden,
            bytes_accessed=2 * (2 * rows * D + 3 * hidden * D + 3 * rows * hidden),
            transcendentals=rows * hidden,
        ),
    )(x, u, w_gate, w_gate if joined else w_lift, w_down, scale)


def window(blocks, first, count, axis):
    size = blocks[0].shape[axis]
    return lax.dynamic_slice_in_dim(
        jnp.concatenate(blocks, axis=axis), first * size, count * size, axis
    )


def gather_seq(value):
    seq, place = lax.axis_size("seq"), lax.axis_index("seq")
    if seq != 4:
        return lax.all_gather(value, "seq", axis=0, tiled=True)
    lower, higher, up, down = [], [], value, value
    for hop in range(seq - 1):
        up = lax.ppermute(up, "seq", [(i, i + 1) for i in range(hop, seq - 1)])
        down = lax.ppermute(down, "seq", [(i + 1, i) for i in range(seq - 1 - hop)])
        lower.insert(0, up)
        higher.append(down)
    return window(lower + [value] + higher, seq - 1 - place, seq, 0)


def together(*values):
    return lax.optimization_barrier(values)


def exchange_seq(value, axis_out, axis_in):
    seq, place = lax.axis_size("seq"), lax.axis_index("seq")
    if seq != 4:
        return lax.all_to_all(value, "seq", axis_out, axis_in, tiled=True)
    size = value.shape[axis_out] // seq
    came = []
    for shift in range(seq):
        block = lax.dynamic_slice_in_dim(value, lax.rem(place + shift, seq) * size, size, axis_out)
        if shift:
            block = lax.ppermute(block, "seq", [(i, (i + shift) % seq) for i in range(seq)])
        came.append(block)
    order = [came[shift % seq] for shift in range(seq - 1, -seq, -1)]
    return window(order, seq - 1 - place, seq, axis_in)


def swap(value):
    return lax.all_to_all(value, "fsdp", 0, 0, tiled=True)


def sum_fsdp(value):
    return lax.psum_scatter(value, "fsdp", scatter_dimension=0, tiled=True)


def on_device(
    tokens,
    segments,
    expert_ids,
    expert_gates,
    attn_gain,
    qkv_weight,
    qkv_bias,
    out_weight,
    ffn_gain,
    shared_gate_up,
    shared_down,
    shared_gate,
    expert_gate_up,
    expert_down,
    cotangent,
):
    fsdp, seq = lax.axis_size("fsdp"), lax.axis_size("seq")
    me, place = lax.axis_index("fsdp"), lax.axis_index("seq")
    row_count, length = tokens.shape[1], segments.shape[1]
    heads = HEADS // seq
    group = heads * HEAD_DIM
    copies = fsdp // EXPERTS
    width = D // fsdp
    hidden_own = FF_EXPERT // copies
    piece = hidden_own // fsdp
    factor = 1.0 / math.sqrt(HEAD_DIM)
    capacity = length * TOP // EXPERTS

    names = jnp.arange(EXPERTS, dtype=jnp.int32)
    matches = expert_ids[0][None, :, :] == names[:, None, None]
    gates = jnp.sum(jnp.where(matches, expert_gates[0][None], 0.0), axis=-1)
    gates = jnp.where(jnp.any(matches, axis=-1), gates, -1.0)
    chosen = (gates >= 0.0).astype(jnp.int32)
    tallies = lax.all_gather(jnp.sum(chosen, axis=1), "seq")
    before = jnp.arange(seq, dtype=jnp.int32)[:, None] < place
    offsets = jnp.sum(jnp.where(before, tallies, 0), axis=0)
    earlier = offsets[:, None] + jnp.cumsum(chosen, axis=1) - chosen
    gates = jnp.where((chosen > 0) & (earlier < capacity), gates, 0.0)
    vectors = jnp.concatenate([attn_gain, ffn_gain, shared_gate, qkv_bias]).astype(f32)
    small = lax.all_gather(jnp.concatenate([gates.reshape(-1), vectors]), "fsdp", axis=0)
    gates = small[:, : EXPERTS * row_count].reshape(fsdp, EXPERTS, row_count)
    share = lax.dynamic_index_in_dim(gates, me // copies, 1, keepdims=False).reshape(-1, 1)
    vectors = small[:, EXPERTS * row_count :]
    gain_one = vectors[:, :width].reshape(D)
    gain_two = vectors[:, width : 2 * width].reshape(D)
    gate_vector = vectors[:, 2 * width : 3 * width].reshape(D).astype(bf16)
    bias = vectors[:, 3 * width : 6 * width].reshape(3, seq, group)
    bias = lax.dynamic_index_in_dim(bias, place, 1, keepdims=False).reshape(-1)

    all_tokens = gather_seq(tokens[0])
    own = [
        lax.dynamic_slice_in_dim(qkv_weight, part * D + place * group, group, 1)
        for part in range(3)
    ]
    extra = -(-6 * width // (3 * group) // 16) * 16
    weight_qkv = lax.all_gather(
        after(jnp.concatenate(own, axis=1), small), "fsdp", axis=0, tiled=True
    )
    weight_out = lax.all_gather(out_weight, "fsdp", axis=0, tiled=True)
    upstream_all = lax.all_gather(cotangent[0], "fsdp", axis=0, tiled=True)

    up_sent = expert_gate_up.reshape(EXPERTS, width, 2, fsdp, copies, piece)
    up_sent = up_sent.transpose(0, 4, 1, 2, 3, 5).reshape(fsdp, width, 2 * hidden_own)
    down_sent = expert_down.reshape(fsdp, piece, D)
    if seq == 4:
        half = lax.rem(place, 2)
        fetched = swap(lax.dynamic_slice_in_dim(up_sent, half * (width // 2), width // 2, 1))
        given = lax.ppermute(fetched, "seq", [(0, 1), (1, 0), (2, 3), (3, 2)])
    else:
        fetched = given = swap(up_sent)

    x_all = all_tokens.astype(f32)
    normed_unit = x_all * rms_scale(x_all)
    normed = (normed_unit * gain_one).astype(bf16)
    cosine, sine = rope_tables(jnp.arange(length, dtype=jnp.int32))
    normed = after(normed, weight_qkv)
    joined = dot(normed, weight_qkv, ((1,), (0,))) + bias
    split = joined.reshape(length, 3, heads, HEAD_DIM)
    queries = rotate(split[:, 0], cosine, sine).astype(bf16)
    keys = rotate(split[:, 1], cosine, sine).astype(bf16)
    values = split[:, 2].astype(bf16)
    documents = segments[0]
    mixed, logs = attend(queries, keys, values, documents, factor)
    mixed_rows = exchange_seq(mixed.reshape(length, group), 0, 1)
    inputs = tokens[0].astype(f32)
    hidden = inputs + dot(mixed_rows, weight_out, ((1,), (0,)))
    scale_two = rms_scale(hidden)
    second = (hidden * scale_two * gain_two).astype(bf16)
    second_all = lax.all_gather(after(second, fetched, upstream_all), "fsdp", axis=0, tiled=True)

    weight_down = swap(after(down_sent, second_all)).reshape(hidden_own, D)
    by_kernel = seq == 4 and fsdp == 8
    s_gate, s_lift = shared_gate_up[:, 0], shared_gate_up[:, 1]
    opening_all = jax.nn.sigmoid(dot(second_all, gate_vector, ((1,), (0,))))[:, None]
    raw_s = dot(after(upstream_all, second), shared_down, ((1,), (1,)))
    inner_s, ga_s, gl_s, reach = middle(
        second_all, raw_s, s_gate, s_lift, shared_down, opening_all
    )
    grad_s_down = dot(upstream_all, inner_s, ((0,), (0,)), bf16)
    grad_s_gate = dot(second_all, ga_s, ((0,), (0,)), bf16)
    grad_s_lift = dot(second_all, gl_s, ((0,), (0,)), bf16)

    given, fetched = after((given, fetched), grad_s_down, grad_s_gate, grad_s_lift)
    if by_kernel:
        *sum_s, inner_e, grads_e, grad_second_all, out_all = feed_forward(
            (grad_s_down, grad_s_gate, grad_s_lift),
            (second_all, upstream_all, ga_s, gl_s, inner_s),
            (
                fetched.reshape(D // 2, -1),
                given.reshape(D // 2, -1),
                weight_down,
                s_gate,
                s_lift,
                shared_down,
            ),
            share,
            2,
        )
        grad_second = sum_fsdp(grad_second_all)
        grad_e_down = dot(inner_e, upstream_all, ((0,), (0,)), bf16)
        grad_e_up = dot(second_all, after(grads_e, grad_e_down), ((0,), (0,)), bf16)
        reach = jnp.sum(swap(after(reach.reshape(fsdp, row_count), inner_e)), axis=0)
        out_all = after(out_all, grad_e_up)
    else:
        weight_up = given
        if seq == 4:
            weight_up = jnp.concatenate(
                [jnp.where(half == 0, fetched, given), jnp.where(half == 0, given, fetched)],
                axis=1,
            )
        weight_up = weight_up.reshape(D, 2 * hidden_own)
        held = after(second_all, grad_s_down, grad_s_gate, grad_s_lift)
        if hidden_own % 128 == 0:
            inner_e, grads_e, _ = middle(held, upstream_all, weight_up, None, weight_down, share)
        else:
            inner_e, ga_e, gl_e, _ = middle(
                held,
                upstream_all,
                weight_up[:, :hidden_own],
                weight_up[:, hidden_own:],
                weight_down,
                share,
            )
            grads_e = jnp.concatenate([ga_e, gl_e], axis=1)
        part = dot(inner_e, upstream_all, ((0,), (0,)), bf16)
        grad_e_down = part
        reach = jnp.sum(swap(after(reach.reshape(fsdp, row_count), part)), axis=0)

        grads_e, ga_s, gl_s = after((grads_e, ga_s, gl_s), part)
        grad_second_all = (
            dot(ga_s, s_gate, ((1,), (1,)))
            + dot(gl_s, s_lift, ((1,), (1,)))
            + dot(grads_e, weight_up, ((1,), (1,)))
        ).astype(bf16)
        grad_second = sum_fsdp(grad_second_all)

        grad_e_up = dot(second_all, after(grads_e, grad_second_all), ((0,), (0,)), bf16)

        inner_s, inner_e = after((inner_s, inner_e), grad_e_up)
        out_all = (
            dot(inner_s, shared_down, ((1,), (0,))) + dot(inner_e, weight_down, ((1,), (0,)))
        ).astype(bf16)
        sum_s = lax.psum((grad_s_down, grad_s_gate, grad_s_lift), "seq")

    grad_second, reach = after((grad_second, reach), out_all)
    upstream = cotangent[0].astype(f32)
    opening = jax.nn.sigmoid(dot(second, gate_vector, ((1,), (0,))))
    grad_logit = reach * opening * (1.0 - opening)
    grad_second = grad_second.astype(f32) + grad_logit[:, None] * gate_vector.astype(f32)[None, :]
    grad_gate_vector = jnp.sum(grad_logit[:, None] * second.astype(f32), axis=0)
    grad_hidden = upstream + norm_back(hidden, scale_two, gain_two, grad_second)
    grad_gain_two = jnp.sum(grad_second * hidden * scale_two, axis=0)
    grad_projected = grad_hidden.astype(bf16)
    grad_mixture = dot(grad_projected, weight_out, ((1,), (1,)), bf16)
    grad_heads = exchange_seq(grad_mixture, 1, 0)
    grad_out = dot(mixed_rows, after(grad_projected, grad_mixture), ((0,), (0,)), bf16)

    grad_heads = after(grad_heads, grad_out)
    grad_queries, grad_keys, grad_values = attend_back(
        queries,
        keys,
        values,
        documents,
        factor,
        logs,
        grad_heads.reshape(length, heads, HEAD_DIM),
    )
    grad_joined = jnp.stack(
        [
            rotate_back(grad_queries.astype(bf16).astype(f32), cosine, sine),
            rotate_back(grad_keys.astype(bf16).astype(f32), cosine, sine),
            grad_values,
        ],
        axis=1,
    )
    grad_joined = grad_joined.reshape(length, 3 * group).astype(bf16)
    grad_normed_all = dot(grad_joined, weight_qkv, ((1,), (1,)))
    grad_gain_one = jnp.sum(grad_normed_all * normed_unit, axis=0)

    grad_qkv = dot(normed, grad_joined, ((0,), (0,)), bf16).reshape(fsdp, width, 3 * group)
    grad_bias = jnp.sum(grad_joined.astype(f32), axis=0).reshape(3, 1, group)
    own_heads = (jnp.arange(seq, dtype=jnp.int32) == place).astype(f32)
    grad_bias = (grad_bias * own_heads[None, :, None]).reshape(fsdp, 3 * width)
    rows = jnp.concatenate(
        [
            grad_gain_one.reshape(fsdp, width),
            grad_gain_two.reshape(fsdp, width),
            grad_gate_vector.reshape(fsdp, width),
            grad_bias,
        ],
        axis=1,
    ).astype(bf16)
    rows = jnp.pad(rows, ((0, 0), (0, extra * 3 * group - 6 * width)))
    rows = rows.reshape(fsdp, extra, 3 * group)
    grad_qkv = jnp.concatenate([grad_qkv, rows], axis=1)

    grad_out = sum_fsdp(grad_out)
    grad_normed_all = grad_normed_all.astype(bf16)
    grad_e_up, grad_out, grad_qkv, grad_normed_all, out_all = together(
        grad_e_up, grad_out, grad_qkv, grad_normed_all, out_all
    )
    grad_qkv = lax.psum_scatter(
        grad_qkv.reshape(-1, 3 * group), "fsdp", scatter_dimension=0, tiled=True
    )
    grad_normed = lax.psum_scatter(grad_normed_all, "seq", scatter_dimension=0, tiled=True)
    out_part = lax.psum_scatter(out_all, "fsdp", scatter_dimension=0, tiled=True)
    if by_kernel:
        sum_e_up, sum_e_down, sum_out = combine(
            [(grad_e_up, True, 64), (grad_e_down, True, 176), (grad_out, False, 64)], 1
        )
        sum_e_up = sum_e_up.reshape(EXPERTS, width, 2 * FF_EXPERT)
        sum_e_down = sum_e_down.reshape(EXPERTS, piece, D)
    else:
        sum_e_up = swap(grad_e_up.reshape(fsdp, width, 2 * hidden_own))
        sum_e_down = swap(grad_e_down.reshape(fsdp, piece, D))
        sum_e_up, sum_e_down, sum_out = lax.psum((sum_e_up, sum_e_down, grad_out), "seq")
        sum_e_down = sum_e_down.reshape(EXPERTS, copies * piece, D)
        sum_e_up = sum_e_up.reshape(EXPERTS, copies, width, 2, fsdp, piece)
        sum_e_up = sum_e_up.transpose(0, 2, 3, 4, 1, 5).reshape(EXPERTS, width, 2 * FF_EXPERT)
    output = (hidden + out_part.astype(f32)).astype(bf16)
    grad_normed = grad_normed.astype(f32)
    grad_qkv = lax.all_gather(after(grad_qkv, sum_out), "seq", axis=0)
    rows = jnp.sum(grad_qkv[:, width:].astype(f32), axis=0).reshape(-1)
    grad_qkv = jnp.concatenate(
        [
            grad_qkv[owner, :width, part * group : (part + 1) * group]
            for part in range(3)
            for owner in range(seq)
        ],
        axis=1,
    ).astype(f32)
    input_grad = (grad_hidden + norm_back(inputs, rms_scale(inputs), gain_one, grad_normed)).astype(
        bf16
    )
    sum_s_up = jnp.stack([sum_s[1], sum_s[2]], axis=1)

    return (
        output[None],
        input_grad[None],
        rows[:width],
        grad_qkv,
        rows[3 * width : 6 * width],
        sum_out.astype(f32),
        rows[width : 2 * width],
        sum_s_up.astype(f32),
        sum_s[0].T.astype(f32),
        rows[2 * width : 3 * width],
        sum_e_up.astype(f32),
        sum_e_down.astype(f32),
    )


def solution(mesh):
    return jax.shard_map(
        on_device,
        mesh=mesh,
        in_specs=(
            P("fsdp", "seq", None),
            P("fsdp", None),
            P("fsdp", "seq", None),
            P("fsdp", "seq", None),
            P("fsdp"),
            P("fsdp", None),
            P("fsdp"),
            P("fsdp", None),
            P("fsdp"),
            P(None, None, "fsdp"),
            P("fsdp", None),
            P("fsdp"),
            P(None, "fsdp", None),
            P(None, "fsdp", None),
            P("fsdp", "seq", None),
        ),
        out_specs=(
            P("fsdp", "seq", None),
            P("fsdp", "seq", None),
            P("fsdp"),
            P("fsdp", None),
            P("fsdp"),
            P("fsdp", None),
            P("fsdp"),
            P(None, None, "fsdp"),
            P("fsdp", None),
            P("fsdp"),
            P(None, "fsdp", None),
            P(None, "fsdp", None),
        ),
        check_vma=False,
    )
```
